32 devices in a mesh: dp: 16 (over z, y, x), tp: 2 (over core).
Axes of the slice: x: 2, y: 2, z: 4, core: 2. Of those that a mesh axis runs over, the one named last changes fastest.
Arguments:
- inputs: bfloat16 [50688, 384], P(('dp', 'tp')), may hold values from -6 to 6
- keep_mask: int32 [50688], P('dp'), may hold values from 0 to 1, as said below
- cotangent: bfloat16 [50688, 384], P(('dp', 'tp')), may hold values from -6 to 6
- qkv_master: float32 [3, 384, 384], P(None, 'dp', 'tp'), may hold values from -0.3125 to 0.3125
- qkv_first: float32 [3, 384, 384], P(None, 'dp', 'tp'), may hold values from -160 to 160
- qkv_second: float32 [3, 384, 384], P(None, 'dp', 'tp'), may hold values from 25.344 to 405.504
- proj_master: float32 [384, 384], P('tp', 'dp'), may hold values from -3.5 to 3.5
- proj_first: float32 [384, 384], P('tp', 'dp'), may hold values from -24 to 24
- proj_second: float32 [384, 384], P('tp', 'dp'), may hold values from 0.57024 to 9.12384
- fc1_master: float32 [384, 1536], P('dp', 'tp'), may hold values from -0.3125 to 0.3125
- fc1_first: float32 [384, 1536], P('dp', 'tp'), may hold values from -64 to 64
- fc1_second: float32 [384, 1536], P('dp', 'tp'), may hold values from 4.05504 to 64.88064
- fc2_master: float32 [1536, 384], P('tp', 'dp'), may hold values from -0.15625 to 0.15625
- fc2_first: float32 [1536, 384], P('tp', 'dp'), may hold values from -112 to 112
- fc2_second: float32 [1536, 384], P('tp', 'dp'), may hold values from 12.41856 to 198.69696
- norm_master: float32 [6, 384], replicated, may hold values from -4 to 4, as said below
- norm_first: float32 [6, 384], replicated, may hold values from -224 to 224
- norm_second: float32 [6, 384], replicated, may hold values from 57.024 to 912.384
- bias_master: float32 [2, 1152], P('tp'), may hold values from -6 to 6
- bias_first: float32 [2, 1152], P('tp'), may hold values from -160 to 160
- bias_second: float32 [2, 1152], P('tp'), may hold values from 25.344 to 405.504
Outputs:
- output: bfloat16 [50688, 384], P(('dp', 'tp'))
- grad_inputs: float32 [50688, 384], P(('dp', 'tp'))
- qkv_first_new: float32 [3, 384, 384], P(None, 'dp', 'tp')
- qkv_second_new: float32 [3, 384, 384], P(None, 'dp', 'tp')
- qkv_master_new: float32 [3, 384, 384], P(None, 'dp', 'tp')
- qkv_copy: bfloat16 [3, 384, 384], P(None, 'dp', 'tp')
- proj_first_new: float32 [384, 384], P('tp', 'dp')
- proj_second_new: float32 [384, 384], P('tp', 'dp')
- proj_master_new: float32 [384, 384], P('tp', 'dp')
- proj_copy: bfloat16 [384, 384], P('tp', 'dp')
- fc1_first_new: float32 [384, 1536], P('dp', 'tp')
- fc1_second_new: float32 [384, 1536], P('dp', 'tp')
- fc1_master_new: float32 [384, 1536], P('dp', 'tp')
- fc1_copy: bfloat16 [384, 1536], P('dp', 'tp')
- fc2_first_new: float32 [1536, 384], P('tp', 'dp')
- fc2_second_new: float32 [1536, 384], P('tp', 'dp')
- fc2_master_new: float32 [1536, 384], P('tp', 'dp')
- fc2_copy: bfloat16 [1536, 384], P('tp', 'dp')
- norm_first_new: float32 [6, 384], replicated
- norm_second_new: float32 [6, 384], replicated
- norm_master_new: float32 [6, 384], replicated
- bias_first_new: float32 [2, 1152], P('tp')
- bias_second_new: float32 [2, 1152], P('tp')
- bias_master_new: float32 [2, 1152], P('tp')
The draws below stay inside these ranges and needn't reach their ends.
Inputs may be any that keep to these rules, and one draw needn't show every extreme that they name: `keep_mask`: 1 keeps a token, 0 drops it; the first two tokens of each image of 198 (class and distillation) are always kept. `norm_master`: rows 0 and 2 lie between 0.6 and 1.4.
All inputs are finite; a program needn't handle non-finite values.
Results may differ from the reference program's by a relative error of at most 0.012.
The reference program's roundings to bfloat16 on the way count: a program that leaves them out, or rounds other values in their place, can miss the bound.
Values may be sent and summed in bfloat16 or wider, within the bound.
A program may use at most 128 MiB of HBM per device.

```python
import math
import jax
import jax.numpy as jnp
from jax import lax

D = 384
HEADS = 6
HEAD_DIM = 64
FF = 1536
PATCHES = 196
IMG_DEV = 16
STEP = 5
SEQ = 198
IMAGES = 256
TOKENS = 50688
BIASW = 1152
N_TP = 2


def draw_keep_mask(key, part):
    key = jax.random.fold_in(key, 11)
    tail_key, order_key = jax.random.split(key)
    device_count = IMAGES // IMG_DEV
    owner = jnp.arange(IMAGES, dtype=jnp.int32) // IMG_DEV
    least = PATCHES // 3
    base_kept = least + (PATCHES - least) * owner // max(device_count - 1, 1)
    tail_draw = jax.random.randint(tail_key, (IMAGES,), 0, 4)
    patch_kept = jnp.maximum(base_kept // (1 + tail_draw * tail_draw), 1)
    order_keys = jax.random.split(order_key, IMAGES)
    ranks = jax.vmap(lambda one_key: jax.random.permutation(one_key, PATCHES))(order_keys)
    patches_on = (ranks < patch_kept[:, None]).astype(jnp.int32)
    leading = jnp.ones((IMAGES, 2), jnp.int32)
    return jnp.concatenate([leading, patches_on], axis=1).reshape(TOKENS)


def draw_norm_master(key, part):
    key = jax.random.fold_in(key, 12)
    gain_key, shift_key = jax.random.split(key)
    gains = jax.random.uniform(gain_key, (6, D), jnp.float32, 0.6, 1.4)
    shifts = 0.4 * jax.random.normal(shift_key, (6, D), jnp.float32)
    row_number = jnp.arange(6)
    gain_rows = (row_number % 2 == 0) & (row_number < 4)
    return jnp.where(gain_rows[:, None], gains, shifts)


def block_scale(stream_key, dims, cuts, smallest, high):
    factor_of, own = 1.0, jax.random.fold_in(stream_key, 6)
    for axis_at, shards_of in cuts:
        steps = jnp.exp(jax.random.uniform(jax.random.fold_in(own, axis_at), (shards_of,), jnp.float32, smallest / len(cuts), high / len(cuts)))
        factor_of = factor_of * jnp.repeat(steps, dims[axis_at] // shards_of).reshape([-1 if axis == axis_at else 1 for axis in range(len(dims))])
    return factor_of


def bell_draw(rng, dims, scale, reach, pieces=(), held_as=jnp.bfloat16):
    entries = jax.random.normal(rng, dims, jnp.float32) * scale
    if len(pieces) > 0:
        entries = block_scale(rng, dims, pieces, -0.22, 0.18) * entries
    return jnp.clip(entries, min=-reach, max=reach).astype(held_as)


def setup_inputs(seed: int = 0) -> dict:
    splits = jax.random.split(jax.random.key(seed), 22)
    inputs = bell_draw(splits[0], (TOKENS, D), 1.0, 6.0, ((0, 32),))
    keep_mask = draw_keep_mask(jax.random.fold_in(splits[21], 71), 0)
    cotangent = bell_draw(splits[2], (TOKENS, D), 1.0, 6.0, ((0, 32),))
    qkv_master = bell_draw(splits[3], (3, D, D), D ** -0.5, 0.3125, ((1, 16), (2, 2)), jnp.float32)
    qkv_first = bell_draw(splits[4], (3, D, D), (0.111 * TOKENS ** 0.5), 160.0, ((1, 16), (2, 2)), jnp.float32)
    qkv_second = jnp.clip(jnp.exp(math.log(405.504) - 2.7725887 * jax.random.uniform(splits[5], (3, D, D), jnp.float32) ** block_scale(splits[5], (3, D, D), ((1, 16), (2, 2)), -0.2, 0.2)), 25.344, 405.504)
    proj_master = bell_draw(splits[6], (D, D), (5 * D // (3 * SEQ)) ** -0.5, 3.5, ((0, 2), (1, 16)), jnp.float32)
    proj_first = bell_draw(splits[7], (D, D), (0.0167 * TOKENS ** 0.5), 24.0, ((0, 2), (1, 16)), jnp.float32)
    proj_second = jnp.clip(jnp.exp(math.log(9.12384) - 2.7725887 * jax.random.uniform(splits[8], (D, D), jnp.float32) ** block_scale(splits[8], (D, D), ((0, 2), (1, 16)), -0.2, 0.2)), 0.57024, 9.12384)
    fc1_master = bell_draw(splits[9], (D, FF), D ** -0.5, 0.3125, ((0, 16), (1, 2)), jnp.float32)
    fc1_first = bell_draw(splits[10], (D, FF), (0.0444 * TOKENS ** 0.5), 64.0, ((0, 16), (1, 2)), jnp.float32)
    fc1_second = jnp.clip(jnp.exp(math.log(64.88064) - 2.7725887 * jax.random.uniform(splits[11], (D, FF), jnp.float32) ** block_scale(splits[11], (D, FF), ((0, 16), (1, 2)), -0.2, 0.2)), 4.05504, 64.88064)
    fc2_master = bell_draw(splits[12], (FF, D), FF ** -0.5, 0.15625, ((0, 2), (1, 16)), jnp.float32)
    fc2_first = bell_draw(splits[13], (FF, D), (0.0778 * TOKENS ** 0.5), 112.0, ((0, 2), (1, 16)), jnp.float32)
    fc2_second = jnp.clip(jnp.exp(math.log(198.69696) - 2.7725887 * jax.random.uniform(splits[14], (FF, D), jnp.float32) ** block_scale(splits[14], (FF, D), ((0, 2), (1, 16)), -0.2, 0.2)), 12.41856, 198.69696)
    norm_master = draw_norm_master(jax.random.fold_in(splits[21], 71), 0)
    norm_first = bell_draw(splits[16], (6, D), (0.167 * TOKENS ** 0.5), 224.0, (), jnp.float32)
    norm_second = jnp.clip(jnp.exp(jax.random.uniform(splits[17], (6, D), jnp.float32, math.log(57.024), math.log(912.384))), 57.024, 912.384)
    bias_master = bell_draw(splits[18], (N_TP, BIASW), 0.4, 6.0, ((0, 2),), jnp.float32)
    bias_first = bell_draw(splits[19], (N_TP, BIASW), (0.111 * TOKENS ** 0.5), 160.0, ((0, 2),), jnp.float32)
    bias_second = jnp.clip(jnp.exp(math.log(405.504) - 2.7725887 * jax.random.uniform(splits[20], (N_TP, BIASW), jnp.float32) ** block_scale(splits[20], (N_TP, BIASW), ((0, 2),), -0.2, 0.2)), 25.344, 405.504)
    return {"inputs": inputs, "keep_mask": keep_mask, "cotangent": cotangent, "qkv_master": qkv_master, "qkv_first": qkv_first, "qkv_second": qkv_second, "proj_master": proj_master, "proj_first": proj_first, "proj_second": proj_second, "fc1_master": fc1_master, "fc1_first": fc1_first, "fc1_second": fc1_second, "fc2_master": fc2_master, "fc2_first": fc2_first, "fc2_second": fc2_second, "norm_master": norm_master, "norm_first": norm_first, "norm_second": norm_second, "bias_master": bias_master, "bias_first": bias_first, "bias_second": bias_second}


@jax.custom_vjp
def low(v):
    return lax.optimization_barrier(v.astype(jnp.bfloat16)).astype(jnp.float32)

@jax.custom_vjp
def low_back(v):
    return v

def low_keep(v):
    return (low(v), None)

def low_pass(kept, grad):
    return (grad,)

def back_keep(v):
    return (v, None)

def back_low(kept, grad):
    return (low(grad),)
low.defvjp(low_keep, low_pass)
low_back.defvjp(back_keep, back_low)
norm_eps = 1e-06
beta_one = 0.9
beta_two = 0.999
adam_eps = 1e-08
matrix_decay = 0.05

def product(left_side, right_side):
    return jnp.dot(left_side, right_side, preferred_element_type=jnp.float32, precision=lax.Precision.HIGHEST)

def normalize(values_in, gain_row, shift_row):
    row_mean = lax.optimization_barrier(jnp.mean(values_in, axis=-1, keepdims=True))
    centred = values_in - row_mean
    variance = lax.optimization_barrier(jnp.mean(centred * centred, axis=-1, keepdims=True))
    return centred * lax.rsqrt(variance + norm_eps) * gain_row + shift_row

def attend(block):
    query_rows, key_rows, value_rows, keep_rows = block
    raw_scores = jnp.einsum('gthd,gshd->ghts', query_rows, key_rows, precision=lax.Precision.HIGHEST) * HEAD_DIM ** (-0.5)
    raw_scores = low_back(raw_scores)
    scores = jnp.where(keep_rows[:, None, None, :] > 0, raw_scores, -1000000000.0)
    top_score = lax.optimization_barrier(jnp.max(scores, axis=-1, keepdims=True))
    exp_scores = jnp.exp(scores - top_score)
    probs_full = exp_scores / lax.optimization_barrier(jnp.sum(exp_scores, axis=-1, keepdims=True))
    probs_low = low(probs_full)
    return jnp.einsum('ghts,gshd->gthd', probs_low, value_rows, precision=lax.Precision.HIGHEST)

def adam_step(master, first, second, grad, rate, decay):
    first = beta_one * first + (1.0 - beta_one) * grad
    second = beta_two * second + (1.0 - beta_two) * grad * grad
    first_hat = first / (1.0 - beta_one ** STEP)
    second_hat = second / (1.0 - beta_two ** STEP)
    master = master - rate * (first_hat / (jnp.sqrt(second_hat) + adam_eps) + decay * master)
    return (first, second, master)

def reference(inputs, keep_mask, cotangent, qkv_master, qkv_first, qkv_second, proj_master, proj_first, proj_second, fc1_master, fc1_first, fc1_second, fc2_master, fc2_first, fc2_second, norm_master, norm_first, norm_second, bias_master, bias_first, bias_second):
    input_float = inputs.astype(jnp.float32)
    group_size = IMG_DEV * 8
    group_count = IMAGES // group_size
    head_shape = (group_count, group_size, SEQ, HEADS, HEAD_DIM)
    keep_groups = keep_mask.reshape(group_count, group_size, SEQ)

    def forward(stream_in, qkv_weight, proj_weight, fc1_weight, fc2_weight, norm_params, split_bias):
        part_width = D // N_TP
        query_bias = split_bias[:, :part_width].reshape(D)
        value_bias = split_bias[:, part_width:2 * part_width].reshape(D)
        hidden_bias = split_bias[:, 2 * part_width:].reshape(FF)
        qkv_low = low(qkv_weight)
        normed1 = low(normalize(stream_in, norm_params[0], norm_params[1]))
        query_rows = low(low_back(product(normed1, qkv_low[0]) + query_bias))
        key_rows = low(low_back(product(normed1, qkv_low[1])))
        value_rows = low(low_back(product(normed1, qkv_low[2]) + value_bias))
        attended = lax.map(jax.checkpoint(attend), (query_rows.reshape(head_shape), key_rows.reshape(head_shape), value_rows.reshape(head_shape), keep_groups))
        attended = low(low_back(attended.reshape(TOKENS, D)))
        branch = low_back(product(attended, low(proj_weight)) + norm_params[4])
        mid_stream = stream_in + branch
        normed2 = low(normalize(mid_stream, norm_params[2], norm_params[3]))
        pre_act = low_back(product(normed2, low(fc1_weight)) + hidden_bias)
        activated = low(jax.nn.gelu(pre_act, approximate=False))
        mlp_out = low_back(product(activated, low(fc2_weight)) + norm_params[5])
        return mid_stream + mlp_out
    result, backward = jax.vjp(forward, input_float, qkv_master, proj_master, fc1_master, fc2_master, norm_master, bias_master)
    kept_rows = keep_mask.astype(jnp.float32)
    grads = backward(cotangent.astype(jnp.float32) * kept_rows[:, None])
    grad_scale = TOKENS / jnp.sum(kept_rows)
    grads = [grad_scale * one_grad for one_grad in grads]
    outputs = [result.astype(jnp.bfloat16), grads[0]]
    states = [(qkv_master, qkv_first, qkv_second, 0.08, matrix_decay, True), (proj_master, proj_first, proj_second, 0.8, matrix_decay, True), (fc1_master, fc1_first, fc1_second, 0.08, matrix_decay, True), (fc2_master, fc2_first, fc2_second, 0.04, matrix_decay, True), (norm_master, norm_first, norm_second, 0.5, 0.0, False), (bias_master, bias_first, bias_second, 0.5, 0.0, False)]
    for (master, first, second, rate, decay, with_copy), grad in zip(states, grads[1:]):
        first, second, master = adam_step(master, first, second, grad, rate, decay)
        outputs.extend([first, second, master])
        if with_copy:
            outputs.append(master.astype(jnp.bfloat16))
    return tuple(outputs)
```

```python
import functools

import jax
import jax.numpy as jnp
from jax import lax
from jax.experimental import pallas as pl
from jax.experimental.pallas import tpu as pltpu
from jax.sharding import PartitionSpec as P

HEAD_DIM = 64
PATCHES = 196
STEP = 5

norm_eps = 1e-06
beta_one = 0.9
beta_two = 0.999
adam_eps = 1e-08
matrix_decay = 0.05

F32 = jnp.float32
BF16 = jnp.bfloat16
MESH = pl.DeviceIdType.MESH
SEQ = PATCHES + 2
PAD = 208
NEG = -1000000000.0
SCALE = HEAD_DIM**-0.5


def dot_nn(a, b):
    return lax.dot_general(a, b, (((1,), (0,)), ((), ())), preferred_element_type=F32)


def dot_nt(a, b):
    return lax.dot_general(a, b, (((1,), (1,)), ((), ())), preferred_element_type=F32)


def dot_tn(a, b):
    return lax.dot_general(a, b, (((0,), (0,)), ((), ())), preferred_element_type=F32)


def norm_parts(v):
    mean = jnp.mean(v, axis=-1, keepdims=True)
    centred = v - mean
    var = jnp.mean(centred * centred, axis=-1, keepdims=True)
    rstd = lax.rsqrt(var + norm_eps)
    return centred * rstd, rstd


def norm_back(grad, xhat, rstd, gain):
    u = grad * gain
    return (
        u
        - jnp.mean(u, axis=-1, keepdims=True)
        - xhat * jnp.mean(u * xhat, axis=-1, keepdims=True)
    ) * rstd


def gelu_parts(u):
    gauss = jnp.exp(-0.5 * u * u)
    t = 1.0 / (1.0 + (0.3275911 * 0.7071067811865476) * jnp.abs(u))
    poly = t * (
        0.5 * 0.254829592
        + t
        * (
            0.5 * -0.284496736
            + t * (0.5 * 1.421413741 + t * (0.5 * -1.453152027 + t * (0.5 * 1.061405429)))
        )
    )
    tail = poly * gauss
    cdf = jnp.where(u < 0.0, tail, 1.0 - tail)
    return u * cdf, cdf + u * (0.3989422804014327 * gauss)


def adam(master, first, second, grad, rate, decay):
    first = beta_one * first + (1.0 - beta_one) * grad
    second = beta_two * second + (1.0 - beta_two) * grad * grad
    first_hat = first / (1.0 - beta_one**STEP)
    second_hat = second / (1.0 - beta_two**STEP)
    master = master - rate * (first_hat / (jnp.sqrt(second_hat) + adam_eps) + decay * master)
    return first, second, master


def kernel(
    nl,
    np_,
    x_h,
    keep_v,
    cot_h,
    qm,
    qf,
    qs,
    pm,
    pf,
    ps,
    am,
    af,
    as_,
    cm,
    cf,
    cs,
    nm,
    nf,
    ns,
    bm,
    bf,
    bs,
    out_h,
    gin_h,
    qf_o,
    qs_o,
    qm_o,
    qc_o,
    pf_o,
    ps_o,
    pm_o,
    pc_o,
    af_o,
    as_o,
    am_o,
    ac_o,
    cf_o,
    cs_o,
    cm_o,
    cc_o,
    nf_o,
    ns_o,
    nm_o,
    bf_o,
    bs_o,
    bm_o,
    wbuf,
    wts,
    grd,
    sib,
    rpl,
    lsn,
    rln,
    fin,
    pk,
    tr_a,
    tr_b,
    bias2,
    cntl,
    cntp,
    vec,
    vsib,
    vpl,
    vln,
    stage,
    mid,
    probs,
    mcol,
    mkt,
    xpad,
    back,
    n1,
    qkv,
    att,
    n2,
    gbr,
    gatt,
    opad,
    act,
    gp,
    dma_sem,
    bar_sems,
    ag_ls,
    ag_lr,
    ag_ps,
    ag_pr,
    ag_ss,
    ag_sr,
    rs_ss,
    rs_sr,
    rs_ps,
    rs_pr,
    rs_ls,
    rs_lr,
    cn_s,
    cn_r,
    cm_s,
    cm_r,
    vs_s,
    vs_r,
):
    rows, dim = x_h.shape
    images = rows // SEQ
    r = qm.shape[1]
    hw = qm.shape[2]
    ff = wts.shape[2]
    fw = am.shape[1]
    half = fw // 2
    slot_rows = wbuf.shape[4]
    heads = dim // HEAD_DIM
    pairs = heads // 2
    t = lax.axis_index("tp")
    d = lax.axis_index("dp")
    l = d // np_
    p = d - l * np_
    o = 1 - t

    def at(ll, pp):
        return {"dp": ll * np_ + pp}

    def line_peer(k):
        return lax.rem(l + k, nl)

    def plane_peer(k):
        return lax.rem(p + k, np_)

    x_in = pltpu.make_async_copy(x_h, gp.at[0:rows, 0:dim], dma_sem.at[0])
    c_in = pltpu.make_async_copy(cot_h, gp.at[0:rows, dim : 2 * dim], dma_sem.at[1])
    x_in.start()
    c_in.start()

    barrier = pltpu.get_barrier_semaphore()
    for k in range(1, nl):
        pl.semaphore_signal(barrier, inc=1, device_id=at(line_peer(k), p), device_id_type=MESH)
    for k in range(1, np_):
        pl.semaphore_signal(barrier, inc=1, device_id=at(l, plane_peer(k)), device_id_type=MESH)
    pl.semaphore_signal(barrier, inc=1, device_id={"tp": o}, device_id_type=MESH)

    tr_a[...] = jnp.zeros_like(tr_a)

    def put_slot(pc, top_parts, bottom_parts):
        at_col = 0
        for part in top_parts:
            pk[0:r, at_col : at_col + part.shape[1]] = part
            at_col += part.shape[1]
        at_col = 0
        for part in bottom_parts:
            pk[r : 2 * r, at_col : at_col + part.shape[1]] = part
            at_col += part.shape[1]
        wbuf[pc, t, p, l] = pk[...].astype(BF16)

    if 2 * r < slot_rows:
        pk[...] = jnp.zeros_like(pk)
    tr_a[0:hw, 0:r] = pm[...]
    tr_b[:, 0:hw] = tr_a[0:hw, :].T
    put_slot(0, (qm[0], qm[1]), (qm[2], tr_b[0:r, 0:hw]))
    put_slot(1, (am[:, 0:half],), (am[:, half:],))
    tr_a[0:fw, 0:r] = cm[...]
    tr_b[...] = tr_a[...].T
    put_slot(2, (tr_b[0:r, 0:half],), (tr_b[0:r, half:],))
    bias2[t] = jnp.broadcast_to(bm[...], bias2.shape[1:])
    keep_all = keep_v[...].astype(F32)
    count = jnp.sum(jnp.sum(keep_all, axis=1, keepdims=True), axis=0, keepdims=True)
    cntl[l] = jnp.broadcast_to(count, cntl.shape[1:])

    pl.semaphore_wait(barrier, nl - 1 + np_ - 1 + 1)

    def remote(src, dst, ssem, rsem, device):
        return pltpu.make_async_remote_copy(
            src_ref=src, dst_ref=dst, send_sem=ssem, recv_sem=rsem, device_id=device, device_id_type=MESH
        )

    sends = []
    bias_cp = remote(bias2.at[t], bias2.at[t], cm_s.at[0], cm_r.at[0], {"tp": o})
    bias_cp.start()
    sends.append(bias_cp)
    for k in range(1, nl):
        cp = remote(cntl.at[l], cntl.at[l], cn_s.at[k], cn_r.at[k], at(line_peer(k), p))
        cp.start()
        sends.append(cp)
    for pc in range(3):
        for k in range(1, nl):
            cp = remote(
                wbuf.at[pc, t, p, l], wbuf.at[pc, t, p, l], ag_ls.at[pc, k], ag_lr.at[pc, k], at(line_peer(k), p)
            )
            cp.start()
            sends.append(cp)

    def got(dst, rsem):
        return remote(dst, dst, dma_sem.at[2], rsem, {"tp": o})

    def line_done(pc):
        for k in range(1, nl):
            src_l = lax.rem(l + nl - k, nl)
            got(wbuf.at[pc, t, p, src_l], ag_lr.at[pc, k]).wait_recv()
        for k in range(1, np_):
            cp = remote(wbuf.at[pc, t, p], wbuf.at[pc, t, p], ag_ps.at[pc, k], ag_pr.at[pc, k], at(l, plane_peer(k)))
            cp.start()
            sends.append(cp)
        cp = remote(wbuf.at[pc, t, p], wbuf.at[pc, t, p], ag_ss.at[pc, 0], ag_sr.at[pc, 0], {"tp": o})
        cp.start()
        sends.append(cp)

    def plane_done(pc):
        for k in range(1, np_):
            src_p = lax.rem(p + np_ - k, np_)
            got(wbuf.at[pc, t, src_p], ag_pr.at[pc, k]).wait_recv()
            cp = remote(wbuf.at[pc, t, src_p], wbuf.at[pc, t, src_p], ag_ss.at[pc, k], ag_sr.at[pc, k], {"tp": o})
            cp.start()
            sends.append(cp)

    def sibling_done(pc):
        for k in range(np_):
            src_p = lax.rem(p + np_ - k, np_)
            got(wbuf.at[pc, o, src_p], ag_sr.at[pc, k]).wait_recv()

    def cols_of(pc, tt):
        if pc == 0:
            return (
                (0, hw, hw * tt),
                (hw, hw, dim + hw * tt),
            ), (
                (0, hw, 2 * dim + hw * tt),
                (hw, hw, 3 * dim + hw * tt),
            )
        return ((0, half, fw * tt),), ((0, half, fw * tt + half),)

    def assemble(pc):
        for tt in range(2):
            top, bottom = cols_of(pc, tt)
            for ll in range(nl):
                for pp in range(np_):
                    slot = wbuf[pc, tt, pp, ll].astype(F32)
                    row = (ll * np_ + pp) * r
                    for base, parts in ((0, top), (r, bottom)):
                        for at_slot, width, at_col in parts:
                            grd[row : row + r, at_col : at_col + width] = slot[
                                base : base + r, at_slot : at_slot + width
                            ]
        wts[pc] = grd[...].astype(BF16)

    def cast_in(col):
        def step(c, carry):
            at_row = pl.ds(pl.multiple_of(c * 16, 16), 16)
            stage[at_row, :] = gp[at_row, col : col + dim].astype(F32)
            return carry

        lax.fori_loop(0, rows // 16, step, 0)

    stage[rows:, :] = jnp.zeros((stage.shape[0] - rows, dim), F32)
    own_keep = keep_v[pl.ds(pl.multiple_of(t * images, images), images), :].astype(F32)
    mkt[...] = jnp.zeros_like(mkt)
    mkt[0:images, 0:SEQ] = own_keep
    keep_t = mkt[...].T
    for i in range(images):
        mcol[i] = jnp.broadcast_to(keep_t[0:PAD, i : i + 1], (PAD, 128))
    inside = lax.broadcasted_iota(jnp.int32, (PAD, dim), 0) < SEQ
    x_in.wait()
    cast_in(0)
    gain1, shift1 = nm[0:1, :], nm[1:2, :]
    for i in range(images):
        v = jnp.where(inside, stage[i * SEQ : i * SEQ + PAD, :], 0.0)
        xpad[i * PAD : (i + 1) * PAD, :] = v.astype(BF16)
        xhat, _ = norm_parts(v)
        n1[i * PAD : (i + 1) * PAD, :] = (xhat * gain1 + shift1).astype(BF16)
    line_done(0)
    c_in.wait()
    cast_in(dim)
    for i in range(images):
        v = jnp.where(inside, stage[i * SEQ : i * SEQ + PAD, :], 0.0)
        m = mcol[i]
        back[i * PAD : (i + 1) * PAD, :] = (v * jnp.concatenate([m] * (dim // 128), axis=1)).astype(BF16)
    line_done(1)
    for k in range(1, nl):
        src_l = lax.rem(l + nl - k, nl)
        got(cntl.at[src_l], cn_r.at[k]).wait_recv()
    cntp[p] = functools.reduce(lambda a, b: a + b, [cntl[ll] for ll in range(nl)])
    for k in range(1, np_):
        cp = remote(cntp.at[p], cntp.at[p], cm_s.at[k], cm_r.at[k], at(l, plane_peer(k)))
        cp.start()
        sends.append(cp)
    line_done(2)
    plane_done(0)
    sibling_done(0)
    got(bias2.at[o], cm_r.at[0]).wait_recv()
    assemble(0)
    for k in range(1, np_):
        src_p = lax.rem(p + np_ - k, np_)
        got(cntp.at[src_p], cm_r.at[k]).wait_recv()
    kept = functools.reduce(lambda a, b: a + b, [cntp[pp] for pp in range(np_)])
    grad_scale = (rows * 2.0 * nl * np_) / kept[0:1, 0:1]

    def image_rows(i):
        return pl.ds(pl.multiple_of(i * PAD, 16), PAD)

    q_bias = jnp.concatenate([bias2[0, 0:1, 0:hw], bias2[1, 0:1, 0:hw]], axis=1)
    v_bias = jnp.concatenate([bias2[0, 0:1, hw : 2 * hw], bias2[1, 0:1, hw : 2 * hw]], axis=1)
    h_bias = jnp.concatenate([bias2[0, 0:1, 2 * hw :], bias2[1, 0:1, 2 * hw :]], axis=1)
    qkv_bias = jnp.concatenate([q_bias, jnp.zeros_like(q_bias), v_bias], axis=1)

    def qkv_step(i, carry):
        here = image_rows(i)
        v = n1[here, :]
        for c in range(3):
            cols = slice(c * dim, (c + 1) * dim)
            qkv[here, cols] = (dot_nn(v, wts[0, :, cols]) + qkv_bias[:, cols]).astype(BF16)
        return carry

    lax.fori_loop(0, images, qkv_step, 0)
    plane_done(1)

    lane = lax.broadcasted_iota(jnp.int32, (1, 128), 1)
    head_mask = [(lane < HEAD_DIM).astype(F32).astype(BF16), (lane >= HEAD_DIM).astype(F32).astype(BF16)]

    def attend_step(i, carry):
        here = image_rows(i)
        m = mcol[i]
        m = jnp.concatenate([m, m], axis=1)[:, 0:PAD] > 0.0
        for c in range(pairs):
            qp = qkv[here, c * 128 : (c + 1) * 128]
            kp = qkv[here, dim + c * 128 : dim + (c + 1) * 128]
            vp = qkv[here, 2 * dim + c * 128 : 2 * dim + (c + 1) * 128]
            total = None
            for h in range(2):
                s = dot_nt(kp * head_mask[h], qp) * SCALE
                s = jnp.where(m, s, NEG)
                e = jnp.exp(s - jnp.max(s, axis=0, keepdims=True))
                pr = e * (1.0 / jnp.sum(e, axis=0, keepdims=True))
                probs[i * heads + 2 * c + h] = pr
                term = dot_tn(pr.astype(BF16), vp * head_mask[h])
                total = term if total is None else total + term
            att[here, c * 128 : (c + 1) * 128] = total.astype(BF16)
        return carry

    lax.fori_loop(0, images, attend_step, 0)
    plane_done(2)
    sibling_done(1)
    sibling_done(2)
    assemble(1)
    assemble(2)
    for cp in sends:
        cp.wait_send()

    vec[...] = jnp.zeros_like(vec)
    bias4, gain2, shift2, bias5 = nm[4:5, :], nm[2:3, :], nm[3:4, :], nm[5:6, :]
    chunk = 512

    def ff_step(i, carry):
        here = image_rows(i)
        proj_t = wts[0, :, 3 * dim : 4 * dim]
        m = xpad[here, :].astype(F32) + (dot_nt(att[here, :], proj_t) + bias4)
        xhat, rstd = norm_parts(m)
        normed = (xhat * gain2 + shift2).astype(BF16)
        n2[here, :] = normed
        b = back[here, :]
        for j in range(ff // chunk):
            cols = slice(j * chunk, (j + 1) * chunk)
            pre = dot_nn(normed, wts[1, :, cols]) + h_bias[:, cols]
            ga = dot_nn(b, wts[2, :, cols])
            value, slope = gelu_parts(pre)
            act[here, cols] = value.astype(BF16)
            gpre = (ga * slope).astype(BF16)
            gp[here, cols] = gpre
            sums = jnp.sum(gpre.astype(F32), axis=0, keepdims=True)
            vec[8:9, cols] += sums
        opad[here, :] = (m + (dot_nt(act[here, :], wts[2]) + bias5)).astype(BF16)
        dn = dot_nt(gp[here, :], wts[1])
        bfl = b.astype(F32)
        gm = bfl + norm_back(dn, xhat, rstd, gain2)
        mid[here, :] = gm
        g16 = gm.astype(BF16)
        gbr[here, :] = g16
        gatt[here, :] = dot_nn(g16, proj_t).astype(BF16)
        vec[2:3, 0:dim] += jnp.sum(dn * xhat, axis=0, keepdims=True)
        vec[3:4, 0:dim] += jnp.sum(dn, axis=0, keepdims=True)
        vec[4:5, 0:dim] += jnp.sum(g16.astype(F32), axis=0, keepdims=True)
        vec[5:6, 0:dim] += jnp.sum(bfl, axis=0, keepdims=True)
        return carry

    lax.fori_loop(0, images, ff_step, 0)

    def pack(pc):
        for tt in range(2):
            top, bottom = cols_of(pc, tt)
            for ll in range(nl):
                for pp in range(np_):
                    row = (ll * np_ + pp) * r
                    for base, parts in ((0, top), (r, bottom)):
                        for at_slot, width, at_col in parts:
                            pk[base : base + r, at_slot : at_slot + width] = grd[
                                row : row + r, at_col : at_col + width
                            ]
                    wbuf[pc, tt, pp, ll] = pk[...].astype(BF16)

    sib_sends = {}

    def send_sibling(pc):
        cp = remote(wbuf.at[pc, o], sib.at[pc], rs_ss.at[pc], rs_sr.at[pc], {"tp": o})
        cp.start()
        sib_sends[pc] = cp

    late = []

    def send_plane(pc):
        got(sib.at[pc], rs_sr.at[pc]).wait_recv()
        for pp in range(np_):
            for ll in range(nl):
                sib[pc, pp, ll] = (sib[pc, pp, ll].astype(F32) + wbuf[pc, t, pp, ll].astype(F32)).astype(BF16)
        for k in range(1, np_):
            cp = remote(
                sib.at[pc, plane_peer(k)], rpl.at[pc, p], rs_ps.at[pc, k], rs_pr.at[pc, k], at(l, plane_peer(k))
            )
            cp.start()
            late.append(cp)
        rpl[pc, p] = sib[pc, p]

    def send_line(pc):
        for k in range(1, np_):
            src_p = lax.rem(p + np_ - k, np_)
            got(rpl.at[pc, src_p], rs_pr.at[pc, k]).wait_recv()
        for ll in range(nl):
            lsn[pc, ll] = functools.reduce(
                lambda a, b: a + b, [rpl[pc, pp, ll].astype(F32) for pp in range(np_)]
            ).astype(BF16)
        for k in range(1, nl):
            cp = remote(
                lsn.at[pc, line_peer(k)], rln.at[pc, l], rs_ls.at[pc, k], rs_lr.at[pc, k], at(line_peer(k), p)
            )
            cp.start()
            late.append(cp)
        rln[pc, l] = lsn[pc, l]

    def sum_line(pc):
        for k in range(1, nl):
            src_l = lax.rem(l + nl - k, nl)
            got(rln.at[pc, src_l], rs_lr.at[pc, k]).wait_recv()
        fin[pc] = functools.reduce(lambda a, b: a + b, [rln[pc, ll].astype(F32) for ll in range(nl)])

    def grad_step(left, right, width):
        def step(j, carry):
            cols = pl.ds(pl.multiple_of(j * 256, 256), 256)
            grd[:, cols] = dot_tn(left[...], right[:, cols])
            return carry

        lax.fori_loop(0, width // 256, step, 0)

    grad_step(back, act, ff)
    pack(2)
    send_sibling(2)
    grad_step(n2, gp, ff)
    pack(1)
    send_sibling(1)
    send_plane(2)
    grd[:, 3 * dim :] = dot_tn(gbr[...], att[...])
    send_plane(1)
    send_line(2)

    def attend_back(i, carry):
        here = image_rows(i)
        for c in range(pairs):
            qp = qkv[here, c * 128 : (c + 1) * 128]
            kp = qkv[here, dim + c * 128 : dim + (c + 1) * 128]
            vp = qkv[here, 2 * dim + c * 128 : 2 * dim + (c + 1) * 128]
            da = gatt[here, c * 128 : (c + 1) * 128]
            dq = dk = dv = 0.0
            for h in range(2):
                hm = head_mask[h]
                pr = probs[i * heads + 2 * c + h]
                dp = dot_nt(vp * hm, da)
                inner = jnp.sum(pr * dp, axis=0, keepdims=True)
                ds = (pr * (dp - inner)).astype(BF16)
                dv = dv + dot_nn(pr.astype(BF16), da * hm)
                dk = dk + dot_nn(ds, qp * hm)
                dq = dq + dot_tn(ds, kp * hm)
            dq = (dq * SCALE).astype(BF16)
            dv = dv.astype(BF16)
            act[here, c * 128 : (c + 1) * 128] = dq
            act[here, dim + c * 128 : dim + (c + 1) * 128] = (dk * SCALE).astype(BF16)
            act[here, 2 * dim + c * 128 : 2 * dim + (c + 1) * 128] = dv
            vec[6:7, c * 128 : (c + 1) * 128] += jnp.sum(dq.astype(F32), axis=0, keepdims=True)
            vec[7:8, c * 128 : (c + 1) * 128] += jnp.sum(dv.astype(F32), axis=0, keepdims=True)
        return carry

    lax.fori_loop(0, images, attend_back, 0)
    send_line(1)

    def qkv_grad(j, carry):
        cols = pl.ds(pl.multiple_of(j * 384, 128), 384)
        grd[:, cols] = dot_tn(n1[...], act[:, cols])
        return carry

    lax.fori_loop(0, 3, qkv_grad, 0)
    pack(0)
    send_sibling(0)

    def last_step(i, carry):
        here = image_rows(i)
        dn = dot_nt(act[here, 0 : 3 * dim], wts[0, :, 0 : 3 * dim])
        xhat, rstd = norm_parts(xpad[here, :].astype(F32))
        mid[here, :] = (mid[here, :] + norm_back(dn, xhat, rstd, gain1)) * grad_scale
        vec[0:1, 0:dim] += jnp.sum(dn * xhat, axis=0, keepdims=True)
        vec[1:2, 0:dim] += jnp.sum(dn, axis=0, keepdims=True)
        return carry

    lax.fori_loop(0, images, last_step, 0)
    vec_cp = remote(vec, vsib, vs_s.at[0], vs_r.at[0], {"tp": o})
    vec_cp.start()
    send_plane(0)

    for i in range(images):
        stage[i * SEQ : (i + 1) * SEQ, :] = opad[i * PAD : i * PAD + SEQ, :].astype(F32)

    def cast_out(c, carry):
        at_row = pl.ds(pl.multiple_of(c * 16, 16), 16)
        gp[at_row, 0:dim] = stage[at_row, :].astype(BF16)
        return carry

    lax.fori_loop(0, rows // 16, cast_out, 0)
    out_cp = pltpu.make_async_copy(gp.at[0:rows, 0:dim], out_h, dma_sem.at[0])
    out_cp.start()
    got(vsib, vs_r.at[0]).wait_recv()
    vpl[p] = vec[...] + vsib[...]
    for k in range(1, np_):
        cp = remote(vpl.at[p], vpl.at[p], vs_s.at[k], vs_r.at[k], at(l, plane_peer(k)))
        cp.start()
        late.append(cp)
    for i in range(images):
        stage[i * SEQ : (i + 1) * SEQ, :] = mid[i * PAD : i * PAD + SEQ, :]
    gin_cp = pltpu.make_async_copy(stage.at[0:rows, :], gin_h, dma_sem.at[1])
    gin_cp.start()
    for k in range(1, np_):
        src_p = lax.rem(p + np_ - k, np_)
        got(vpl.at[src_p], vs_r.at[k]).wait_recv()
    vln[l] = functools.reduce(lambda a, b: a + b, [vpl[pp] for pp in range(np_)])
    for k in range(1, nl):
        cp = remote(vln.at[l], vln.at[l], vs_s.at[np_ + k], vs_r.at[np_ + k], at(line_peer(k), p))
        cp.start()
        late.append(cp)
    send_line(0)

    def update(grad, m_in, f_in, s_in, f_out, s_out, m_out, c_out, rate, decay):
        first, second, master = adam(m_in, f_in, s_in, grad * grad_scale, rate, decay)
        f_out[...] = first
        s_out[...] = second
        m_out[...] = master
        if c_out is not None:
            c_out[...] = master.astype(BF16)

    sum_line(1)
    update(
        jnp.concatenate([fin[1, 0:r, :], fin[1, r : 2 * r, :]], axis=1),
        am[...], af[...], as_[...], af_o, as_o, am_o, ac_o, 0.08, matrix_decay,
    )
    sum_line(2)
    tr_b[0:r, 0:half] = fin[2, 0:r, :]
    tr_b[0:r, half:] = fin[2, r : 2 * r, :]
    tr_a[...] = tr_b[...].T
    update(
        tr_a[0:fw, 0:r], cm[...], cf[...], cs[...], cf_o, cs_o, cm_o, cc_o, 0.04, matrix_decay
    )
    for k in range(1, nl):
        src_l = lax.rem(l + nl - k, nl)
        got(vln.at[src_l], vs_r.at[np_ + k]).wait_recv()
    vec_cp.wait_send()
    vec[...] = functools.reduce(lambda a, b: a + b, [vln[ll] for ll in range(nl)])
    update(vec[0:6, 0:dim], nm[...], nf[...], ns[...], nf_o, ns_o, nm_o, None, 0.5, 0.0)
    own = t == 0

    def pick(row, width):
        return jnp.where(own, vec[row : row + 1, 0:width], vec[row : row + 1, width : 2 * width])

    update(
        jnp.concatenate([pick(6, hw), pick(7, hw), pick(8, fw)], axis=1),
        bm[...], bf[...], bs[...], bf_o, bs_o, bm_o, None, 0.5, 0.0,
    )
    sum_line(0)
    g0 = fin[0]
    for c, grad in enumerate((g0[0:r, 0:hw], g0[0:r, hw:], g0[r : 2 * r, 0:hw])):
        update(
            grad, qm[c], qf[c], qs[c], qf_o.at[c], qs_o.at[c], qm_o.at[c], qc_o.at[c], 0.08, matrix_decay
        )
    tr_b[0:r, 0:hw] = g0[r : 2 * r, hw:]
    tr_a[0:hw, :] = tr_b[:, 0:hw].T
    update(tr_a[0:hw, 0:r], pm[...], pf[...], ps[...], pf_o, ps_o, pm_o, pc_o, 0.8, matrix_decay)

    out_cp.wait()
    gin_cp.wait()
    for cp in late:
        cp.wait_send()
    for cp in sib_sends.values():
        cp.wait_send()


def body(
    inputs, keep_mask, cotangent,
    qkv_master, qkv_first, qkv_second,
    proj_master, proj_first, proj_second,
    fc1_master, fc1_first, fc1_second,
    fc2_master, fc2_first, fc2_second,
    norm_master, norm_first, norm_second,
    bias_master, bias_first, bias_second,
):
    n = lax.axis_size("dp")
    nl = 4 if n % 4 == 0 else n
    np_ = n // nl
    rows, dim = inputs.shape
    images = rows // SEQ
    padded = images * PAD
    r = qkv_master.shape[1]
    hw = qkv_master.shape[2]
    fw = fc1_master.shape[1]
    ff = 2 * fw
    slot = -(-2 * r // 16) * 16
    keep = keep_mask.reshape(2 * images, SEQ)
    vm = pl.BlockSpec(memory_space=pltpu.VMEM)
    hbm = pl.BlockSpec(memory_space=pl.ANY)

    def like(a, dtype=None):
        return jax.ShapeDtypeStruct(a.shape, dtype or a.dtype)

    outs = [like(inputs), like(inputs, F32)]
    for a in (qkv_master, proj_master, fc1_master, fc2_master):
        outs += [like(a), like(a), like(a), like(a, BF16)]
    for a in (norm_master, bias_master):
        outs += [like(a)] * 3
    dma = pltpu.SemaphoreType.DMA
    scratch = [
        pltpu.VMEM((3, 2, np_, nl, slot, dim), BF16),
        pltpu.VMEM((3, dim, ff), BF16),
        pltpu.VMEM((dim, ff), F32),
        pltpu.VMEM((3, np_, nl, slot, dim), BF16),
        pltpu.VMEM((3, np_, nl, slot, dim), BF16),
        pltpu.VMEM((3, nl, slot, dim), BF16),
        pltpu.VMEM((3, nl, slot, dim), BF16),
        pltpu.VMEM((3, slot, dim), F32),
        pltpu.VMEM((slot, dim), F32),
        pltpu.VMEM((fw, 128), F32),
        pltpu.VMEM((128, fw), F32),
        pltpu.VMEM((2, 8, bias_master.shape[1]), F32),
        pltpu.VMEM((nl, 8, 128), F32),
        pltpu.VMEM((np_, 8, 128), F32),
        pltpu.VMEM((16, ff), F32),
        pltpu.VMEM((16, ff), F32),
        pltpu.VMEM((np_, 16, ff), F32),
        pltpu.VMEM((nl, 16, ff), F32),
        pltpu.VMEM((-(-(rows - SEQ + PAD) // 16) * 16, dim), F32),
        pltpu.VMEM((padded, dim), F32),
        pltpu.VMEM((images * (dim // HEAD_DIM), PAD, PAD), F32),
        pltpu.VMEM((images, PAD, 128), F32),
        pltpu.VMEM((128, 256), F32),
        pltpu.VMEM((padded, dim), BF16),
        pltpu.VMEM((padded, dim), BF16),
        pltpu.VMEM((padded, dim), BF16),
        pltpu.VMEM((padded, 3 * dim), BF16),
        pltpu.VMEM((padded, dim), BF16),
        pltpu.VMEM((padded, dim), BF16),
        pltpu.VMEM((padded, dim), BF16),
        pltpu.VMEM((padded, dim), BF16),
        pltpu.VMEM((padded, dim), BF16),
        pltpu.VMEM((padded, ff), BF16),
        pltpu.VMEM((padded, ff), BF16),
        dma((3,)),
        dma((1,)),
        dma((3, nl)),
        dma((3, nl)),
        dma((3, np_)),
        dma((3, np_)),
        dma((3, np_)),
        dma((3, np_)),
        dma((3,)),
        dma((3,)),
        dma((3, np_)),
        dma((3, np_)),
        dma((3, nl)),
        dma((3, nl)),
        dma((nl,)),
        dma((nl,)),
        dma((np_,)),
        dma((np_,)),
        dma((np_ + nl,)),
        dma((np_ + nl,)),
    ]
    return pl.pallas_call(
        functools.partial(kernel, nl, np_),
        out_shape=outs,
        in_specs=[hbm, vm, hbm] + [vm] * 18,
        out_specs=[hbm, hbm] + [vm] * 22,
        scratch_shapes=scratch,
        compiler_params=pltpu.CompilerParams(
            collective_id=0, has_side_effects=True, vmem_limit_bytes=64 * 1024 * 1024
        ),
    )(
        inputs, keep, cotangent,
        qkv_master, qkv_first, qkv_second,
        proj_master, proj_first, proj_second,
        fc1_master, fc1_first, fc1_second,
        fc2_master, fc2_first, fc2_second,
        norm_master, norm_first, norm_second,
        bias_master, bias_first, bias_second,
    )


def solution(mesh):
    mats = [P(None, "dp", "tp"), P("tp", "dp"), P("dp", "tp"), P("tp", "dp")]
    in_specs = [P(("dp", "tp"), None), P("dp"), P(("dp", "tp"), None)]
    out_specs = [P(("dp", "tp"), None), P(("dp", "tp"), None)]
    for m in mats:
        in_specs += [m] * 3
        out_specs += [m] * 4
    in_specs += [P()] * 3 + [P("tp", None)] * 3
    out_specs += [P()] * 3 + [P("tp", None)] * 3
    return jax.shard_map(
        body, mesh=mesh, in_specs=tuple(in_specs), out_specs=tuple(out_specs), check_vma=False
    )
```

```python
import functools

import jax
import jax.numpy as jnp
from jax import lax
from jax.experimental import pallas as pl
from jax.experimental.pallas import tpu as pltpu
from jax.sharding import PartitionSpec as P

HEAD_DIM = 64
PATCHES = 196
STEP = 5

norm_eps = 1e-06
beta_one = 0.9
beta_two = 0.999
adam_eps = 1e-08
matrix_decay = 0.05

F32 = jnp.float32
BF16 = jnp.bfloat16
MESH = pl.DeviceIdType.MESH
SEQ = PATCHES + 2
PAD = 208
NEG = -1000000000.0
SCALE = HEAD_DIM**-0.5


def dot_nn(a, b):
    return lax.dot_general(a, b, (((1,), (0,)), ((), ())), preferred_element_type=F32)


def dot_nt(a, b):
    return lax.dot_general(a, b, (((1,), (1,)), ((), ())), preferred_element_type=F32)


def dot_tn(a, b):
    return lax.dot_general(a, b, (((0,), (0,)), ((), ())), preferred_element_type=F32)


def norm_parts(v):
    mean = jnp.mean(v, axis=-1, keepdims=True)
    centred = v - mean
    var = jnp.mean(centred * centred, axis=-1, keepdims=True)
    rstd = lax.rsqrt(var + norm_eps)
    return centred * rstd, rstd


def norm_back(grad, xhat, rstd, gain):
    u = grad * gain
    return (
        u
        - jnp.mean(u, axis=-1, keepdims=True)
        - xhat * jnp.mean(u * xhat, axis=-1, keepdims=True)
    ) * rstd


def gelu_parts(u):
    gauss = jnp.exp(-0.5 * u * u)
    t = 1.0 / (1.0 + (0.3275911 * 0.7071067811865476) * jnp.abs(u))
    poly = t * (
        0.5 * 0.254829592
        + t
        * (
            0.5 * -0.284496736
            + t * (0.5 * 1.421413741 + t * (0.5 * -1.453152027 + t * (0.5 * 1.061405429)))
        )
    )
    tail = poly * gauss
    cdf = jnp.where(u < 0.0, tail, 1.0 - tail)
    return u * cdf, cdf + u * (0.3989422804014327 * gauss)


def adam(master, first, second, grad, rate, decay):
    first = beta_one * first + (1.0 - beta_one) * grad
    second = beta_two * second + (1.0 - beta_two) * grad * grad
    first_hat = first / (1.0 - beta_one**STEP)
    second_hat = second / (1.0 - beta_two**STEP)
    master = master - rate * (first_hat / (jnp.sqrt(second_hat) + adam_eps) + decay * master)
    return first, second, master


def kernel(
    nl,
    np_,
    x_h,
    keep_v,
    cot_h,
    qm,
    pm,
    am,
    cm,
    nm,
    bm,
    out_h,
    gin_h,
    fin,
    vec_o,
    kept_o,
    wbuf,
    wts,
    grd,
    sib,
    rpl,
    lsn,
    rln,
    pk,
    bias2,
    cntl,
    cntp,
    vec,
    vsib,
    vpl,
    vln,
    stage,
    mid,
    probs,
    mcol,
    mkt,
    xpad,
    back,
    n1,
    qkv,
    att,
    n2,
    gbr,
    gatt,
    opad,
    act,
    gp,
    dma_sem,
    bar_sems,
    ag_ls,
    ag_lr,
    ag_ps,
    ag_pr,
    ag_ss,
    ag_sr,
    rs_ss,
    rs_sr,
    rs_ps,
    rs_pr,
    rs_ls,
    rs_lr,
    cn_s,
    cn_r,
    cm_s,
    cm_r,
    vs_s,
    vs_r,
):
    rows, dim = x_h.shape
    images = rows // SEQ
    r = qm.shape[1]
    hw = qm.shape[2]
    ff = wts.shape[2]
    fw = am.shape[1]
    half = fw // 2
    slot_rows = wbuf.shape[4]
    heads = dim // HEAD_DIM
    pairs = heads // 2
    t = lax.axis_index("tp")
    d = lax.axis_index("dp")
    l = d // np_
    p = d - l * np_
    o = 1 - t

    def at(ll, pp):
        return {"dp": ll * np_ + pp}

    def line_peer(k):
        return lax.rem(l + k, nl)

    def plane_peer(k):
        return lax.rem(p + k, np_)

    x_in = pltpu.make_async_copy(x_h, gp.at[0:rows, 0:dim], dma_sem.at[0])
    c_in = pltpu.make_async_copy(cot_h, gp.at[0:rows, dim : 2 * dim], dma_sem.at[1])
    x_in.start()
    c_in.start()

    barrier = pltpu.get_barrier_semaphore()
    for k in range(1, nl):
        pl.semaphore_signal(barrier, inc=1, device_id=at(line_peer(k), p), device_id_type=MESH)
    for k in range(1, np_):
        pl.semaphore_signal(barrier, inc=1, device_id=at(l, plane_peer(k)), device_id_type=MESH)
    pl.semaphore_signal(barrier, inc=1, device_id={"tp": o}, device_id_type=MESH)

    def put_slot(pc, top_parts, bottom_parts):
        at_col = 0
        for part in top_parts:
            pk[0:r, at_col : at_col + part.shape[1]] = part
            at_col += part.shape[1]
        at_col = 0
        for part in bottom_parts:
            pk[r : 2 * r, at_col : at_col + part.shape[1]] = part
            at_col += part.shape[1]
        wbuf[pc, t, p, l] = pk[...].astype(BF16)

    if 2 * r < slot_rows:
        pk[...] = jnp.zeros_like(pk)
    put_slot(0, (qm[0], qm[1]), (qm[2], pm[...]))
    put_slot(1, (am[:, 0:half],), (am[:, half:],))
    put_slot(2, (cm[:, 0:half],), (cm[:, half:],))
    bias2[t] = jnp.broadcast_to(bm[...], bias2.shape[1:])
    keep_all = keep_v[...].astype(F32)
    count = jnp.sum(jnp.sum(keep_all, axis=1, keepdims=True), axis=0, keepdims=True)
    cntl[l] = jnp.broadcast_to(count, cntl.shape[1:])

    pl.semaphore_wait(barrier, nl - 1 + np_ - 1 + 1)

    def remote(src, dst, ssem, rsem, device):
        return pltpu.make_async_remote_copy(
            src_ref=src, dst_ref=dst, send_sem=ssem, recv_sem=rsem, device_id=device, device_id_type=MESH
        )

    sends = []
    bias_cp = remote(bias2.at[t], bias2.at[t], cm_s.at[0], cm_r.at[0], {"tp": o})
    bias_cp.start()
    sends.append(bias_cp)
    for k in range(1, nl):
        cp = remote(cntl.at[l], cntl.at[l], cn_s.at[k], cn_r.at[k], at(line_peer(k), p))
        cp.start()
        sends.append(cp)
    for pc in range(3):
        for k in range(1, nl):
            cp = remote(
                wbuf.at[pc, t, p, l], wbuf.at[pc, t, p, l], ag_ls.at[pc, k], ag_lr.at[pc, k], at(line_peer(k), p)
            )
            cp.start()
            sends.append(cp)

    def got(dst, rsem):
        return remote(dst, dst, dma_sem.at[2], rsem, {"tp": o})

    def line_done(pc):
        for k in range(1, nl):
            src_l = lax.rem(l + nl - k, nl)
            got(wbuf.at[pc, t, p, src_l], ag_lr.at[pc, k]).wait_recv()
        for k in range(1, np_):
            cp = remote(wbuf.at[pc, t, p], wbuf.at[pc, t, p], ag_ps.at[pc, k], ag_pr.at[pc, k], at(l, plane_peer(k)))
            cp.start()
            sends.append(cp)
        cp = remote(wbuf.at[pc, t, p], wbuf.at[pc, t, p], ag_ss.at[pc, 0], ag_sr.at[pc, 0], {"tp": o})
        cp.start()
        sends.append(cp)

    def plane_done(pc):
        for k in range(1, np_):
            src_p = lax.rem(p + np_ - k, np_)
            got(wbuf.at[pc, t, src_p], ag_pr.at[pc, k]).wait_recv()
            cp = remote(wbuf.at[pc, t, src_p], wbuf.at[pc, t, src_p], ag_ss.at[pc, k], ag_sr.at[pc, k], {"tp": o})
            cp.start()
            sends.append(cp)

    def sibling_done(pc):
        for k in range(np_):
            src_p = lax.rem(p + np_ - k, np_)
            got(wbuf.at[pc, o, src_p], ag_sr.at[pc, k]).wait_recv()

    def cols_of(pc, tt):
        if pc == 0:
            return (
                (0, hw, hw * tt),
                (hw, hw, dim + hw * tt),
            ), (
                (0, hw, 2 * dim + hw * tt),
                (hw, hw, 3 * dim + hw * tt),
            )
        return ((0, half, fw * tt),), ((0, half, fw * tt + half),)

    def assemble(pc):
        for tt in range(2):
            top, bottom = cols_of(pc, tt)
            for ll in range(nl):
                for pp in range(np_):
                    slot = wbuf[pc, tt, pp, ll].astype(F32)
                    row = (ll * np_ + pp) * r
                    for base, parts in ((0, top), (r, bottom)):
                        for at_slot, width, at_col in parts:
                            grd[row : row + r, at_col : at_col + width] = slot[
                                base : base + r, at_slot : at_slot + width
                            ]
        wts[pc] = grd[...].astype(BF16)

    def cast_in(col):
        def step(c, carry):
            at_row = pl.ds(pl.multiple_of(c * 16, 16), 16)
            stage[at_row, :] = gp[at_row, col : col + dim].astype(F32)
            return carry

        lax.fori_loop(0, rows // 16, step, 0)

    stage[rows:, :] = jnp.zeros((stage.shape[0] - rows, dim), F32)
    own_keep = keep_v[pl.ds(pl.multiple_of(t * images, images), images), :].astype(F32)
    mkt[...] = jnp.zeros_like(mkt)
    mkt[0:images, 0:SEQ] = own_keep
    keep_t = mkt[...].T
    for i in range(images):
        mcol[i] = jnp.broadcast_to(keep_t[0:PAD, i : i + 1], (PAD, 128))
    inside = lax.broadcasted_iota(jnp.int32, (PAD, dim), 0) < SEQ
    x_in.wait()
    cast_in(0)
    gain1, shift1 = nm[0:1, :], nm[1:2, :]
    for i in range(images):
        v = jnp.where(inside, stage[i * SEQ : i * SEQ + PAD, :], 0.0)
        xpad[i * PAD : (i + 1) * PAD, :] = v.astype(BF16)
        xhat, _ = norm_parts(v)
        n1[i * PAD : (i + 1) * PAD, :] = (xhat * gain1 + shift1).astype(BF16)
    line_done(0)
    c_in.wait()
    cast_in(dim)
    for i in range(images):
        v = jnp.where(inside, stage[i * SEQ : i * SEQ + PAD, :], 0.0)
        m = mcol[i]
        back[i * PAD : (i + 1) * PAD, :] = (v * jnp.concatenate([m] * (dim // 128), axis=1)).astype(BF16)
    line_done(1)
    for k in range(1, nl):
        src_l = lax.rem(l + nl - k, nl)
        got(cntl.at[src_l], cn_r.at[k]).wait_recv()
    cntp[p] = functools.reduce(lambda a, b: a + b, [cntl[ll] for ll in range(nl)])
    for k in range(1, np_):
        cp = remote(cntp.at[p], cntp.at[p], cm_s.at[k], cm_r.at[k], at(l, plane_peer(k)))
        cp.start()
        sends.append(cp)
    line_done(2)
    plane_done(0)
    sibling_done(0)
    got(bias2.at[o], cm_r.at[0]).wait_recv()
    assemble(0)
    for k in range(1, np_):
        src_p = lax.rem(p + np_ - k, np_)
        got(cntp.at[src_p], cm_r.at[k]).wait_recv()
    kept = functools.reduce(lambda a, b: a + b, [cntp[pp] for pp in range(np_)])
    grad_scale = (rows * 2.0 * nl * np_) / kept[0:1, 0:1]

    def image_rows(i):
        return pl.ds(pl.multiple_of(i * PAD, 16), PAD)

    q_bias = jnp.concatenate([bias2[0, 0:1, 0:hw], bias2[1, 0:1, 0:hw]], axis=1)
    v_bias = jnp.concatenate([bias2[0, 0:1, hw : 2 * hw], bias2[1, 0:1, hw : 2 * hw]], axis=1)
    h_bias = jnp.concatenate([bias2[0, 0:1, 2 * hw :], bias2[1, 0:1, 2 * hw :]], axis=1)
    qkv_bias = jnp.concatenate([q_bias, jnp.zeros_like(q_bias), v_bias], axis=1)

    def qkv_step(i, carry):
        here = image_rows(i)
        v = n1[here, :]
        for c in range(3):
            cols = slice(c * dim, (c + 1) * dim)
            qkv[here, cols] = (dot_nn(v, wts[0, :, cols]) + qkv_bias[:, cols]).astype(BF16)
        return carry

    lax.fori_loop(0, images, qkv_step, 0)
    plane_done(1)

    lane = lax.broadcasted_iota(jnp.int32, (1, 128), 1)
    head_mask = [(lane < HEAD_DIM).astype(F32).astype(BF16), (lane >= HEAD_DIM).astype(F32).astype(BF16)]

    def attend_step(i, carry):
        here = image_rows(i)
        m = mcol[i]
        m = jnp.concatenate([m, m], axis=1)[:, 0:PAD] > 0.0
        for c in range(pairs):
            qp = qkv[here, c * 128 : (c + 1) * 128]
            kp = qkv[here, dim + c * 128 : dim + (c + 1) * 128]
            vp = qkv[here, 2 * dim + c * 128 : 2 * dim + (c + 1) * 128]
            total = None
            for h in range(2):
                s = dot_nt(kp * head_mask[h], qp) * SCALE
                s = jnp.where(m, s, NEG)
                e = jnp.exp(s - jnp.max(s, axis=0, keepdims=True))
                pr = e * (1.0 / jnp.sum(e, axis=0, keepdims=True))
                probs[i * heads + 2 * c + h] = pr
                term = dot_tn(pr.astype(BF16), vp * head_mask[h])
                total = term if total is None else total + term
            att[here, c * 128 : (c + 1) * 128] = total.astype(BF16)
        return carry

    lax.fori_loop(0, images, attend_step, 0)
    plane_done(2)
    sibling_done(1)
    sibling_done(2)
    assemble(1)
    assemble(2)
    for cp in sends:
        cp.wait_send()

    vec[...] = jnp.zeros_like(vec)
    bias4, gain2, shift2, bias5 = nm[4:5, :], nm[2:3, :], nm[3:4, :], nm[5:6, :]
    chunk = 512

    def ff_step(i, carry):
        here = image_rows(i)
        proj_t = wts[0, :, 3 * dim : 4 * dim]
        m = xpad[here, :].astype(F32) + (dot_nt(att[here, :], proj_t) + bias4)
        xhat, rstd = norm_parts(m)
        normed = (xhat * gain2 + shift2).astype(BF16)
        n2[here, :] = normed
        b = back[here, :]
        for j in range(ff // chunk):
            cols = slice(j * chunk, (j + 1) * chunk)
            pre = dot_nn(normed, wts[1, :, cols]) + h_bias[:, cols]
            ga = dot_nn(b, wts[2, :, cols])
            value, slope = gelu_parts(pre)
            act[here, cols] = value.astype(BF16)
            gpre = (ga * slope).astype(BF16)
            gp[here, cols] = gpre
            sums = jnp.sum(gpre.astype(F32), axis=0, keepdims=True)
            vec[8:9, cols] += sums
        opad[here, :] = (m + (dot_nt(act[here, :], wts[2]) + bias5)).astype(BF16)
        dn = dot_nt(gp[here, :], wts[1])
        bfl = b.astype(F32)
        gm = bfl + norm_back(dn, xhat, rstd, gain2)
        mid[here, :] = gm
        g16 = gm.astype(BF16)
        gbr[here, :] = g16
        gatt[here, :] = dot_nn(g16, proj_t).astype(BF16)
        vec[2:3, 0:dim] += jnp.sum(dn * xhat, axis=0, keepdims=True)
        vec[3:4, 0:dim] += jnp.sum(dn, axis=0, keepdims=True)
        vec[4:5, 0:dim] += jnp.sum(g16.astype(F32), axis=0, keepdims=True)
        vec[5:6, 0:dim] += jnp.sum(bfl, axis=0, keepdims=True)
        return carry

    lax.fori_loop(0, images, ff_step, 0)

    def pack(pc):
        for tt in range(2):
            top, bottom = cols_of(pc, tt)
            for ll in range(nl):
                for pp in range(np_):
                    row = (ll * np_ + pp) * r
                    for base, parts in ((0, top), (r, bottom)):
                        for at_slot, width, at_col in parts:
                            pk[base : base + r, at_slot : at_slot + width] = grd[
                                row : row + r, at_col : at_col + width
                            ]
                    wbuf[pc, tt, pp, ll] = pk[...].astype(BF16)

    sib_sends = {}

    def send_sibling(pc):
        cp = remote(wbuf.at[pc, o], sib.at[pc], rs_ss.at[pc], rs_sr.at[pc], {"tp": o})
        cp.start()
        sib_sends[pc] = cp

    late = []

    def send_plane(pc):
        got(sib.at[pc], rs_sr.at[pc]).wait_recv()
        for pp in range(np_):
            for ll in range(nl):
                sib[pc, pp, ll] = (sib[pc, pp, ll].astype(F32) + wbuf[pc, t, pp, ll].astype(F32)).astype(BF16)
        for k in range(1, np_):
            cp = remote(
                sib.at[pc, plane_peer(k)], rpl.at[pc, p], rs_ps.at[pc, k], rs_pr.at[pc, k], at(l, plane_peer(k))
            )
            cp.start()
            late.append(cp)
        rpl[pc, p] = sib[pc, p]

    def send_line(pc):
        for k in range(1, np_):
            src_p = lax.rem(p + np_ - k, np_)
            got(rpl.at[pc, src_p], rs_pr.at[pc, k]).wait_recv()
        for ll in range(nl):
            lsn[pc, ll] = functools.reduce(
                lambda a, b: a + b, [rpl[pc, pp, ll].astype(F32) for pp in range(np_)]
            ).astype(BF16)
        for k in range(1, nl):
            cp = remote(
                lsn.at[pc, line_peer(k)], rln.at[pc, l], rs_ls.at[pc, k], rs_lr.at[pc, k], at(line_peer(k), p)
            )
            cp.start()
            late.append(cp)
        rln[pc, l] = lsn[pc, l]

    def sum_line(pc):
        for k in range(1, nl):
            src_l = lax.rem(l + nl - k, nl)
            got(rln.at[pc, src_l], rs_lr.at[pc, k]).wait_recv()
        fin[pc] = functools.reduce(lambda a, b: a + b, [rln[pc, ll].astype(F32) for ll in range(nl)])

    def grad_step(left, right, width):
        def step(j, carry):
            cols = pl.ds(pl.multiple_of(j * 256, 256), 256)
            grd[:, cols] = dot_tn(left[...], right[:, cols])
            return carry

        lax.fori_loop(0, width // 256, step, 0)

    grad_step(back, act, ff)
    pack(2)
    send_sibling(2)
    grad_step(n2, gp, ff)
    pack(1)
    send_sibling(1)
    send_plane(2)
    grd[:, 3 * dim :] = dot_tn(gbr[...], att[...])
    send_plane(1)
    send_line(2)

    def attend_back(i, carry):
        here = image_rows(i)
        for c in range(pairs):
            qp = qkv[here, c * 128 : (c + 1) * 128]
            kp = qkv[here, dim + c * 128 : dim + (c + 1) * 128]
            vp = qkv[here, 2 * dim + c * 128 : 2 * dim + (c + 1) * 128]
            da = gatt[here, c * 128 : (c + 1) * 128]
            dq = dk = dv = 0.0
            for h in range(2):
                hm = head_mask[h]
                pr = probs[i * heads + 2 * c + h]
                dp = dot_nt(vp * hm, da)
                inner = jnp.sum(pr * dp, axis=0, keepdims=True)
                ds = (pr * (dp - inner)).astype(BF16)
                dv = dv + dot_nn(pr.astype(BF16), da * hm)
                dk = dk + dot_nn(ds, qp * hm)
                dq = dq + dot_tn(ds, kp * hm)
            dq = (dq * SCALE).astype(BF16)
            dv = dv.astype(BF16)
            act[here, c * 128 : (c + 1) * 128] = dq
            act[here, dim + c * 128 : dim + (c + 1) * 128] = (dk * SCALE).astype(BF16)
            act[here, 2 * dim + c * 128 : 2 * dim + (c + 1) * 128] = dv
            vec[6:7, c * 128 : (c + 1) * 128] += jnp.sum(dq.astype(F32), axis=0, keepdims=True)
            vec[7:8, c * 128 : (c + 1) * 128] += jnp.sum(dv.astype(F32), axis=0, keepdims=True)
        return carry

    lax.fori_loop(0, images, attend_back, 0)
    send_line(1)

    def qkv_grad(j, carry):
        cols = pl.ds(pl.multiple_of(j * 384, 128), 384)
        grd[:, cols] = dot_tn(n1[...], act[:, cols])
        return carry

    lax.fori_loop(0, 3, qkv_grad, 0)
    pack(0)
    send_sibling(0)

    def last_step(i, carry):
        here = image_rows(i)
        dn = dot_nt(act[here, 0 : 3 * dim], wts[0, :, 0 : 3 * dim])
        xhat, rstd = norm_parts(xpad[here, :].astype(F32))
        mid[here, :] = (mid[here, :] + norm_back(dn, xhat, rstd, gain1)) * grad_scale
        vec[0:1, 0:dim] += jnp.sum(dn * xhat, axis=0, keepdims=True)
        vec[1:2, 0:dim] += jnp.sum(dn, axis=0, keepdims=True)
        return carry

    lax.fori_loop(0, images, last_step, 0)
    vec_cp = remote(vec, vsib, vs_s.at[0], vs_r.at[0], {"tp": o})
    vec_cp.start()
    send_plane(0)

    for i in range(images):
        stage[i * SEQ : (i + 1) * SEQ, :] = opad[i * PAD : i * PAD + SEQ, :].astype(F32)

    def cast_out(c, carry):
        at_row = pl.ds(pl.multiple_of(c * 16, 16), 16)
        gp[at_row, 0:dim] = stage[at_row, :].astype(BF16)
        return carry

    lax.fori_loop(0, rows // 16, cast_out, 0)
    out_cp = pltpu.make_async_copy(gp.at[0:rows, 0:dim], out_h, dma_sem.at[0])
    out_cp.start()
    got(vsib, vs_r.at[0]).wait_recv()
    vpl[p] = vec[...] + vsib[...]
    for k in range(1, np_):
        cp = remote(vpl.at[p], vpl.at[p], vs_s.at[k], vs_r.at[k], at(l, plane_peer(k)))
        cp.start()
        late.append(cp)
    for i in range(images):
        stage[i * SEQ : (i + 1) * SEQ, :] = mid[i * PAD : i * PAD + SEQ, :]
    gin_cp = pltpu.make_async_copy(stage.at[0:rows, :], gin_h, dma_sem.at[1])
    gin_cp.start()
    for k in range(1, np_):
        src_p = lax.rem(p + np_ - k, np_)
        got(vpl.at[src_p], vs_r.at[k]).wait_recv()
    vln[l] = functools.reduce(lambda a, b: a + b, [vpl[pp] for pp in range(np_)])
    for k in range(1, nl):
        cp = remote(vln.at[l], vln.at[l], vs_s.at[np_ + k], vs_r.at[np_ + k], at(line_peer(k), p))
        cp.start()
        late.append(cp)
    send_line(0)

    for k in range(1, nl):
        src_l = lax.rem(l + nl - k, nl)
        got(vln.at[src_l], vs_r.at[np_ + k]).wait_recv()
    vec_o[...] = functools.reduce(lambda a, b: a + b, [vln[ll] for ll in range(nl)])
    kept_o[...] = kept
    sum_line(1)
    sum_line(2)
    sum_line(0)
    vec_cp.wait_send()
    out_cp.wait()
    gin_cp.wait()
    for cp in late:
        cp.wait_send()
    for cp in sib_sends.values():
        cp.wait_send()


def update_kernel(scale_rows, *refs):
    fin, vec, kept, out_in, gin_in = refs[:5]
    states = [refs[5 + 3 * k : 8 + 3 * k] for k in range(6)]
    out_h, gin_h = refs[23:25]
    q_o, p_o, a_o, c_o = (refs[25 + 4 * k : 29 + 4 * k] for k in range(4))
    n_o, b_o = refs[41:44], refs[44:47]
    out_v, gin_v, sems_in, sems_out = refs[47:]
    parts = 3
    size = out_in.shape[0] // parts
    loads, stores = [], []
    for k in range(parts):
        here = pl.ds(k * size, size)
        for j, (src, via, dst) in enumerate(((out_in, out_v, out_h), (gin_in, gin_v, gin_h))):
            loads.append(pltpu.make_async_copy(src.at[here, :], via.at[here, :], sems_in.at[j, k]))
            stores.append(pltpu.make_async_copy(via.at[here, :], dst.at[here, :], sems_out.at[j, k]))
    for cp in loads:
        cp.start()
    for load, store in zip(loads, stores):
        load.wait()
        store.start()
    qkv, proj, fc1, fc2, norm, bias = states
    r, hw = proj[0].shape
    fw = fc1[0].shape[1]
    half = fw // 2
    grad_scale = scale_rows / kept[0:1, 0:1]

    def update(grad, state, outs, rate, decay, c=None):
        pick = (lambda ref: ref[...]) if c is None else (lambda ref: ref[c])
        master, first, second = (pick(ref) for ref in state)
        first, second, master = adam(master, first, second, grad * grad_scale, rate, decay)
        for ref, value in zip(outs, (first, second, master, master)):
            if c is None:
                ref[...] = value.astype(ref.dtype)
            else:
                ref[c] = value.astype(ref.dtype)

    def halves(pc):
        g = fin[pc]
        return jnp.concatenate([g[0:r, :], g[r : 2 * r, :]], axis=1)

    g0 = fin[0]
    update(g0[0:r, 0:hw], qkv, q_o, 0.08, matrix_decay, 0)
    update(g0[0:r, hw:], qkv, q_o, 0.08, matrix_decay, 1)
    update(g0[r : 2 * r, 0:hw], qkv, q_o, 0.08, matrix_decay, 2)
    update(g0[r : 2 * r, hw:], proj, p_o, 0.8, matrix_decay)
    update(halves(1), fc1, a_o, 0.08, matrix_decay)
    update(halves(2), fc2, c_o, 0.04, matrix_decay)
    update(vec[0:6, 0 : norm[0].shape[1]], norm, n_o, 0.5, 0.0)
    own = lax.axis_index("tp") == 0

    def pick(row, width):
        return jnp.where(own, vec[row : row + 1, 0:width], vec[row : row + 1, width : 2 * width])

    update(jnp.concatenate([pick(6, hw), pick(7, hw), pick(8, fw)], axis=1), bias, b_o, 0.5, 0.0)
    for store in stores:
        store.wait()


def body(
    inputs, keep_mask, cotangent,
    qkv_master, qkv_first, qkv_second,
    proj_master, proj_first, proj_second,
    fc1_master, fc1_first, fc1_second,
    fc2_master, fc2_first, fc2_second,
    norm_master, norm_first, norm_second,
    bias_master, bias_first, bias_second,
):
    n = lax.axis_size("dp")
    nl = 4 if n % 4 == 0 else n
    np_ = n // nl
    rows, dim = inputs.shape
    images = rows // SEQ
    padded = images * PAD
    r = qkv_master.shape[1]
    hw = qkv_master.shape[2]
    fw = fc1_master.shape[1]
    ff = 2 * fw
    slot = -(-2 * r // 16) * 16
    keep = keep_mask.reshape(2 * images, SEQ)
    vm = pl.BlockSpec(memory_space=pltpu.VMEM)
    hbm = pl.BlockSpec(memory_space=pl.ANY)

    def like(a, dtype=None):
        return jax.ShapeDtypeStruct(a.shape, dtype or a.dtype)

    proj_master, proj_first, proj_second = proj_master.T, proj_first.T, proj_second.T
    fc2_master, fc2_first, fc2_second = fc2_master.T, fc2_first.T, fc2_second.T
    large = [like(inputs), like(inputs, F32)]
    sums = [
        jax.ShapeDtypeStruct((3, slot, dim), F32),
        jax.ShapeDtypeStruct((16, ff), F32),
        jax.ShapeDtypeStruct((8, 128), F32),
    ]
    dma = pltpu.SemaphoreType.DMA
    scratch = [
        pltpu.VMEM((3, 2, np_, nl, slot, dim), BF16),
        pltpu.VMEM((3, dim, ff), BF16),
        pltpu.VMEM((dim, ff), F32),
        pltpu.VMEM((3, np_, nl, slot, dim), BF16),
        pltpu.VMEM((3, np_, nl, slot, dim), BF16),
        pltpu.VMEM((3, nl, slot, dim), BF16),
        pltpu.VMEM((3, nl, slot, dim), BF16),
        pltpu.VMEM((slot, dim), F32),
        pltpu.VMEM((2, 8, bias_master.shape[1]), F32),
        pltpu.VMEM((nl, 8, 128), F32),
        pltpu.VMEM((np_, 8, 128), F32),
        pltpu.VMEM((16, ff), F32),
        pltpu.VMEM((16, ff), F32),
        pltpu.VMEM((np_, 16, ff), F32),
        pltpu.VMEM((nl, 16, ff), F32),
        pltpu.VMEM((-(-(rows - SEQ + PAD) // 16) * 16, dim), F32),
        pltpu.VMEM((padded, dim), F32),
        pltpu.VMEM((images * (dim // HEAD_DIM), PAD, PAD), F32),
        pltpu.VMEM((images, PAD, 128), F32),
        pltpu.VMEM((128, 256), F32),
        pltpu.VMEM((padded, dim), BF16),
        pltpu.VMEM((padded, dim), BF16),
        pltpu.VMEM((padded, dim), BF16),
        pltpu.VMEM((padded, 3 * dim), BF16),
        pltpu.VMEM((padded, dim), BF16),
        pltpu.VMEM((padded, dim), BF16),
        pltpu.VMEM((padded, dim), BF16),
        pltpu.VMEM((padded, dim), BF16),
        pltpu.VMEM((padded, dim), BF16),
        pltpu.VMEM((padded, ff), BF16),
        pltpu.VMEM((padded, ff), BF16),
        dma((3,)),
        dma((1,)),
        dma((3, nl)),
        dma((3, nl)),
        dma((3, np_)),
        dma((3, np_)),
        dma((3, np_)),
        dma((3, np_)),
        dma((3,)),
        dma((3,)),
        dma((3, np_)),
        dma((3, np_)),
        dma((3, nl)),
        dma((3, nl)),
        dma((nl,)),
        dma((nl,)),
        dma((np_,)),
        dma((np_,)),
        dma((np_ + nl,)),
        dma((np_ + nl,)),
    ]
    out, gin, fin, vec, kept = pl.pallas_call(
        functools.partial(kernel, nl, np_),
        out_shape=large + sums,
        in_specs=[hbm, vm, hbm] + [vm] * 6,
        out_specs=[hbm, hbm] + [vm] * 3,
        scratch_shapes=scratch,
        compiler_params=pltpu.CompilerParams(
            collective_id=0, has_side_effects=True, vmem_limit_bytes=64 * 1024 * 1024
        ),
    )(inputs, keep, cotangent, qkv_master, proj_master, fc1_master, fc2_master, norm_master, bias_master)
    states = [
        qkv_master, qkv_first, qkv_second,
        proj_master, proj_first, proj_second,
        fc1_master, fc1_first, fc1_second,
        fc2_master, fc2_first, fc2_second,
        norm_master, norm_first, norm_second,
        bias_master, bias_first, bias_second,
    ]
    outs = list(large)
    for a in (qkv_master, proj_master, fc1_master, fc2_master):
        outs += [like(a), like(a), like(a), like(a, BF16)]
    for a in (norm_master, bias_master):
        outs += [like(a)] * 3
    res = list(
        pl.pallas_call(
            functools.partial(update_kernel, rows * 2.0 * n),
            out_shape=outs,
            in_specs=[vm] * 3 + [hbm] * 2 + [vm] * 18,
            out_specs=[hbm] * 2 + [vm] * 22,
            scratch_shapes=[pltpu.VMEM((rows, dim), BF16), pltpu.VMEM((rows, dim), F32), dma((2, 3)), dma((2, 3))],
            compiler_params=pltpu.CompilerParams(vmem_limit_bytes=64 * 1024 * 1024),
        )(fin, vec, kept, out, gin, *states)
    )
    for k in (6, 7, 8, 9, 14, 15, 16, 17):
        res[k] = res[k].T
    return tuple(res)


def solution(mesh):
    mats = [P(None, "dp", "tp"), P("tp", "dp"), P("dp", "tp"), P("tp", "dp")]
    in_specs = [P(("dp", "tp"), None), P("dp"), P(("dp", "tp"), None)]
    out_specs = [P(("dp", "tp"), None), P(("dp", "tp"), None)]
    for m in mats:
        in_specs += [m] * 3
        out_specs += [m] * 4
    in_specs += [P()] * 3 + [P("tp", None)] * 3
    out_specs += [P()] * 3 + [P("tp", None)] * 3
    return jax.shard_map(
        body, mesh=mesh, in_specs=tuple(in_specs), out_specs=tuple(out_specs), check_vma=False
    )
```

```python
import functools

import jax
import jax.numpy as jnp
from jax import lax
from jax.experimental import pallas as pl
from jax.experimental.pallas import tpu as pltpu
from jax.sharding import PartitionSpec as P

HEAD_DIM = 64
PATCHES = 196
STEP = 5

norm_eps = 1e-06
beta_one = 0.9
beta_two = 0.999
adam_eps = 1e-08
matrix_decay = 0.05

F32 = jnp.float32
BF16 = jnp.bfloat16
MESH = pl.DeviceIdType.MESH
SEQ = PATCHES + 2
PAD = 208
NEG = -1000000000.0
SCALE = HEAD_DIM**-0.5
G_QKV, G_MID, G_FF, G_BACK, G_LAST = 8, 4, 8, 4, 4
U_ATT, U_ATB = 4, 2


def dot_nn(a, b):
    return lax.dot_general(a, b, (((1,), (0,)), ((), ())), preferred_element_type=F32)


def dot_nt(a, b):
    return lax.dot_general(a, b, (((1,), (1,)), ((), ())), preferred_element_type=F32)


def dot_tn(a, b):
    return lax.dot_general(a, b, (((0,), (0,)), ((), ())), preferred_element_type=F32)


def norm_parts(v):
    mean = jnp.mean(v, axis=-1, keepdims=True)
    centred = v - mean
    var = jnp.mean(centred * centred, axis=-1, keepdims=True)
    rstd = lax.rsqrt(var + norm_eps)
    return centred * rstd, rstd


def norm_back(grad, xhat, rstd, gain):
    u = grad * gain
    return (
        u
        - jnp.mean(u, axis=-1, keepdims=True)
        - xhat * jnp.mean(u * xhat, axis=-1, keepdims=True)
    ) * rstd


def gelu_parts(u):
    cdf = 0.5 + 0.5 * lax.erf(0.7071067811865476 * u)
    return u * cdf, cdf + u * (0.3989422804014327 * jnp.exp(-0.5 * u * u))


def adam(master, first, second, grad, rate, decay):
    first = beta_one * first + (1.0 - beta_one) * grad
    second = beta_two * second + (1.0 - beta_two) * grad * grad
    first_hat = first / (1.0 - beta_one**STEP)
    second_hat = second / (1.0 - beta_two**STEP)
    master = master - rate * (first_hat / (jnp.sqrt(second_hat) + adam_eps) + decay * master)
    return first, second, master


def piece_parts(piece, tt, hw, width):
    if piece == 0:
        return [(b, 0, 128, 384 * tt + 128 * b) for b in range(3)]
    if piece == 1:
        at, rest = 768, hw - 128
        proj = 1152 + hw * tt
        return [
            (0, 0, rest, at + rest * tt),
            (0, rest, rest, at + 128 + rest * tt),
            (1, 0, rest, at + 256 + rest * tt),
            (1, rest, rest, proj),
            (2, 0, 128, proj + rest),
        ]
    return [(0, 0, width, width * tt), (1, 0, width, 2 * width + width * tt)]


def kernel(
    nl,
    np_,
    x_h,
    keep_v,
    cot_h,
    qm,
    pm,
    am,
    cm,
    nm,
    bm,
    out_h,
    gin_h,
    fin_a,
    fin_m,
    vec_o,
    kept_o,
    wba,
    wbm,
    w_qkv,
    w_proj,
    w_ff,
    grd,
    sib_a,
    sib_m,
    rpl_a,
    rpl_m,
    lsn_a,
    lsn_m,
    rln_a,
    rln_m,
    pk_a,
    pk_m,
    bias2,
    cntl,
    cntp,
    vec,
    vsib,
    vpl,
    vln,
    stage,
    mid,
    acc_o,
    acc_d,
    probs,
    mcol,
    mkt,
    xpad,
    back,
    n1,
    qkv,
    att,
    n2,
    gbr,
    gatt,
    opad,
    act,
    gp,
    dqkv,
    dma_sem,
    ag_ls,
    ag_lr,
    ag_ps,
    ag_pr,
    ag_ss,
    ag_sr,
    rs_ss,
    rs_sr,
    rs_ps,
    rs_pr,
    rs_ls,
    rs_lr,
    cn_s,
    cn_r,
    cm_s,
    cm_r,
    vs_s,
    vs_r,
):
    rows, dim = x_h.shape
    images = rows // SEQ
    r = qm.shape[1]
    hw = qm.shape[2]
    width = wbm.shape[5]
    chunks = wbm.shape[0]
    chunk = 2 * width
    heads = dim // HEAD_DIM
    t = lax.axis_index("tp")
    d = lax.axis_index("dp")
    l = d // np_
    p = d - l * np_
    o = 1 - t
    first_half = t == 0

    def at(ll, pp):
        return {"dp": ll * np_ + pp}

    def line_peer(k):
        return lax.rem(l + k, nl)

    def line_from(k):
        return lax.rem(l + nl - k, nl)

    def plane_peer(k):
        return lax.rem(p + k, np_)

    def plane_from(k):
        return lax.rem(p + np_ - k, np_)

    x_in = pltpu.make_async_copy(x_h, dqkv.at[0:rows, 0:dim], dma_sem.at[0])
    c_in = pltpu.make_async_copy(cot_h, dqkv.at[0:rows, dim : 2 * dim], dma_sem.at[1])
    x_in.start()
    c_in.start()

    barrier = pltpu.get_barrier_semaphore()
    for k in range(1, nl):
        pl.semaphore_signal(barrier, inc=1, device_id=at(line_peer(k), p), device_id_type=MESH)
    for k in range(1, np_):
        pl.semaphore_signal(barrier, inc=1, device_id=at(l, plane_peer(k)), device_id_type=MESH)
    pl.semaphore_signal(barrier, inc=1, device_id={"tp": o}, device_id_type=MESH)

    def w_buf(pc):
        return wba.at[pc] if pc < 2 else wbm.at[pc - 2]

    def of(a_ref, m_ref, pc):
        return a_ref.at[pc] if pc < 2 else m_ref.at[pc - 2]

    def stacked(pc, blocks):
        pk = pk_a if pc < 2 else pk_m
        have, need = r * len(blocks), pk.shape[0]
        if r % 8 == 0:
            pad = [jnp.zeros((need - have, pk.shape[1]), F32)] if need > have else []
            return jnp.concatenate(list(blocks) + pad, axis=0)
        if need > have:
            pk[...] = jnp.zeros_like(pk)
        for b, block in enumerate(blocks):
            pk[b * r : (b + 1) * r, :] = block
        return pk[...]

    def either(a, b):
        return jnp.where(first_half, a, b)

    rest = hw - 128
    q3 = [qm[c] for c in range(3)]
    big = [either(q[:, 0:128], q[:, rest:]) for q in q3]
    small = [either(q[:, 128:], q[:, 0:rest]) for q in q3]
    wba[0, t, p, l] = stacked(0, big).astype(BF16)
    proj_own = pm[...]
    wba[1, t, p, l] = stacked(
        1,
        [
            jnp.concatenate([small[0], small[1]], axis=1),
            jnp.concatenate([small[2], proj_own[:, 0:rest]], axis=1),
            proj_own[:, rest:],
        ],
    ).astype(BF16)
    for j in range(chunks):
        cols = slice(j * width, (j + 1) * width)
        wbm[j, t, p, l] = stacked(2 + j, [am[:, cols], cm[:, cols]]).astype(BF16)
    bias2[t] = jnp.broadcast_to(bm[...], bias2.shape[1:])
    keep_all = keep_v[...].astype(F32)
    count = jnp.sum(jnp.sum(keep_all, axis=1, keepdims=True), axis=0, keepdims=True)
    cntl[l] = jnp.broadcast_to(count, cntl.shape[1:])

    pl.semaphore_wait(barrier, nl - 1 + np_ - 1 + 1)

    def remote(src, dst, ssem, rsem, device):
        return pltpu.make_async_remote_copy(
            src_ref=src, dst_ref=dst, send_sem=ssem, recv_sem=rsem, device_id=device, device_id_type=MESH
        )

    def got(dst, rsem):
        return remote(dst, dst, dma_sem.at[2], rsem, {"tp": o})

    sends = {pc: [] for pc in range(2 + chunks)}

    def send(pc, src, dst, ssem, rsem, device):
        cp = remote(src, dst, ssem, rsem, device)
        cp.start()
        sends[pc].append(cp)

    def to_plane(pc, ll, kl):
        here = w_buf(pc).at[t, p, ll]
        for k in range(1, np_):
            send(pc, here, here, ag_ps.at[pc, kl, k], ag_pr.at[pc, kl, k], at(l, plane_peer(k)))

    def start_piece(pc):
        here = w_buf(pc).at[t, p, l]
        for k in range(1, nl):
            send(pc, here, here, ag_ls.at[pc, k], ag_lr.at[pc, k], at(line_peer(k), p))
        to_plane(pc, l, 0)

    def line_done(pc):
        for k in range(1, nl):
            ll = line_from(k)
            got(w_buf(pc).at[t, p, ll], ag_lr.at[pc, k]).wait_recv()
            to_plane(pc, ll, k)
        here = w_buf(pc).at[t, p]
        send(pc, here, here, ag_ss.at[pc, 0], ag_sr.at[pc, 0], {"tp": o})

    def plane_done(pc):
        for k in range(1, np_):
            pp = plane_from(k)
            for kl in range(nl):
                got(w_buf(pc).at[t, pp, line_from(kl) if kl else l], ag_pr.at[pc, kl, k]).wait_recv()
            here = w_buf(pc).at[t, pp]
            send(pc, here, here, ag_ss.at[pc, k], ag_sr.at[pc, k], {"tp": o})

    def sibling_done(pc):
        for k in range(np_):
            got(w_buf(pc).at[o, plane_from(k) if k else p], ag_sr.at[pc, k]).wait_recv()

    def assemble(pc):
        for tt in range(2):
            for ll in range(nl):
                for pp in range(np_):
                    slot = w_buf(pc)[tt, pp, ll].astype(F32)
                    row = (ll * np_ + pp) * r
                    for b, lane_at, cols, col in piece_parts(pc, tt, hw, width):
                        grd[row : row + r, col : col + cols] = slot[b * r : (b + 1) * r, lane_at : lane_at + cols]
        if pc == 0:
            w_qkv[:, 0:768] = grd[:, 0:768].astype(BF16)
        elif pc == 1:
            w_qkv[:, 768:1152] = grd[:, 768:1152].astype(BF16)
            w_proj[...] = grd[:, 1152:1536].astype(BF16)
        else:
            w_ff[pc - 2] = grd[:, 0 : 2 * chunk].astype(BF16)

    start_piece(0)
    send(0, bias2.at[t], bias2.at[t], cm_s.at[0], cm_r.at[0], {"tp": o})
    for k in range(1, nl):
        send(0, cntl.at[l], cntl.at[l], cn_s.at[k], cn_r.at[k], at(line_peer(k), p))

    def cast_in(col):
        def step(c, carry):
            at_row = pl.ds(pl.multiple_of(c * 16, 16), 16)
            stage[at_row, :] = dqkv[at_row, col : col + dim].astype(F32)
            return carry

        lax.fori_loop(0, rows // 16, step, 0)

    stage[rows:, :] = jnp.zeros((stage.shape[0] - rows, dim), F32)
    own_keep = keep_v[pl.ds(pl.multiple_of(t * images, images), images), :].astype(F32)
    mkt[...] = jnp.zeros_like(mkt)
    mkt[0:images, 0:SEQ] = own_keep
    keep_t = mkt[...].T
    for i in range(images):
        mcol[i] = jnp.broadcast_to(keep_t[0:PAD, i : i + 1], (PAD, 128))
    inside = lax.broadcasted_iota(jnp.int32, (PAD, dim), 0) < SEQ
    x_in.wait()
    cast_in(0)
    gain1, shift1 = nm[0:1, :], nm[1:2, :]

    def norm_in(i):
        v = jnp.where(inside, stage[i * SEQ : i * SEQ + PAD, :], 0.0)
        xpad[i * PAD : (i + 1) * PAD, :] = v.astype(BF16)
        xhat, _ = norm_parts(v)
        n1[i * PAD : (i + 1) * PAD, :] = (xhat * gain1 + shift1).astype(BF16)

    for i in range(images // 4):
        norm_in(i)
    line_done(0)
    start_piece(1)
    for k in range(1, nl):
        got(cntl.at[line_from(k)], cn_r.at[k]).wait_recv()
    cntp[p] = functools.reduce(lambda a, b: a + b, [cntl[ll] for ll in range(nl)])
    for k in range(1, np_):
        send(0, cntp.at[p], cntp.at[p], cm_s.at[k], cm_r.at[k], at(l, plane_peer(k)))
    for i in range(images // 4, images):
        norm_in(i)
    plane_done(0)
    line_done(1)
    for j in range(chunks):
        start_piece(2 + j)
    sibling_done(0)
    got(bias2.at[o], cm_r.at[0]).wait_recv()
    assemble(0)

    def image_rows(i, many=1):
        return pl.ds(pl.multiple_of(i * (many * PAD), 16), many * PAD)

    def over_images(step, many=1, unroll=1):
        lax.fori_loop(0, images // many, lambda i, carry: step(i) or carry, 0, unroll=unroll)

    order = (0, 2, 1)
    both = [bias2[0, 0:1, :], bias2[1, 0:1, :]]
    q_bias = jnp.concatenate([b[:, 0:hw] for b in both], axis=1)
    v_bias = jnp.concatenate([b[:, hw : 2 * hw] for b in both], axis=1)
    h_bias = [
        jnp.concatenate([b[:, 2 * hw + j * width : 2 * hw + (j + 1) * width] for b in both], axis=1)
        for j in range(chunks)
    ]

    def pair_bias(pos):
        cols = slice(128 * order[pos], 128 * order[pos] + 128)
        return jnp.concatenate([q_bias[:, cols], jnp.zeros((1, 128), F32), v_bias[:, cols]], axis=1)

    def qkv_rows(group):
        cols = slice(384 * group[0], 384 * group[-1] + 384)
        bias = jnp.concatenate([pair_bias(pos) for pos in group], axis=1)

        def step(i):
            here = image_rows(i, G_QKV)
            qkv[here, cols] = (dot_nn(n1[here, :], w_qkv[:, cols]) + bias).astype(BF16)

        over_images(step, G_QKV)

    lane = lax.broadcasted_iota(jnp.int32, (1, 128), 1)
    head_mask = [(lane < HEAD_DIM).astype(F32).astype(BF16), (lane >= HEAD_DIM).astype(F32).astype(BF16)]
    head_scale = [(SCALE * mask.astype(F32)).astype(BF16) for mask in head_mask]

    def attend(group):
        def step(i):
            here = image_rows(i)
            m = mcol[i]
            m = jnp.concatenate([m, m], axis=1)[:, 0:PAD] > 0.0
            for pos in group:
                c = order[pos]
                qp, kp, vp = (qkv[here, 384 * pos + 128 * b : 384 * pos + 128 * b + 128] for b in range(3))
                total = None
                for h in range(2):
                    s = jnp.where(m, dot_nt(kp * head_scale[h], qp), NEG)
                    e = jnp.exp(s - jnp.max(s, axis=0, keepdims=True))
                    pr = e * (1.0 / jnp.sum(e, axis=0, keepdims=True))
                    probs[i * heads + 2 * pos + h] = pr
                    term = dot_tn(pr.astype(BF16), vp * head_mask[h])
                    total = term if total is None else total + term
                att[here, c * 128 : (c + 1) * 128] = total.astype(BF16)

        over_images(step, unroll=U_ATT)

    qkv_rows((0, 1))
    plane_done(1)
    line_done(2)
    attend((0, 1))
    sibling_done(1)
    for j in range(1, chunks):
        line_done(2 + j)
    assemble(1)
    qkv_rows((2,))
    plane_done(2)

    c_in.wait()
    cast_in(dim)
    for i in range(images):
        v = jnp.where(inside, stage[i * SEQ : i * SEQ + PAD, :], 0.0)
        m = mcol[i]
        back[i * PAD : (i + 1) * PAD, :] = (v * jnp.concatenate([m] * (dim // 128), axis=1)).astype(BF16)
    attend((2,))
    for j in range(1, chunks):
        plane_done(2 + j)
    for k in range(1, np_):
        got(cntp.at[plane_from(k)], cm_r.at[k]).wait_recv()
    kept = functools.reduce(lambda a, b: a + b, [cntp[pp] for pp in range(np_)])
    grad_scale = (rows * 2.0 * nl * np_) / kept[0:1, 0:1]

    vec[...] = jnp.zeros_like(vec)
    bias4, gain2, shift2, bias5 = nm[4:5, :], nm[2:3, :], nm[3:4, :], nm[5:6, :]

    def mid_step(i):
        here = image_rows(i, G_MID)
        m = xpad[here, :].astype(F32) + (dot_nt(att[here, :], w_proj[...]) + bias4)
        mid[here, :] = m
        xhat, _ = norm_parts(m)
        n2[here, :] = (xhat * gain2 + shift2).astype(BF16)

    over_images(mid_step, G_MID)

    def pack(pc):
        for cp in sends[pc]:
            cp.wait_send()
        for tt in range(2):
            parts = piece_parts(pc, tt, hw, width)
            for ll in range(nl):
                for pp in range(np_):
                    row = (ll * np_ + pp) * r
                    blocks = []
                    for b in range(parts[-1][0] + 1):
                        own = [grd[row : row + r, col : col + cols] for bb, _, cols, col in parts if bb == b]
                        blocks.append(jnp.concatenate(own, axis=1) if len(own) > 1 else own[0])
                    w_buf(pc)[tt, pp, ll] = stacked(pc, blocks).astype(BF16)

    late = []

    def send_late(src, dst, ssem, rsem, device):
        cp = remote(src, dst, ssem, rsem, device)
        cp.start()
        late.append(cp)

    def send_sibling(pc):
        send_late(w_buf(pc).at[o], of(sib_a, sib_m, pc), rs_ss.at[pc], rs_sr.at[pc], {"tp": o})

    def send_plane(pc):
        sib, rpl = of(sib_a, sib_m, pc), of(rpl_a, rpl_m, pc)
        got(sib, rs_sr.at[pc]).wait_recv()
        for pp in range(np_):
            for ll in range(nl):
                sib[pp, ll] = (sib[pp, ll].astype(F32) + w_buf(pc)[t, pp, ll].astype(F32)).astype(BF16)
        for k in range(1, np_):
            send_late(sib.at[plane_peer(k)], rpl.at[p], rs_ps.at[pc, k], rs_pr.at[pc, k], at(l, plane_peer(k)))
        rpl[p] = sib[p]

    def send_line(pc):
        rpl, lsn, rln = of(rpl_a, rpl_m, pc), of(lsn_a, lsn_m, pc), of(rln_a, rln_m, pc)
        for k in range(1, np_):
            got(rpl.at[plane_from(k)], rs_pr.at[pc, k]).wait_recv()
        for ll in range(nl):
            lsn[ll] = functools.reduce(
                lambda a, b: a + b, [rpl[pp, ll].astype(F32) for pp in range(np_)]
            ).astype(BF16)
        for k in range(1, nl):
            send_late(lsn.at[line_peer(k)], rln.at[l], rs_ls.at[pc, k], rs_lr.at[pc, k], at(line_peer(k), p))
        rln[l] = lsn[l]

    def sum_line(pc):
        rln, fin = of(rln_a, rln_m, pc), of(fin_a, fin_m, pc)
        for k in range(1, nl):
            got(rln.at[line_from(k)], rs_lr.at[pc, k]).wait_recv()
        fin[...] = functools.reduce(lambda a, b: a + b, [rln[ll].astype(F32) for ll in range(nl)])

    def ff_chunk(j):
        def step(i):
            here = image_rows(i, G_FF)
            b = back[here, :]
            w1, w2 = w_ff[j, :, 0:chunk], w_ff[j, :, chunk : 2 * chunk]
            pre = dot_nn(n2[here, :], w1) + h_bias[j]
            ga = dot_nn(b, w2)
            value, slope = gelu_parts(pre)
            value = value.astype(BF16)
            gpre = (ga * slope).astype(BF16)
            act[here, :] = value
            gp[here, :] = gpre
            vec[8 + j : 9 + j, :] += jnp.sum(gpre.astype(F32), axis=0, keepdims=True)
            term_o = dot_nt(value, w2)
            term_d = dot_nt(gpre, w1)
            if j == 0:
                acc_o[here, :] = term_o
                acc_d[here, :] = term_d
            else:
                acc_o[here, :] += term_o
                acc_d[here, :] += term_d

        over_images(step, G_FF)
        grd[:, 0:chunk] = dot_tn(n2[...], gp[...])
        grd[:, chunk : 2 * chunk] = dot_tn(back[...], act[...])

    for j in range(chunks):
        sibling_done(2 + j)
        assemble(2 + j)
        ff_chunk(j)
        pack(2 + j)
        send_sibling(2 + j)
        if j > 0:
            send_line(1 + j)
        send_plane(2 + j)

    def back_step(i):
        here = image_rows(i, G_BACK)
        m = mid[here, :]
        opad[here, :] = (m + (acc_o[here, :] + bias5)).astype(BF16)
        xhat, rstd = norm_parts(m)
        dn = acc_d[here, :]
        bfl = back[here, :].astype(F32)
        gm = bfl + norm_back(dn, xhat, rstd, gain2)
        mid[here, :] = gm
        g16 = gm.astype(BF16)
        gbr[here, :] = g16
        gatt[here, :] = dot_nn(g16, w_proj[...]).astype(BF16)
        vec[2:3, 0:dim] += jnp.sum(dn * xhat, axis=0, keepdims=True)
        vec[3:4, 0:dim] += jnp.sum(dn, axis=0, keepdims=True)
        vec[4:5, 0:dim] += jnp.sum(g16.astype(F32), axis=0, keepdims=True)
        vec[5:6, 0:dim] += jnp.sum(bfl, axis=0, keepdims=True)

    over_images(back_step, G_BACK)

    def attend_back(group):
        def step(i):
            here = image_rows(i)
            for pos in group:
                c = order[pos]
                qp, kp, vp = (qkv[here, 384 * pos + 128 * b : 384 * pos + 128 * b + 128] for b in range(3))
                da = gatt[here, c * 128 : (c + 1) * 128]
                dq = dk = dv = 0.0
                for h in range(2):
                    hm = head_mask[h]
                    pr = probs[i * heads + 2 * pos + h]
                    dp = dot_nt(vp * hm, da)
                    inner = jnp.sum(pr * dp, axis=0, keepdims=True)
                    ds = (pr * (dp - inner)).astype(BF16)
                    dv = dv + dot_nn(pr.astype(BF16), da * hm)
                    dk = dk + dot_nn(ds, qp * head_scale[h])
                    dq = dq + dot_tn(ds, kp * head_scale[h])
                dq = dq.astype(BF16)
                dv = dv.astype(BF16)
                dqkv[here, 384 * pos : 384 * pos + 128] = dq
                dqkv[here, 384 * pos + 128 : 384 * pos + 256] = dk.astype(BF16)
                dqkv[here, 384 * pos + 256 : 384 * pos + 384] = dv
                vec[6:7, c * 128 : (c + 1) * 128] += jnp.sum(dq.astype(F32), axis=0, keepdims=True)
                vec[7:8, c * 128 : (c + 1) * 128] += jnp.sum(dv.astype(F32), axis=0, keepdims=True)

        over_images(step, unroll=U_ATB)

    attend_back((0, 1))
    send_line(1 + chunks)
    for pos in range(2):
        cols = slice(384 * pos, 384 * pos + 384)
        grd[:, cols] = dot_tn(n1[...], dqkv[:, cols])
    pack(0)
    send_sibling(0)
    grd[:, 1152:1536] = dot_tn(gbr[...], att[...])
    send_plane(0)
    attend_back((2,))
    grd[:, 768:1152] = dot_tn(n1[...], dqkv[:, 768:1152])
    pack(1)
    send_sibling(1)
    send_line(0)
    send_plane(1)

    def last_step(i):
        here = image_rows(i, G_LAST)
        dn = dot_nt(dqkv[here, :], w_qkv[...])
        xhat, rstd = norm_parts(xpad[here, :].astype(F32))
        mid[here, :] = (mid[here, :] + norm_back(dn, xhat, rstd, gain1)) * grad_scale
        vec[0:1, 0:dim] += jnp.sum(dn * xhat, axis=0, keepdims=True)
        vec[1:2, 0:dim] += jnp.sum(dn, axis=0, keepdims=True)

    over_images(last_step, G_LAST)
    send_late(vec, vsib, vs_s.at[0], vs_r.at[0], {"tp": o})

    for i in range(images):
        stage[i * SEQ : (i + 1) * SEQ, :] = opad[i * PAD : i * PAD + SEQ, :].astype(F32)

    def cast_out(c, carry):
        at_row = pl.ds(pl.multiple_of(c * 16, 16), 16)
        n2[at_row, :] = stage[at_row, :].astype(BF16)
        return carry

    lax.fori_loop(0, rows // 16, cast_out, 0)
    out_cp = pltpu.make_async_copy(n2.at[0:rows, :], out_h, dma_sem.at[0])
    out_cp.start()
    got(vsib, vs_r.at[0]).wait_recv()
    vpl[p] = vec[...] + vsib[...]
    for k in range(1, np_):
        send_late(vpl.at[p], vpl.at[p], vs_s.at[k], vs_r.at[k], at(l, plane_peer(k)))
    for i in range(images):
        stage[i * SEQ : (i + 1) * SEQ, :] = mid[i * PAD : i * PAD + SEQ, :]
    gin_cp = pltpu.make_async_copy(stage.at[0:rows, :], gin_h, dma_sem.at[1])
    gin_cp.start()
    send_line(1)
    for k in range(1, np_):
        got(vpl.at[plane_from(k)], vs_r.at[k]).wait_recv()
    vln[l] = functools.reduce(lambda a, b: a + b, [vpl[pp] for pp in range(np_)])
    for k in range(1, nl):
        send_late(vln.at[l], vln.at[l], vs_s.at[np_ + k], vs_r.at[np_ + k], at(line_peer(k), p))
    kept_o[...] = kept
    for pc in range(2, 2 + chunks):
        sum_line(pc)
    sum_line(0)
    sum_line(1)
    for k in range(1, nl):
        got(vln.at[line_from(k)], vs_r.at[np_ + k]).wait_recv()
    vec_o[...] = functools.reduce(lambda a, b: a + b, [vln[ll] for ll in range(nl)])
    out_cp.wait()
    gin_cp.wait()
    for cp in late:
        cp.wait_send()


def update_kernel(scale_rows, *refs):
    fin_a, fin_m, vec, kept, out_in, gin_in = refs[:6]
    states = [refs[6 + 3 * k : 9 + 3 * k] for k in range(6)]
    out_h, gin_h = refs[24:26]
    q_o, p_o, a_o, c_o = (refs[26 + 4 * k : 30 + 4 * k] for k in range(4))
    n_o, b_o = refs[42:45], refs[45:48]
    out_v, gin_v, sems_in, sems_out = refs[48:]
    parts = 3
    size = out_in.shape[0] // parts
    loads, stores = [], []
    for k in range(parts):
        here = pl.ds(k * size, size)
        for j, (src, via, dst) in enumerate(((out_in, out_v, out_h), (gin_in, gin_v, gin_h))):
            loads.append(pltpu.make_async_copy(src.at[here, :], via.at[here, :], sems_in.at[j, k]))
            stores.append(pltpu.make_async_copy(via.at[here, :], dst.at[here, :], sems_out.at[j, k]))
    for cp in loads:
        cp.start()
    for load, store in zip(loads, stores):
        load.wait()
        store.start()
    qkv, proj, fc1, fc2, norm, bias = states
    r, hw = proj[0].shape
    rest = hw - 128
    chunks, _, width = fin_m.shape
    own = lax.axis_index("tp") == 0
    grad_scale = scale_rows / kept[0:1, 0:1]

    def update(grad, state, outs, rate, decay, c=None):
        pick = (lambda ref: ref[...]) if c is None else (lambda ref: ref[c])
        master, first, second = (pick(ref) for ref in state)
        first, second, master = adam(master, first, second, grad * grad_scale, rate, decay)
        for ref, value in zip(outs, (first, second, master, master)):
            if c is None:
                ref[...] = value.astype(ref.dtype)
            else:
                ref[c] = value.astype(ref.dtype)

    big, small = fin_a[0], fin_a[1]
    pieces = (small[0:r, 0:rest], small[0:r, rest:], small[r : 2 * r, 0:rest])
    for c in range(3):
        first, second = big[c * r : (c + 1) * r, :], pieces[c]
        grad = jnp.where(
            own, jnp.concatenate([first, second], axis=1), jnp.concatenate([second, first], axis=1)
        )
        update(grad, qkv, q_o, 0.08, matrix_decay, c)
    update(
        jnp.concatenate([small[r : 2 * r, rest:], small[2 * r : 3 * r, :]], axis=1), proj, p_o, 0.8, matrix_decay
    )
    update(jnp.concatenate([fin_m[j, 0:r, :] for j in range(chunks)], axis=1), fc1, a_o, 0.08, matrix_decay)
    update(jnp.concatenate([fin_m[j, r : 2 * r, :] for j in range(chunks)], axis=1), fc2, c_o, 0.04, matrix_decay)
    update(vec[0:6, 0 : norm[0].shape[1]], norm, n_o, 0.5, 0.0)

    def pick(row, cols):
        return jnp.where(own, vec[row : row + 1, 0:cols], vec[row : row + 1, cols : 2 * cols])

    bias_parts = [pick(6, hw), pick(7, hw)] + [pick(8 + j, width) for j in range(chunks)]
    update(jnp.concatenate(bias_parts, axis=1), bias, b_o, 0.5, 0.0)
    for store in stores:
        store.wait()


def body(
    inputs, keep_mask, cotangent,
    qkv_master, qkv_first, qkv_second,
    proj_master, proj_first, proj_second,
    fc1_master, fc1_first, fc1_second,
    fc2_master, fc2_first, fc2_second,
    norm_master, norm_first, norm_second,
    bias_master, bias_first, bias_second,
):
    n = lax.axis_size("dp")
    nl = 4 if n % 4 == 0 else n
    np_ = n // nl
    rows, dim = inputs.shape
    images = rows // SEQ
    padded = images * PAD
    r = qkv_master.shape[1]
    hw = qkv_master.shape[2]
    fw = fc1_master.shape[1]
    width = 256
    chunks = fw // width
    chunk = 2 * width
    slot_a = -(-3 * r // 16) * 16
    slot_m = -(-2 * r // 16) * 16
    keep = keep_mask.reshape(2 * images, SEQ)
    vm = pl.BlockSpec(memory_space=pltpu.VMEM)
    hbm = pl.BlockSpec(memory_space=pl.ANY)

    def like(a, dtype=None):
        return jax.ShapeDtypeStruct(a.shape, dtype or a.dtype)

    proj_master, proj_first, proj_second = proj_master.T, proj_first.T, proj_second.T
    fc2_master, fc2_first, fc2_second = fc2_master.T, fc2_first.T, fc2_second.T
    large = [like(inputs), like(inputs, F32)]
    sums = [
        jax.ShapeDtypeStruct((2, slot_a, 128), F32),
        jax.ShapeDtypeStruct((chunks, slot_m, width), F32),
        jax.ShapeDtypeStruct((16, chunk), F32),
        jax.ShapeDtypeStruct((8, 128), F32),
    ]
    dma = pltpu.SemaphoreType.DMA
    pieces = 2 + chunks
    scratch = [
        pltpu.VMEM((2, 2, np_, nl, slot_a, 128), BF16),
        pltpu.VMEM((chunks, 2, np_, nl, slot_m, width), BF16),
        pltpu.VMEM((dim, 3 * dim), BF16),
        pltpu.VMEM((dim, dim), BF16),
        pltpu.VMEM((chunks, dim, 2 * chunk), BF16),
        pltpu.VMEM((dim, 4 * dim), F32),
        pltpu.VMEM((2, np_, nl, slot_a, 128), BF16),
        pltpu.VMEM((chunks, np_, nl, slot_m, width), BF16),
        pltpu.VMEM((2, np_, nl, slot_a, 128), BF16),
        pltpu.VMEM((chunks, np_, nl, slot_m, width), BF16),
        pltpu.VMEM((2, nl, slot_a, 128), BF16),
        pltpu.VMEM((chunks, nl, slot_m, width), BF16),
        pltpu.VMEM((2, nl, slot_a, 128), BF16),
        pltpu.VMEM((chunks, nl, slot_m, width), BF16),
        pltpu.VMEM((slot_a, 128), F32),
        pltpu.VMEM((slot_m, width), F32),
        pltpu.VMEM((2, 8, bias_master.shape[1]), F32),
        pltpu.VMEM((nl, 8, 128), F32),
        pltpu.VMEM((np_, 8, 128), F32),
        pltpu.VMEM((16, chunk), F32),
        pltpu.VMEM((16, chunk), F32),
        pltpu.VMEM((np_, 16, chunk), F32),
        pltpu.VMEM((nl, 16, chunk), F32),
        pltpu.VMEM((-(-(rows - SEQ + PAD) // 16) * 16, dim), F32),
        pltpu.VMEM((padded, dim), F32),
        pltpu.VMEM((padded, dim), F32),
        pltpu.VMEM((padded, dim), F32),
        pltpu.VMEM((images * (dim // HEAD_DIM), PAD, PAD), F32),
        pltpu.VMEM((images, PAD, 128), F32),
        pltpu.VMEM((128, 256), F32),
        pltpu.VMEM((padded, dim), BF16),
        pltpu.VMEM((padded, dim), BF16),
        pltpu.VMEM((padded, dim), BF16),
        pltpu.VMEM((padded, 3 * dim), BF16),
        pltpu.VMEM((padded, dim), BF16),
        pltpu.VMEM((padded, dim), BF16),
        pltpu.VMEM((padded, dim), BF16),
        pltpu.VMEM((padded, dim), BF16),
        pltpu.VMEM((padded, dim), BF16),
        pltpu.VMEM((padded, chunk), BF16),
        pltpu.VMEM((padded, chunk), BF16),
        pltpu.VMEM((padded, 3 * dim), BF16),
        dma((3,)),
        dma((pieces, nl)),
        dma((pieces, nl)),
        dma((pieces, nl, np_)),
        dma((pieces, nl, np_)),
        dma((pieces, np_)),
        dma((pieces, np_)),
        dma((pieces,)),
        dma((pieces,)),
        dma((pieces, np_)),
        dma((pieces, np_)),
        dma((pieces, nl)),
        dma((pieces, nl)),
        dma((nl,)),
        dma((nl,)),
        dma((np_,)),
        dma((np_,)),
        dma((np_ + nl,)),
        dma((np_ + nl,)),
    ]
    out, gin, fin_a, fin_m, vec, kept = pl.pallas_call(
        functools.partial(kernel, nl, np_),
        out_shape=large + sums,
        in_specs=[hbm, vm, hbm] + [vm] * 6,
        out_specs=[hbm, hbm] + [vm] * 4,
        scratch_shapes=scratch,
        compiler_params=pltpu.CompilerParams(
            collective_id=0, has_side_effects=True, vmem_limit_bytes=64 * 1024 * 1024
        ),
    )(inputs, keep, cotangent, qkv_master, proj_master, fc1_master, fc2_master, norm_master, bias_master)
    states = [
        qkv_master, qkv_first, qkv_second,
        proj_master, proj_first, proj_second,
        fc1_master, fc1_first, fc1_second,
        fc2_master, fc2_first, fc2_second,
        norm_master, norm_first, norm_second,
        bias_master, bias_first, bias_second,
    ]
    outs = list(large)
    for a in (qkv_master, proj_master, fc1_master, fc2_master):
        outs += [like(a), like(a), like(a), like(a, BF16)]
    for a in (norm_master, bias_master):
        outs += [like(a)] * 3
    res = list(
        pl.pallas_call(
            functools.partial(update_kernel, rows * 2.0 * n),
            out_shape=outs,
            in_specs=[vm] * 4 + [hbm] * 2 + [vm] * 18,
            out_specs=[hbm] * 2 + [vm] * 22,
            scratch_shapes=[pltpu.VMEM((rows, dim), BF16), pltpu.VMEM((rows, dim), F32), dma((2, 3)), dma((2, 3))],
            compiler_params=pltpu.CompilerParams(vmem_limit_bytes=64 * 1024 * 1024),
        )(fin_a, fin_m, vec, kept, out, gin, *states)
    )
    for k in (6, 7, 8, 9, 14, 15, 16, 17):
        res[k] = res[k].T
    return tuple(res)


def solution(mesh):
    mats = [P(None, "dp", "tp"), P("tp", "dp"), P("dp", "tp"), P("tp", "dp")]
    in_specs = [P(("dp", "tp"), None), P("dp"), P(("dp", "tp"), None)]
    out_specs = [P(("dp", "tp"), None), P(("dp", "tp"), None)]
    for m in mats:
        in_specs += [m] * 3
        out_specs += [m] * 4
    in_specs += [P()] * 3 + [P("tp", None)] * 3
    out_specs += [P()] * 3 + [P("tp", None)] * 3
    return jax.shard_map(
        body, mesh=mesh, in_specs=tuple(in_specs), out_specs=tuple(out_specs), check_vma=False
    )
```

```python
import functools

import jax
import jax.numpy as jnp
from jax import lax
from jax.experimental import pallas as pl
from jax.experimental.pallas import tpu as pltpu
from jax.sharding import PartitionSpec as P

HEAD_DIM = 64
PATCHES = 196
STEP = 5

norm_eps = 1e-06
beta_one = 0.9
beta_two = 0.999
adam_eps = 1e-08
matrix_decay = 0.05

F32 = jnp.float32
BF16 = jnp.bfloat16
MESH = pl.DeviceIdType.MESH
SEQ = PATCHES + 2
PAD = 208
WIDE = 256
NEG = -1000000000.0
SCALE = HEAD_DIM**-0.5
G_QKV, G_MID, G_FF, G_BACK, G_LAST, G_OUT = 8, 4, 8, 4, 4, 4
U_ATT, U_ATB = 8, 4


def dot_nn(a, b):
    return lax.dot_general(a, b, (((1,), (0,)), ((), ())), preferred_element_type=F32)


def dot_nt(a, b):
    return lax.dot_general(a, b, (((1,), (1,)), ((), ())), preferred_element_type=F32)


def dot_tn(a, b):
    return lax.dot_general(a, b, (((0,), (0,)), ((), ())), preferred_element_type=F32)


def norm_parts(v):
    mean = jnp.mean(v, axis=-1, keepdims=True)
    centred = v - mean
    var = jnp.mean(centred * centred, axis=-1, keepdims=True)
    rstd = lax.rsqrt(var + norm_eps)
    return centred * rstd, rstd


def norm_back(grad, xhat, rstd, gain):
    u = grad * gain
    return (
        u
        - jnp.mean(u, axis=-1, keepdims=True)
        - xhat * jnp.mean(u * xhat, axis=-1, keepdims=True)
    ) * rstd


def gelu_parts(u):
    cdf = 0.5 + 0.5 * lax.erf(0.7071067811865476 * u)
    return u * cdf, cdf + u * (0.3989422804014327 * jnp.exp(-0.5 * u * u))


def adam(master, first, second, grad, rate, decay):
    first = beta_one * first + (1.0 - beta_one) * grad
    second = beta_two * second + (1.0 - beta_two) * grad * grad
    first_hat = first / (1.0 - beta_one**STEP)
    second_hat = second / (1.0 - beta_two**STEP)
    master = master - rate * (first_hat / (jnp.sqrt(second_hat) + adam_eps) + decay * master)
    return first, second, master


def piece_parts(piece, tt, pairs, width):
    if piece < pairs:
        return [(b // 2, 64 * (b % 2), 64, 128 * b + 64 * tt) for b in range(4)]
    return [(0, 0, width, width * tt), (1, 0, width, 2 * width + width * tt)]


def kernel(
    nl,
    np_,
    x_h,
    keep_h,
    cot_h,
    qm_h,
    pm_h,
    am_h,
    cm_h,
    nm_h,
    bm_h,
    out_h,
    gin_h,
    fin_a,
    fin_m,
    vec_o,
    kept_o,
    keep_v,
    qm,
    pm,
    am,
    cm,
    nm,
    bm,
    wba,
    wbm,
    w_qkv,
    w_proj,
    w_up,
    w_down,
    grd,
    sib_a,
    sib_m,
    rpl_a,
    rpl_m,
    lsn_a,
    lsn_m,
    rln_a,
    rln_m,
    pk_a,
    pk_m,
    bias2,
    cntl,
    cntp,
    vec,
    vsib,
    vpl,
    vln,
    stage,
    mid,
    gmid,
    probs,
    even,
    odd,
    mcol,
    mkt,
    xpad,
    back,
    n1,
    qkv,
    att,
    n2,
    gbr,
    gatt,
    act,
    gp,
    dqkv,
    dma_sem,
    in_sem,
    ag_ls,
    ag_lr,
    ag_ps,
    ag_pr,
    ag_ss,
    ag_sr,
    rs_ss,
    rs_sr,
    rs_ps,
    rs_pr,
    rs_ls,
    rs_lr,
    cn_s,
    cn_r,
    cm_s,
    cm_r,
    vs_s,
    vs_r,
):
    rows, dim = x_h.shape
    images = rows // SEQ
    r = qm.shape[1]
    hw = qm.shape[2]
    width = wbm.shape[5]
    chunks = wbm.shape[0]
    chunk = 2 * width
    heads = dim // HEAD_DIM
    pairs = heads // 2
    t = lax.axis_index("tp")
    d = lax.axis_index("dp")
    l = d // np_
    p = d - l * np_
    o = 1 - t

    def at(ll, pp):
        return {"dp": ll * np_ + pp}

    def line_peer(k):
        return lax.rem(l + k, nl)

    def line_from(k):
        return lax.rem(l + nl - k, nl)

    def plane_peer(k):
        return lax.rem(p + k, np_)

    def plane_from(k):
        return lax.rem(p + np_ - k, np_)

    x_in = pltpu.make_async_copy(x_h, dqkv.at[0:rows, 0:dim], dma_sem.at[0])
    c_in = pltpu.make_async_copy(cot_h, dqkv.at[0:rows, dim : 2 * dim], dma_sem.at[1])
    small_in = [
        pltpu.make_async_copy(src, dst, in_sem.at[k])
        for k, (src, dst) in enumerate(
            ((qm_h, qm), (pm_h, pm), (am_h, am), (cm_h, cm), (bm_h, bm), (keep_h, keep_v), (nm_h, nm))
        )
    ]
    for cp in small_in:
        cp.start()
    x_in.start()
    c_in.start()

    barrier = pltpu.get_barrier_semaphore()
    for k in range(1, nl):
        pl.semaphore_signal(barrier, inc=1, device_id=at(line_peer(k), p), device_id_type=MESH)
    for k in range(1, np_):
        pl.semaphore_signal(barrier, inc=1, device_id=at(l, plane_peer(k)), device_id_type=MESH)
    pl.semaphore_signal(barrier, inc=1, device_id={"tp": o}, device_id_type=MESH)

    def w_buf(pc):
        return wba.at[pc] if pc < pairs else wbm.at[pc - pairs]

    def of(a_ref, m_ref, pc):
        return a_ref.at[pc] if pc < pairs else m_ref.at[pc - pairs]

    def stacked(pc, blocks):
        pk = pk_a if pc < pairs else pk_m
        have, need = r * len(blocks), pk.shape[0]
        if r % 8 == 0:
            pad = [jnp.zeros((need - have, pk.shape[1]), F32)] if need > have else []
            return jnp.concatenate(list(blocks) + pad, axis=0)
        if need > have:
            pk[...] = jnp.zeros_like(pk)
        for b, block in enumerate(blocks):
            pk[b * r : (b + 1) * r, :] = block
        return pk[...]

    for cp in small_in:
        cp.wait()
    for c in range(pairs):
        cols = slice(64 * c, 64 * c + 64)
        wba[c, t, p, l] = stacked(
            c,
            [
                jnp.concatenate([qm[0, :, cols], qm[1, :, cols]], axis=1),
                jnp.concatenate([qm[2, :, cols], pm[:, cols]], axis=1),
            ],
        ).astype(BF16)
    for j in range(chunks):
        cols = slice(j * width, (j + 1) * width)
        wbm[j, t, p, l] = stacked(pairs + j, [am[:, cols], cm[:, cols]]).astype(BF16)
    bias2[t] = jnp.broadcast_to(bm[...], bias2.shape[1:])
    full = keep_v.shape[0] // 128
    tail = keep_v.shape[0] - full * 128
    mkt[...] = jnp.zeros_like(mkt)
    mkt[0:full, :] = keep_v[pl.ds(0, full * 128)].reshape(full, 128).astype(F32)
    if tail:
        mkt[full : full + 1, 0:tail] = keep_v[pl.ds(full * 128, tail)].reshape(1, tail).astype(F32)
    count = jnp.sum(jnp.sum(mkt[...], axis=1, keepdims=True), axis=0, keepdims=True)
    cntl[l] = jnp.broadcast_to(count, cntl.shape[1:])

    pl.semaphore_wait(barrier, nl - 1 + np_ - 1 + 1)

    def remote(src, dst, ssem, rsem, device):
        return pltpu.make_async_remote_copy(
            src_ref=src, dst_ref=dst, send_sem=ssem, recv_sem=rsem, device_id=device, device_id_type=MESH
        )

    def got(dst, rsem):
        return remote(dst, dst, dma_sem.at[2], rsem, {"tp": o})

    sends = {pc: [] for pc in range(pairs + chunks)}

    def send(pc, src, dst, ssem, rsem, device):
        cp = remote(src, dst, ssem, rsem, device)
        cp.start()
        sends[pc].append(cp)

    def to_plane(pc, ll, kl):
        here = w_buf(pc).at[t, p, ll]
        for k in range(1, np_):
            send(pc, here, here, ag_ps.at[pc, kl, k], ag_pr.at[pc, kl, k], at(l, plane_peer(k)))

    def start_piece(pc):
        here = w_buf(pc).at[t, p, l]
        for k in range(1, nl):
            send(pc, here, here, ag_ls.at[pc, k], ag_lr.at[pc, k], at(line_peer(k), p))
        to_plane(pc, l, 0)

    def line_done(pc):
        for k in range(1, nl):
            ll = line_from(k)
            got(w_buf(pc).at[t, p, ll], ag_lr.at[pc, k]).wait_recv()
            to_plane(pc, ll, k)
        here = w_buf(pc).at[t, p]
        send(pc, here, here, ag_ss.at[pc, 0], ag_sr.at[pc, 0], {"tp": o})

    def plane_done(pc):
        for k in range(1, np_):
            pp = plane_from(k)
            for kl in range(nl):
                got(w_buf(pc).at[t, pp, line_from(kl) if kl else l], ag_pr.at[pc, kl, k]).wait_recv()
            here = w_buf(pc).at[t, pp]
            send(pc, here, here, ag_ss.at[pc, k], ag_sr.at[pc, k], {"tp": o})

    def sibling_done(pc):
        for k in range(np_):
            got(w_buf(pc).at[o, plane_from(k) if k else p], ag_sr.at[pc, k]).wait_recv()

    def assemble(pc):
        for tt in range(2):
            for ll in range(nl):
                for pp in range(np_):
                    slot = w_buf(pc)[tt, pp, ll].astype(F32)
                    row = (ll * np_ + pp) * r
                    for b, lane_at, cols, col in piece_parts(pc, tt, pairs, width):
                        grd[row : row + r, col : col + cols] = slot[b * r : (b + 1) * r, lane_at : lane_at + cols]
        if pc < pairs:
            w_qkv[:, 384 * pc : 384 * pc + 384] = grd[:, 0:384].astype(BF16)
            w_proj[:, 128 * pc : 128 * pc + 128] = grd[:, 384:512].astype(BF16)
        else:
            cols = slice((pc - pairs) * chunk, (pc - pairs + 1) * chunk)
            w_up[:, cols] = grd[:, 0:chunk].astype(BF16)
            w_down[:, cols] = grd[:, chunk : 2 * chunk].astype(BF16)

    start_piece(0)
    send(0, bias2.at[t], bias2.at[t], cm_s.at[0], cm_r.at[0], {"tp": o})
    for k in range(1, nl):
        send(0, cntl.at[l], cntl.at[l], cn_s.at[k], cn_r.at[k], at(line_peer(k), p))

    def cast_in(col):
        def step(c, carry):
            at_row = pl.ds(pl.multiple_of(c * 16, 16), 16)
            stage[at_row, :] = dqkv[at_row, col : col + dim].astype(F32)
            return carry

        lax.fori_loop(0, rows // 16, step, 0)

    stage[rows:, :] = jnp.zeros((stage.shape[0] - rows, dim), F32)
    mask_rows = mkt[...].astype(BF16)
    ones = jnp.ones((128, 128), BF16)
    row_id = lax.broadcasted_iota(jnp.int32, (PAD, 128), 0)
    lane_id = lax.broadcasted_iota(jnp.int32, (PAD, 128), 1)
    for i in range(images):
        token = row_id + (t * rows + i * SEQ)
        picked = dot_nn((lane_id == token // 128).astype(F32).astype(BF16), mask_rows)
        hit = (lane_id == token % 128) & (row_id < SEQ)
        mcol[i] = dot_nn(jnp.where(hit, picked, 0.0).astype(BF16), ones)
    inside = lax.broadcasted_iota(jnp.int32, (PAD, dim), 0) < SEQ
    x_in.wait()
    cast_in(0)
    gain1, shift1 = nm[0:1, :], nm[1:2, :]

    def norm_in(i):
        v = jnp.where(inside, stage[i * SEQ : i * SEQ + PAD, :], 0.0)
        xpad[i * PAD : (i + 1) * PAD, :] = v.astype(BF16)
        xhat, _ = norm_parts(v)
        n1[i * PAD : (i + 1) * PAD, :] = (xhat * gain1 + shift1).astype(BF16)

    def back_in(i):
        v = jnp.where(inside, stage[i * SEQ : i * SEQ + PAD, :], 0.0)
        m = mcol[i]
        back[i * PAD : (i + 1) * PAD, :] = (v * jnp.concatenate([m] * (dim // 128), axis=1)).astype(BF16)

    for i in range(images // 4):
        norm_in(i)
    line_done(0)
    start_piece(1)
    start_piece(2)
    for k in range(1, nl):
        got(cntl.at[line_from(k)], cn_r.at[k]).wait_recv()
    cntp[p] = functools.reduce(lambda a, b: a + b, [cntl[ll] for ll in range(nl)])
    for k in range(1, np_):
        send(0, cntp.at[p], cntp.at[p], cm_s.at[k], cm_r.at[k], at(l, plane_peer(k)))
    for i in range(images // 4, images):
        norm_in(i)
    line_done(1)
    plane_done(0)
    start_piece(3)
    c_in.wait()
    cast_in(dim)
    for i in range(images):
        back_in(i)
    sibling_done(0)
    got(bias2.at[o], cm_r.at[0]).wait_recv()
    assemble(0)

    def image_rows(i, many=1):
        return pl.ds(pl.multiple_of(i * (many * PAD), 16), many * PAD)

    def over_images(step, many=1, unroll=1):
        lax.fori_loop(0, images // many, lambda i, carry: step(i) or carry, 0, unroll=unroll)

    both = [bias2[0, 0:1, :], bias2[1, 0:1, :]]
    h_bias = [
        jnp.concatenate([b[:, 2 * hw + j * width : 2 * hw + (j + 1) * width] for b in both], axis=1)
        for j in range(chunks)
    ]

    def qkv_rows(c):
        cols = slice(384 * c, 384 * c + 384)
        q_bias = [b[:, 64 * c : 64 * c + 64] for b in both]
        v_bias = [b[:, hw + 64 * c : hw + 64 * c + 64] for b in both]
        bias = jnp.concatenate(q_bias + [jnp.zeros((1, 128), F32)] + v_bias, axis=1)

        def step(i):
            here = image_rows(i, G_QKV)
            qkv[here, cols] = (dot_nn(n1[here, :], w_qkv[:, cols]) + bias).astype(BF16)

        over_images(step, G_QKV)

    lane = lax.broadcasted_iota(jnp.int32, (1, 128), 1)
    head_mask = [(lane < HEAD_DIM).astype(F32).astype(BF16), (lane >= HEAD_DIM).astype(F32).astype(BF16)]
    head_scale = [(SCALE * mask.astype(F32)).astype(BF16) for mask in head_mask]

    def both_heads(v, scales):
        gap = jnp.zeros((WIDE - PAD, 128), BF16)
        return jnp.concatenate([v * scales[0], gap, v * scales[1], gap], axis=0)

    def of_heads(v):
        return v[:, 0:PAD], v[:, WIDE : WIDE + PAD]

    def pair_rows(ref, here, c, b):
        return ref[here, 384 * c + 128 * b : 384 * c + 128 * b + 128]

    def attend(c):
        def step(i):
            here = image_rows(i)
            qp, kp, vp = (pair_rows(qkv, here, c, b) for b in range(3))
            open_key = jnp.concatenate([mcol[i]] * (2 * WIDE // 128), axis=1) > 0.0
            s = jnp.where(open_key, dot_nt(kp, both_heads(qp, head_scale)), NEG)
            e = jnp.exp(s - jnp.max(s, axis=0, keepdims=True))
            pr = (e * (1.0 / jnp.sum(e, axis=0, keepdims=True))).astype(BF16)
            probs[i * pairs + c] = pr
            first, second = of_heads(pr)
            total = dot_tn(first, vp * head_mask[0]) + dot_tn(second, vp * head_mask[1])
            att[here, c * 128 : (c + 1) * 128] = total.astype(BF16)

        over_images(step, unroll=U_ATT)

    qkv_rows(0)
    line_done(2)
    plane_done(1)
    start_piece(4)
    attend(0)
    sibling_done(1)
    assemble(1)
    qkv_rows(1)
    line_done(3)
    plane_done(2)
    start_piece(5)
    attend(1)
    sibling_done(2)
    assemble(2)
    qkv_rows(2)
    line_done(4)
    attend(2)
    plane_done(3)
    line_done(5)
    for k in range(1, np_):
        got(cntp.at[plane_from(k)], cm_r.at[k]).wait_recv()
    kept = functools.reduce(lambda a, b: a + b, [cntp[pp] for pp in range(np_)])
    grad_scale = (rows * 2.0 * nl * np_) / kept[0:1, 0:1]

    vec[...] = jnp.zeros_like(vec)
    bias4, gain2, shift2, bias5 = nm[4:5, :], nm[2:3, :], nm[3:4, :], nm[5:6, :]

    def mid_step(i):
        here = image_rows(i, G_MID)
        m = xpad[here, :].astype(F32) + (dot_nt(att[here, :], w_proj[...]) + bias4)
        mid[here, :] = m
        xhat, _ = norm_parts(m)
        n2[here, :] = (xhat * gain2 + shift2).astype(BF16)

    over_images(mid_step, G_MID)
    plane_done(4)

    def pack(pc):
        for cp in sends[pc]:
            cp.wait_send()
        for tt in range(2):
            parts = piece_parts(pc, tt, pairs, width)
            for ll in range(nl):
                for pp in range(np_):
                    row = (ll * np_ + pp) * r
                    blocks = []
                    for b in range(parts[-1][0] + 1):
                        own = [grd[row : row + r, col : col + cols] for bb, _, cols, col in parts if bb == b]
                        blocks.append(jnp.concatenate(own, axis=1) if len(own) > 1 else own[0])
                    w_buf(pc)[tt, pp, ll] = stacked(pc, blocks).astype(BF16)

    late = []

    def send_late(src, dst, ssem, rsem, device):
        cp = remote(src, dst, ssem, rsem, device)
        cp.start()
        late.append(cp)

    def send_sibling(pc):
        send_late(w_buf(pc).at[o], of(sib_a, sib_m, pc), rs_ss.at[pc], rs_sr.at[pc], {"tp": o})

    def send_plane(pc):
        sib, rpl = of(sib_a, sib_m, pc), of(rpl_a, rpl_m, pc)
        got(sib, rs_sr.at[pc]).wait_recv()
        for pp in range(np_):
            for ll in range(nl):
                sib[pp, ll] = (sib[pp, ll].astype(F32) + w_buf(pc)[t, pp, ll].astype(F32)).astype(BF16)
        for k in range(1, np_):
            send_late(sib.at[plane_peer(k)], rpl.at[p], rs_ps.at[pc, k], rs_pr.at[pc, k], at(l, plane_peer(k)))
        rpl[p] = sib[p]

    def send_line(pc):
        rpl, lsn, rln = of(rpl_a, rpl_m, pc), of(lsn_a, lsn_m, pc), of(rln_a, rln_m, pc)
        for k in range(1, np_):
            got(rpl.at[plane_from(k)], rs_pr.at[pc, k]).wait_recv()
        for ll in range(nl):
            lsn[ll] = functools.reduce(
                lambda a, b: a + b, [rpl[pp, ll].astype(F32) for pp in range(np_)]
            ).astype(BF16)
        for k in range(1, nl):
            send_late(lsn.at[line_peer(k)], rln.at[l], rs_ls.at[pc, k], rs_lr.at[pc, k], at(line_peer(k), p))
        rln[l] = lsn[l]

    def sum_line(pc):
        rln, fin = of(rln_a, rln_m, pc), of(fin_a, fin_m, pc)
        for k in range(1, nl):
            got(rln.at[line_from(k)], rs_lr.at[pc, k]).wait_recv()
        fin[...] = functools.reduce(lambda a, b: a + b, [rln[ll].astype(F32) for ll in range(nl)])

    def ff_chunk(j):
        def step(i):
            here = image_rows(i, G_FF)
            b = back[here, :]
            cols = slice(j * chunk, (j + 1) * chunk)
            pre = dot_nn(n2[here, :], w_up[:, cols]) + h_bias[j]
            ga = dot_nn(b, w_down[:, cols])
            value, slope = gelu_parts(pre)
            act[here, cols] = value.astype(BF16)
            gpre = (ga * slope).astype(BF16)
            gp[here, cols] = gpre
            vec[8 + j : 9 + j, :] += jnp.sum(gpre.astype(F32), axis=0, keepdims=True)

        over_images(step, G_FF)

    def ff_grad(j):
        cols = slice(j * chunk, (j + 1) * chunk)
        grd[:, 0:chunk] = dot_tn(n2[...], gp[:, cols])
        grd[:, chunk : 2 * chunk] = dot_tn(back[...], act[:, cols])

    for j in range(chunks):
        sibling_done(pairs + j)
        assemble(pairs + j)
        ff_chunk(j)
        if j == 0:
            plane_done(5)
        if j > 1:
            send_line(pairs + j - 2)
        if j > 0:
            send_plane(pairs + j - 1)
        ff_grad(j)
        pack(pairs + j)
        send_sibling(pairs + j)

    def back_step(i):
        here = image_rows(i, G_BACK)
        m = mid[here, :]
        xhat, rstd = norm_parts(m)
        dn = dot_nt(gp[here, :], w_up[...])
        bfl = back[here, :].astype(F32)
        gm = bfl + norm_back(dn, xhat, rstd, gain2)
        gmid[here, :] = gm
        g16 = gm.astype(BF16)
        gbr[here, :] = g16
        gatt[here, :] = dot_nn(g16, w_proj[...]).astype(BF16)
        vec[2:3, 0:dim] += jnp.sum(dn * xhat, axis=0, keepdims=True)
        vec[3:4, 0:dim] += jnp.sum(dn, axis=0, keepdims=True)
        vec[4:5, 0:dim] += jnp.sum(g16.astype(F32), axis=0, keepdims=True)
        vec[5:6, 0:dim] += jnp.sum(bfl, axis=0, keepdims=True)

    over_images(back_step, G_BACK)

    def attend_back(c):
        cols = slice(c * 128, (c + 1) * 128)

        def start(i, into):
            here = image_rows(i)
            into[...] = dot_nt(pair_rows(qkv, here, c, 2), both_heads(gatt[here, cols], head_mask))

        def finish(i, dp_ref):
            here = image_rows(i)
            qp, kp = pair_rows(qkv, here, c, 0), pair_rows(qkv, here, c, 1)
            pr = probs[i * pairs + c]
            prf = pr.astype(F32)
            dp = dp_ref[...]
            inner = jnp.sum(prf * dp, axis=0, keepdims=True)
            ds = (prf * (dp - inner)).astype(BF16)
            dv = dot_nn(pr, both_heads(gatt[here, cols], head_mask)).astype(BF16)
            dk = dot_nn(ds, both_heads(qp, head_scale)).astype(BF16)
            first, second = of_heads(ds)
            dq = (dot_tn(first, kp * head_scale[0]) + dot_tn(second, kp * head_scale[1])).astype(BF16)
            dqkv[here, 384 * c : 384 * c + 128] = dq
            dqkv[here, 384 * c + 128 : 384 * c + 256] = dk
            dqkv[here, 384 * c + 256 : 384 * c + 384] = dv
            vec[6:7, cols] += jnp.sum(dq.astype(F32), axis=0, keepdims=True)
            vec[7:8, cols] += jnp.sum(dv.astype(F32), axis=0, keepdims=True)

        start(0, even)

        def step(k):
            start(2 * k + 1, odd)
            finish(2 * k, even)
            start(jnp.minimum(2 * k + 2, images - 1), even)
            finish(2 * k + 1, odd)

        over_images(step, 2, unroll=U_ATB)

    def qkv_grad(c):
        grd[:, 0:384] = dot_tn(n1[...], dqkv[:, 384 * c : 384 * c + 384])
        grd[:, 384:512] = dot_tn(gbr[...], att[:, 128 * c : 128 * c + 128])
        pack(c)
        send_sibling(c)

    send_plane(5)
    attend_back(0)
    send_line(4)
    qkv_grad(0)
    attend_back(1)
    send_plane(0)
    send_line(5)
    qkv_grad(1)
    attend_back(2)
    send_plane(1)
    qkv_grad(2)
    send_line(0)

    def last_step(i):
        here = image_rows(i, G_LAST)
        dn = dot_nt(dqkv[here, :], w_qkv[...])
        xhat, rstd = norm_parts(xpad[here, :].astype(F32))
        gmid[here, :] = (gmid[here, :] + norm_back(dn, xhat, rstd, gain1)) * grad_scale
        vec[0:1, 0:dim] += jnp.sum(dn * xhat, axis=0, keepdims=True)
        vec[1:2, 0:dim] += jnp.sum(dn, axis=0, keepdims=True)

    first_part = images // G_LAST // 2
    lax.fori_loop(0, first_part, lambda i, carry: last_step(i) or carry, 0)
    send_plane(2)
    lax.fori_loop(first_part, images // G_LAST, lambda i, carry: last_step(i) or carry, 0)
    send_late(vec, vsib, vs_s.at[0], vs_r.at[0], {"tp": o})

    for i in range(images):
        stage[i * SEQ : (i + 1) * SEQ, :] = gmid[i * PAD : i * PAD + SEQ, :]
    gin_cp = pltpu.make_async_copy(stage.at[0:rows, :], gin_h, dma_sem.at[1])
    gin_cp.start()
    got(vsib, vs_r.at[0]).wait_recv()
    vpl[p] = vec[...] + vsib[...]
    for k in range(1, np_):
        send_late(vpl.at[p], vpl.at[p], vs_s.at[k], vs_r.at[k], at(l, plane_peer(k)))
    send_line(1)

    def out_step(i):
        here = image_rows(i, G_OUT)
        mid[here, :] = mid[here, :] + (dot_nt(act[here, :], w_down[...]) + bias5)

    over_images(out_step, G_OUT)
    send_line(2)
    for k in range(1, np_):
        got(vpl.at[plane_from(k)], vs_r.at[k]).wait_recv()
    vln[l] = functools.reduce(lambda a, b: a + b, [vpl[pp] for pp in range(np_)])
    for k in range(1, nl):
        send_late(vln.at[l], vln.at[l], vs_s.at[np_ + k], vs_r.at[np_ + k], at(line_peer(k), p))
    for i in range(images):
        gmid[i * SEQ : (i + 1) * SEQ, :] = mid[i * PAD : i * PAD + SEQ, :]

    def cast_out(c, carry):
        at_row = pl.ds(pl.multiple_of(c * 16, 16), 16)
        n2[at_row, :] = gmid[at_row, :].astype(BF16)
        return carry

    lax.fori_loop(0, rows // 16, cast_out, 0)
    out_cp = pltpu.make_async_copy(n2.at[0:rows, :], out_h, dma_sem.at[0])
    out_cp.start()
    kept_o[...] = kept
    for pc in list(range(pairs, pairs + chunks)) + list(range(pairs)):
        sum_line(pc)
    for k in range(1, nl):
        got(vln.at[line_from(k)], vs_r.at[np_ + k]).wait_recv()
    vec_o[...] = functools.reduce(lambda a, b: a + b, [vln[ll] for ll in range(nl)])
    out_cp.wait()
    gin_cp.wait()
    for cp in late:
        cp.wait_send()


def update_kernel(scale_rows, *refs):
    ins, outs, kept_vm = refs[:24], refs[24:48], refs[48:]
    out_in, gin_in = ins[4:6]
    out_h, gin_h = outs[:2]
    small_in = ins[:4] + ins[6:]
    in_v, out_v = kept_vm[:22], list(kept_vm[22:40])
    big_out, big_gin, sems_in, sems_out, sems_a, sems_b = kept_vm[40:]
    copies = (3, 7, 11, 15)
    for k in copies:
        out_v.insert(k, outs[2 + k])
    parts = 3
    size = out_in.shape[0] // parts
    loads, stores = [], []
    for k in range(parts):
        here = pl.ds(k * size, size)
        for j, (src, via, dst) in enumerate(((out_in, big_out, out_h), (gin_in, big_gin, gin_h))):
            loads.append(pltpu.make_async_copy(src.at[here, :], via.at[here, :], sems_in.at[j, k]))
            stores.append(pltpu.make_async_copy(via.at[here, :], dst.at[here, :], sems_out.at[j, k]))
    small = [pltpu.make_async_copy(src, dst, sems_a.at[k]) for k, (src, dst) in enumerate(zip(small_in, in_v))]
    for cp in small + loads:
        cp.start()
    for cp in small:
        cp.wait()
    fin_a, fin_m, vec, kept = in_v[:4]
    states = [in_v[4 + 3 * k : 7 + 3 * k] for k in range(6)]
    results = [pltpu.make_async_copy(src, dst, sems_b.at[k]) for k, (src, dst) in enumerate(zip(out_v, outs[2:])) if k not in copies]
    q_o, p_o, a_o, c_o = (out_v[4 * k : 4 * k + 4] for k in range(4))
    n_o, b_o = out_v[16:19], out_v[19:22]
    qkv, proj, fc1, fc2, norm, bias = states
    r, hw = proj[0].shape
    chunks, _, width = fin_m.shape
    own = lax.axis_index("tp") == 0
    grad_scale = scale_rows / kept[0:1, 0:1]

    def update(grad, state, outs, rate, decay, c=None):
        pick = (lambda ref: ref[...]) if c is None else (lambda ref: ref[c])
        master, first, second = (pick(ref) for ref in state)
        first, second, master = adam(master, first, second, grad * grad_scale, rate, decay)
        for ref, value in zip(outs, (first, second, master, master)):
            if c is None:
                ref[...] = value.astype(ref.dtype)
            else:
                ref[c] = value.astype(ref.dtype)

    pairs = fin_a.shape[0]

    def over_pairs(block, lane_at):
        return jnp.concatenate(
            [fin_a[c, block * r : (block + 1) * r, lane_at : lane_at + 64] for c in range(pairs)], axis=1
        )

    update(over_pairs(0, 0), qkv, q_o, 0.08, matrix_decay, 0)
    update(over_pairs(0, 64), qkv, q_o, 0.08, matrix_decay, 1)
    update(over_pairs(1, 0), qkv, q_o, 0.08, matrix_decay, 2)
    update(over_pairs(1, 64), proj, p_o, 0.8, matrix_decay)
    update(jnp.concatenate([fin_m[j, 0:r, :] for j in range(chunks)], axis=1), fc1, a_o, 0.08, matrix_decay)
    update(jnp.concatenate([fin_m[j, r : 2 * r, :] for j in range(chunks)], axis=1), fc2, c_o, 0.04, matrix_decay)
    update(vec[0:6, 0 : norm[0].shape[1]], norm, n_o, 0.5, 0.0)

    def pick(row, col, cols):
        return jnp.where(
            own, vec[row : row + 1, col : col + cols], vec[row : row + 1, col + cols : col + 2 * cols]
        )

    bias_parts = [pick(row, 128 * c, 64) for row in (6, 7) for c in range(pairs)]
    bias_parts += [pick(8 + j, 0, width) for j in range(chunks)]
    update(jnp.concatenate(bias_parts, axis=1), bias, b_o, 0.5, 0.0)
    for cp in results:
        cp.start()
    for load, store in zip(loads, stores):
        load.wait()
        store.start()
    for cp in results + stores:
        cp.wait()


def body(
    inputs, keep_mask, cotangent,
    qkv_master, qkv_first, qkv_second,
    proj_master, proj_first, proj_second,
    fc1_master, fc1_first, fc1_second,
    fc2_master, fc2_first, fc2_second,
    norm_master, norm_first, norm_second,
    bias_master, bias_first, bias_second,
):
    n = lax.axis_size("dp")
    nl = 4 if n % 4 == 0 else n
    np_ = n // nl
    rows, dim = inputs.shape
    images = rows // SEQ
    padded = images * PAD
    r = qkv_master.shape[1]
    hw = qkv_master.shape[2]
    fw = fc1_master.shape[1]
    width = 256
    chunks = fw // width
    chunk = 2 * width
    slot_a = -(-2 * r // 16) * 16
    pairs = dim // HEAD_DIM // 2
    slot_m = -(-2 * r // 16) * 16
    vm = pl.BlockSpec(memory_space=pltpu.VMEM)
    hbm = pl.BlockSpec(memory_space=pl.ANY)

    def like(a, dtype=None):
        return jax.ShapeDtypeStruct(a.shape, dtype or a.dtype)

    proj_master, proj_first, proj_second = proj_master.T, proj_first.T, proj_second.T
    fc2_master, fc2_first, fc2_second = fc2_master.T, fc2_first.T, fc2_second.T
    large = [like(inputs), like(inputs, F32)]
    sums = [
        jax.ShapeDtypeStruct((pairs, slot_a, 128), F32),
        jax.ShapeDtypeStruct((chunks, slot_m, width), F32),
        jax.ShapeDtypeStruct((16, chunk), F32),
        jax.ShapeDtypeStruct((8, 128), F32),
    ]
    dma = pltpu.SemaphoreType.DMA
    pieces = pairs + chunks
    small = (keep_mask, qkv_master, proj_master, fc1_master, fc2_master, norm_master, bias_master)
    scratch = [pltpu.VMEM(a.shape, a.dtype) for a in small] + [
        pltpu.VMEM((pairs, 2, np_, nl, slot_a, 128), BF16),
        pltpu.VMEM((chunks, 2, np_, nl, slot_m, width), BF16),
        pltpu.VMEM((dim, 3 * dim), BF16),
        pltpu.VMEM((dim, dim), BF16),
        pltpu.VMEM((dim, chunks * chunk), BF16),
        pltpu.VMEM((dim, chunks * chunk), BF16),
        pltpu.VMEM((dim, 2 * chunk), F32),
        pltpu.VMEM((pairs, np_, nl, slot_a, 128), BF16),
        pltpu.VMEM((chunks, np_, nl, slot_m, width), BF16),
        pltpu.VMEM((pairs, np_, nl, slot_a, 128), BF16),
        pltpu.VMEM((chunks, np_, nl, slot_m, width), BF16),
        pltpu.VMEM((pairs, nl, slot_a, 128), BF16),
        pltpu.VMEM((chunks, nl, slot_m, width), BF16),
        pltpu.VMEM((pairs, nl, slot_a, 128), BF16),
        pltpu.VMEM((chunks, nl, slot_m, width), BF16),
        pltpu.VMEM((slot_a, 128), F32),
        pltpu.VMEM((slot_m, width), F32),
        pltpu.VMEM((2, 8, bias_master.shape[1]), F32),
        pltpu.VMEM((nl, 8, 128), F32),
        pltpu.VMEM((np_, 8, 128), F32),
        pltpu.VMEM((16, chunk), F32),
        pltpu.VMEM((16, chunk), F32),
        pltpu.VMEM((np_, 16, chunk), F32),
        pltpu.VMEM((nl, 16, chunk), F32),
        pltpu.VMEM((-(-(rows - SEQ + PAD) // 16) * 16, dim), F32),
        pltpu.VMEM((padded, dim), F32),
        pltpu.VMEM((padded, dim), F32),
        pltpu.VMEM((images * pairs, PAD, 2 * WIDE), BF16),
        pltpu.VMEM((PAD, 2 * WIDE), F32),
        pltpu.VMEM((PAD, 2 * WIDE), F32),
        pltpu.VMEM((images, PAD, 128), F32),
        pltpu.VMEM((128, 128), F32),
        pltpu.VMEM((padded, dim), BF16),
        pltpu.VMEM((padded, dim), BF16),
        pltpu.VMEM((padded, dim), BF16),
        pltpu.VMEM((padded, 3 * dim), BF16),
        pltpu.VMEM((padded, dim), BF16),
        pltpu.VMEM((padded, dim), BF16),
        pltpu.VMEM((padded, dim), BF16),
        pltpu.VMEM((padded, dim), BF16),
        pltpu.VMEM((padded, chunks * chunk), BF16),
        pltpu.VMEM((padded, chunks * chunk), BF16),
        pltpu.VMEM((padded, 3 * dim), BF16),
        dma((3,)),
        dma((7,)),
        dma((pieces, nl)),
        dma((pieces, nl)),
        dma((pieces, nl, np_)),
        dma((pieces, nl, np_)),
        dma((pieces, np_)),
        dma((pieces, np_)),
        dma((pieces,)),
        dma((pieces,)),
        dma((pieces, np_)),
        dma((pieces, np_)),
        dma((pieces, nl)),
        dma((pieces, nl)),
        dma((nl,)),
        dma((nl,)),
        dma((np_,)),
        dma((np_,)),
        dma((np_ + nl,)),
        dma((np_ + nl,)),
    ]
    out, gin, fin_a, fin_m, vec, kept = pl.pallas_call(
        functools.partial(kernel, nl, np_),
        out_shape=large + sums,
        in_specs=[hbm] * 9,
        out_specs=[hbm, hbm] + [vm] * 4,
        scratch_shapes=scratch,
        compiler_params=pltpu.CompilerParams(
            collective_id=0, has_side_effects=True, vmem_limit_bytes=64 * 1024 * 1024
        ),
    )(inputs, keep_mask, cotangent, qkv_master, proj_master, fc1_master, fc2_master, norm_master, bias_master)
    states = [
        qkv_master, qkv_first, qkv_second,
        proj_master, proj_first, proj_second,
        fc1_master, fc1_first, fc1_second,
        fc2_master, fc2_first, fc2_second,
        norm_master, norm_first, norm_second,
        bias_master, bias_first, bias_second,
    ]
    outs = list(large)
    for a in (qkv_master, proj_master, fc1_master, fc2_master):
        outs += [like(a), like(a), like(a), like(a, BF16)]
    for a in (norm_master, bias_master):
        outs += [like(a)] * 3
    res = list(
        pl.pallas_call(
            functools.partial(update_kernel, rows * 2.0 * n),
            out_shape=outs,
            in_specs=[hbm] * 24,
            out_specs=[vm if a.dtype == BF16 and k > 0 else hbm for k, a in enumerate(outs)],
            scratch_shapes=[pltpu.VMEM(a.shape, a.dtype) for a in sums + states + [a for a in outs[2:] if a.dtype == F32]]
            + [pltpu.VMEM((rows, dim), BF16), pltpu.VMEM((rows, dim), F32)]
            + [dma((2, 3)), dma((2, 3)), dma((22,)), dma((22,))],
            compiler_params=pltpu.CompilerParams(vmem_limit_bytes=64 * 1024 * 1024),
        )(fin_a, fin_m, vec, kept, out, gin, *states)
    )
    for k in (6, 7, 8, 9, 14, 15, 16, 17):
        res[k] = res[k].T
    return tuple(res)


def solution(mesh):
    mats = [P(None, "dp", "tp"), P("tp", "dp"), P("dp", "tp"), P("tp", "dp")]
    in_specs = [P(("dp", "tp"), None), P("dp"), P(("dp", "tp"), None)]
    out_specs = [P(("dp", "tp"), None), P(("dp", "tp"), None)]
    for m in mats:
        in_specs += [m] * 3
        out_specs += [m] * 4
    in_specs += [P()] * 3 + [P("tp", None)] * 3
    out_specs += [P()] * 3 + [P("tp", None)] * 3
    return jax.shard_map(
        body, mesh=mesh, in_specs=tuple(in_specs), out_specs=tuple(out_specs), check_vma=False
    )
```

```python
import functools

import jax
import jax.numpy as jnp
from jax import lax
from jax.experimental import pallas as pl
from jax.experimental.pallas import tpu as pltpu
from jax.sharding import PartitionSpec as P

HEAD_DIM = 64
PATCHES = 196
STEP = 5

norm_eps = 1e-06
beta_one = 0.9
beta_two = 0.999
adam_eps = 1e-08
matrix_decay = 0.05

F32 = jnp.float32
BF16 = jnp.bfloat16
MESH = pl.DeviceIdType.MESH
SEQ = PATCHES + 2
PAD = 208
WIDE = 256
NEG = -1000000000.0
SCALE = HEAD_DIM**-0.5
G_QKV, G_MID, G_FF, G_BACK, G_LAST, G_OUT = 8, 4, 8, 4, 4, 4
U_ATT, U_ATB = 8, 4


def dot_nn(a, b):
    return lax.dot_general(a, b, (((1,), (0,)), ((), ())), preferred_element_type=F32)


def dot_nt(a, b):
    return lax.dot_general(a, b, (((1,), (1,)), ((), ())), preferred_element_type=F32)


def dot_tn(a, b):
    return lax.dot_general(a, b, (((0,), (0,)), ((), ())), preferred_element_type=F32)


def norm_parts(v):
    mean = jnp.mean(v, axis=-1, keepdims=True)
    centred = v - mean
    var = jnp.mean(centred * centred, axis=-1, keepdims=True)
    rstd = lax.rsqrt(var + norm_eps)
    return centred * rstd, rstd


def norm_back(grad, xhat, rstd, gain):
    u = grad * gain
    return (
        u
        - jnp.mean(u, axis=-1, keepdims=True)
        - xhat * jnp.mean(u * xhat, axis=-1, keepdims=True)
    ) * rstd


def gelu_parts(u):
    cdf = 0.5 + 0.5 * lax.erf(0.7071067811865476 * u)
    return u * cdf, cdf + u * (0.3989422804014327 * jnp.exp(-0.5 * u * u))


def adam(master, first, second, grad, rate, decay):
    first = beta_one * first + (1.0 - beta_one) * grad
    second = beta_two * second + (1.0 - beta_two) * grad * grad
    first_hat = first / (1.0 - beta_one**STEP)
    second_hat = second / (1.0 - beta_two**STEP)
    master = master - rate * (first_hat / (jnp.sqrt(second_hat) + adam_eps) + decay * master)
    return first, second, master


def piece_parts(kind, tt, width):
    if kind == "a":
        return [(b // 2, 64 * (b % 2), 64, 128 * b + 64 * tt) for b in range(4)]
    return [(0, 0, width, width * tt), (1, 0, width, 2 * width + width * tt)]


def kernel(
    nl,
    np_,
    x_h,
    keep_h,
    cot_h,
    qm_h,
    pm_h,
    am_h,
    cm_h,
    nm_h,
    bm_h,
    out_h,
    gin_h,
    fin_a,
    fin_m,
    vec_o,
    kept_o,
    keep_v,
    qm,
    pm,
    am,
    cm,
    nm,
    bm,
    wba,
    wbm,
    w_qkv,
    w_proj,
    w_up,
    w_down,
    grd,
    sib_a,
    sib_m,
    rpl_a,
    rpl_m,
    lsn_a,
    lsn_m,
    rln_a,
    rln_m,
    pk_a,
    pk_m,
    bias2,
    cntl,
    cntp,
    biases,
    hid,
    vec,
    vsib,
    vpl,
    vln,
    stage,
    mid,
    gmid,
    probs,
    even,
    odd,
    mcol,
    mkt,
    xpad,
    back,
    n1,
    qkv,
    att,
    n2,
    gbr,
    gatt,
    act,
    gp,
    dqkv,
    dma_sem,
    in_sem,
    ag_s,
    ag_lr,
    ag_pr,
    ag_cr,
    rs_ss,
    rs_sr,
    rs_ps,
    rs_pr,
    rs_ls,
    rs_lr,
    cn_s,
    cn_r,
    cm_s,
    cm_r,
    vs_s,
    vs_r,
):
    rows, dim = x_h.shape
    images = rows // SEQ
    r = qm.shape[1]
    hw = qm.shape[2]
    width = wbm.shape[3]
    chunks = wbm.shape[0]
    chunk = 2 * width
    heads = dim // HEAD_DIM
    pairs = heads // 2
    t = lax.axis_index("tp")
    d = lax.axis_index("dp")
    l = d // np_
    p = d - l * np_
    o = 1 - t

    line_peer = [lax.rem(l + k, nl) for k in range(nl)]
    line_from = [lax.rem(l + nl - k, nl) for k in range(nl)]
    plane_peer = [lax.rem(p + k, np_) for k in range(np_)]
    plane_from = [lax.rem(p + np_ - k, np_) for k in range(np_)]
    line_dev = [{"dp": ll * np_ + p} for ll in line_peer]
    plane_dev = [{"dp": l * np_ + pp} for pp in plane_peer]
    other_core = {"tp": o}
    block = nl * np_

    def slot_at(tt, pp, ll):
        return tt * block + pp * nl + ll

    own_slot = slot_at(t, p, l)

    x_in = pltpu.make_async_copy(x_h, dqkv.at[0:rows, 0:dim], dma_sem.at[0])
    c_in = pltpu.make_async_copy(cot_h, dqkv.at[0:rows, dim : 2 * dim], dma_sem.at[1])
    small_in = [
        pltpu.make_async_copy(src, dst, in_sem.at[k])
        for k, (src, dst) in enumerate(
            ((qm_h, qm), (pm_h, pm), (am_h, am), (cm_h, cm), (bm_h, bm), (keep_h, keep_v), (nm_h, nm))
        )
    ]
    for cp in small_in:
        cp.start()
    x_in.start()
    c_in.start()

    barrier = pltpu.get_barrier_semaphore()
    for k in range(1, nl):
        pl.semaphore_signal(barrier, inc=1, device_id=line_dev[k], device_id_type=MESH)
    for k in range(1, np_):
        pl.semaphore_signal(barrier, inc=1, device_id=plane_dev[k], device_id_type=MESH)
    pl.semaphore_signal(barrier, inc=1, device_id=other_core, device_id_type=MESH)

    def kind_of(pc):
        return ("a", pc) if pc < pairs else ("m", pc - pairs)

    def of(piece, a_ref, m_ref):
        kind, at = piece
        return a_ref.at[at] if kind == "a" else m_ref.at[at]

    def w_buf(piece):
        return of(piece, wba, wbm)

    def sem_of(piece):
        kind, at = piece
        return at if kind == "a" else pairs + at

    def stacked(kind, blocks):
        pk = pk_a if kind == "a" else pk_m
        have, need = r * len(blocks), pk.shape[0]
        if r % 8 == 0:
            pad = [jnp.zeros((need - have, pk.shape[1]), F32)] if need > have else []
            return jnp.concatenate(list(blocks) + pad, axis=0)
        if need > have:
            pk[...] = jnp.zeros_like(pk)
        for b, block in enumerate(blocks):
            pk[b * r : (b + 1) * r, :] = block
        return pk[...]

    for cp in small_in:
        cp.wait()
    for c in range(pairs):
        cols = slice(64 * c, 64 * c + 64)
        wba[c, own_slot] = stacked(
            "a",
            [
                jnp.concatenate([qm[0, :, cols], qm[1, :, cols]], axis=1),
                jnp.concatenate([qm[2, :, cols], pm[:, cols]], axis=1),
            ],
        ).astype(BF16)
    for j in range(chunks):
        cols = slice(j * width, (j + 1) * width)
        wbm[j, own_slot] = stacked("m", [am[:, cols], cm[:, cols]]).astype(BF16)
    bias2[t] = jnp.broadcast_to(bm[...], bias2.shape[1:])
    full = keep_v.shape[0] // 128
    tail = keep_v.shape[0] - full * 128
    mkt[...] = jnp.zeros_like(mkt)
    mkt[0:full, :] = keep_v[pl.ds(0, full * 128)].reshape(full, 128).astype(F32)
    if tail:
        mkt[full : full + 1, 0:tail] = keep_v[pl.ds(full * 128, tail)].reshape(1, tail).astype(F32)
    count = jnp.sum(jnp.sum(mkt[...], axis=1, keepdims=True), axis=0, keepdims=True)
    cntl[l] = jnp.broadcast_to(count, cntl.shape[1:])

    pl.semaphore_wait(barrier, nl - 1 + np_ - 1 + 1)

    def remote(src, dst, ssem, rsem, device):
        return pltpu.make_async_remote_copy(
            src_ref=src, dst_ref=dst, send_sem=ssem, recv_sem=rsem, device_id=device, device_id_type=MESH
        )

    def got(dst, rsem):
        return remote(dst, dst, dma_sem.at[2], rsem, other_core)

    sends = []

    def send(src, dst, ssem, rsem, device):
        cp = remote(src, dst, ssem, rsem, device)
        cp.start()
        sends.append(cp)

    def line_copy(piece, k):
        pc, here = sem_of(piece), w_buf(piece).at[own_slot]
        return remote(here, here, ag_s.at[pc], ag_lr.at[pc, k - 1], line_dev[k])

    def plane_copy(piece, kl, k):
        pc, here = sem_of(piece), w_buf(piece).at[slot_at(t, p, line_from[kl])]
        return remote(here, here, ag_s.at[pc], ag_pr.at[pc, k - 1], plane_dev[k])

    def core_copy(piece, k):
        pc, here = sem_of(piece), w_buf(piece).at[pl.ds(slot_at(t, plane_from[k], 0), nl)]
        return remote(here, here, ag_s.at[pc], ag_cr.at[pc], other_core)

    def own_to_plane(piece):
        for k in range(1, np_):
            plane_copy(piece, 0, k).start()

    def start_piece(pc):
        piece = kind_of(pc)
        for k in range(1, nl):
            line_copy(piece, k).start()
        if piece[0] == "a":
            own_to_plane(piece)

    def line_done(pc):
        piece = kind_of(pc)
        if piece[0] == "m":
            own_to_plane(piece)
        for k in range(1, nl):
            got(w_buf(piece).at[slot_at(t, p, line_from[k])], ag_lr.at[pc, k - 1]).wait_recv()
            for kp in range(1, np_):
                plane_copy(piece, k, kp).start()
        core_copy(piece, 0).start()

    def plane_done(pc):
        piece = kind_of(pc)
        for k in range(1, np_):
            got(w_buf(piece).at[pl.ds(slot_at(t, plane_from[k], 0), nl)], ag_pr.at[pc, k - 1]).wait_recv()
            core_copy(piece, k).start()

    def core_done(piece):
        got(w_buf(piece).at[pl.ds(o * block, block)], ag_cr.at[sem_of(piece)]).wait_recv()

    def gather_sent(piece):
        sent = w_buf(piece).at[pl.ds(0, 2 * block - 1)]
        remote(sent, sent, ag_s.at[sem_of(piece)], dma_sem.at[2], other_core).wait_send()

    def lanes(at, size):
        return pl.ds(pl.multiple_of(at * size, 128), size)

    def assemble(piece):
        kind, where = piece
        for tt in range(2):
            for ll in range(nl):
                for pp in range(np_):
                    slot = w_buf(piece)[slot_at(tt, pp, ll)].astype(F32)
                    row = (ll * np_ + pp) * r
                    for b, lane_at, cols, col in piece_parts(kind, tt, width):
                        grd[row : row + r, col : col + cols] = slot[b * r : (b + 1) * r, lane_at : lane_at + cols]
        if kind == "a":
            w_qkv[:, lanes(where, 384)] = grd[:, 0:384].astype(BF16)
            w_proj[:, lanes(where, 128)] = grd[:, 384:512].astype(BF16)
        else:
            w_up[:, lanes(where, chunk)] = grd[:, 0:chunk].astype(BF16)
            w_down[:, lanes(where, chunk)] = grd[:, chunk : 2 * chunk].astype(BF16)

    start_piece(0)
    send(bias2.at[t], bias2.at[t], cm_s.at[0], cm_r.at[0], other_core)
    for k in range(1, nl):
        send(cntl.at[l], cntl.at[l], cn_s.at[k], cn_r.at[k], line_dev[k])

    def cast_in(col):
        def step(c, carry):
            at_row = pl.ds(pl.multiple_of(c * 16, 16), 16)
            stage[at_row, :] = dqkv[at_row, col : col + dim].astype(F32)
            return carry

        lax.fori_loop(0, rows // 16, step, 0)

    stage[rows:, :] = jnp.zeros((stage.shape[0] - rows, dim), F32)
    mask_rows = mkt[...].astype(BF16)
    ones = jnp.ones((128, 128), BF16)
    row_id = lax.broadcasted_iota(jnp.int32, (PAD, 128), 0)
    lane_id = lax.broadcasted_iota(jnp.int32, (PAD, 128), 1)
    for i in range(images):
        token = row_id + (t * rows + i * SEQ)
        picked = dot_nn((lane_id == token // 128).astype(F32).astype(BF16), mask_rows)
        hit = (lane_id == token % 128) & (row_id < SEQ)
        mcol[i] = dot_nn(jnp.where(hit, picked, 0.0).astype(BF16), ones)
    inside = lax.broadcasted_iota(jnp.int32, (PAD, dim), 0) < SEQ
    x_in.wait()
    cast_in(0)
    gain1, shift1 = nm[0:1, :], nm[1:2, :]

    def norm_in(i):
        v = jnp.where(inside, stage[i * SEQ : i * SEQ + PAD, :], 0.0)
        xpad[i * PAD : (i + 1) * PAD, :] = v.astype(BF16)
        xhat, _ = norm_parts(v)
        n1[i * PAD : (i + 1) * PAD, :] = (xhat * gain1 + shift1).astype(BF16)

    def back_in(i):
        v = jnp.where(inside, stage[i * SEQ : i * SEQ + PAD, :], 0.0)
        m = mcol[i]
        back[i * PAD : (i + 1) * PAD, :] = (v * jnp.concatenate([m] * (dim // 128), axis=1)).astype(BF16)

    for i in range(images // 4):
        norm_in(i)
    line_done(0)
    start_piece(1)
    start_piece(2)
    start_piece(3)
    for k in range(1, nl):
        got(cntl.at[line_from[k]], cn_r.at[k]).wait_recv()
    cntp[p] = functools.reduce(lambda a, b: a + b, [cntl[ll] for ll in range(nl)])
    for k in range(1, np_):
        send(cntp.at[p], cntp.at[p], cm_s.at[k], cm_r.at[k], plane_dev[k])
    for i in range(images // 4, images):
        norm_in(i)
    line_done(1)
    plane_done(0)
    c_in.wait()
    cast_in(dim)
    for i in range(images):
        back_in(i)
    core_done(kind_of(0))
    got(bias2.at[o], cm_r.at[0]).wait_recv()
    assemble(kind_of(0))

    def image_rows(i, many=1):
        return pl.ds(pl.multiple_of(i * (many * PAD), 16), many * PAD)

    def over_images(step, many=1, unroll=1):
        lax.fori_loop(0, images // many, lambda i, carry: step(i) or carry, 0, unroll=unroll)

    both = [bias2[0, 0:1, :], bias2[1, 0:1, :]]
    for j in range(chunks):
        parts = [b[:, 2 * hw + j * width : 2 * hw + (j + 1) * width] for b in both]
        biases[1:2, j * chunk : (j + 1) * chunk] = jnp.concatenate(parts, axis=1)
    for c in range(pairs):
        parts = [b[:, 64 * c : 64 * c + 64] for b in both] + [jnp.zeros((1, 128), F32)]
        parts += [b[:, hw + 64 * c : hw + 64 * c + 64] for b in both]
        biases[0:1, 384 * c : 384 * c + 384] = jnp.concatenate(parts, axis=1)

    def qkv_rows(c):
        cols = lanes(c, 384)

        def step(i):
            here = image_rows(i, G_QKV)
            qkv[here, cols] = (dot_nn(n1[here, :], w_qkv[:, cols]) + biases[0:1, cols]).astype(BF16)

        over_images(step, G_QKV)

    lane = lax.broadcasted_iota(jnp.int32, (1, 128), 1)
    head_mask = [(lane < HEAD_DIM).astype(F32).astype(BF16), (lane >= HEAD_DIM).astype(F32).astype(BF16)]
    head_scale = [(SCALE * mask.astype(F32)).astype(BF16) for mask in head_mask]

    def both_heads(v, scales):
        gap = jnp.zeros((WIDE - PAD, 128), BF16)
        return jnp.concatenate([v * scales[0], gap, v * scales[1], gap], axis=0)

    def of_heads(v):
        return v[:, 0:PAD], v[:, WIDE : WIDE + PAD]

    def pair_rows(ref, here, c, b):
        return ref[here, lanes(3 * c + b, 128)]

    def attend(c):
        def step(i):
            here = image_rows(i)
            qp, kp, vp = (pair_rows(qkv, here, c, b) for b in range(3))
            open_key = jnp.concatenate([mcol[i]] * (2 * WIDE // 128), axis=1) > 0.0
            s = jnp.where(open_key, dot_nt(kp, both_heads(qp, head_scale)), NEG)
            e = jnp.exp(s - jnp.max(s, axis=0, keepdims=True))
            pr = (e * (1.0 / jnp.sum(e, axis=0, keepdims=True))).astype(BF16)
            probs[i * pairs + c] = pr
            first, second = of_heads(pr)
            total = dot_tn(first, vp * head_mask[0]) + dot_tn(second, vp * head_mask[1])
            att[here, lanes(c, 128)] = total.astype(BF16)

        over_images(step, unroll=U_ATT)

    def pair_forward(c, carry):
        qkv_rows(c)

        @pl.when(c == 0)
        def _():
            line_done(2)
            line_done(3)
            plane_done(1)
            start_piece(4)

        @pl.when(c == 1)
        def _():
            plane_done(2)
            start_piece(5)

        @pl.when(c == 2)
        def _():
            line_done(4)

        attend(c)

        @pl.when(c < pairs - 1)
        def _():
            core_done(("a", c + 1))
            assemble(("a", c + 1))

        return carry

    lax.fori_loop(0, pairs, pair_forward, 0)
    plane_done(3)
    line_done(5)
    for k in range(1, np_):
        got(cntp.at[plane_from[k]], cm_r.at[k]).wait_recv()
    kept = functools.reduce(lambda a, b: a + b, [cntp[pp] for pp in range(np_)])
    grad_scale = (rows * 2.0 * nl * np_) / kept[0:1, 0:1]

    vec[...] = jnp.zeros_like(vec)
    hid[...] = jnp.zeros_like(hid)
    bias4, gain2, shift2, bias5 = nm[4:5, :], nm[2:3, :], nm[3:4, :], nm[5:6, :]

    def mid_step(i):
        here = image_rows(i, G_MID)
        m = xpad[here, :].astype(F32) + (dot_nt(att[here, :], w_proj[...]) + bias4)
        mid[here, :] = m
        xhat, _ = norm_parts(m)
        n2[here, :] = (xhat * gain2 + shift2).astype(BF16)

    over_images(mid_step, G_MID)

    def pack(piece):
        gather_sent(piece)
        kind = piece[0]
        for tt in range(2):
            parts = piece_parts(kind, tt, width)
            for ll in range(nl):
                for pp in range(np_):
                    row = (ll * np_ + pp) * r
                    blocks = []
                    for b in range(2):
                        own = [grd[row : row + r, col : col + cols] for bb, _, cols, col in parts if bb == b]
                        blocks.append(jnp.concatenate(own, axis=1) if len(own) > 1 else own[0])
                    w_buf(piece)[slot_at(tt, pp, ll)] = stacked(kind, blocks).astype(BF16)

    def sib_copy(piece):
        pc, src = sem_of(piece), w_buf(piece).at[pl.ds(o * block, block)]
        return remote(src, of(piece, sib_a, sib_m), rs_ss.at[pc], rs_sr.at[pc], other_core)

    def sum_plane_copy(piece, k):
        pc, src, dst = sem_of(piece), of(piece, sib_a, sib_m), of(piece, rpl_a, rpl_m)
        return remote(
            src.at[pl.ds(plane_peer[k] * nl, nl)], dst.at[pl.ds(p * nl, nl)], rs_ps.at[pc], rs_pr.at[pc], plane_dev[k]
        )

    def sum_line_copy(piece, k):
        pc, src, dst = sem_of(piece), of(piece, lsn_a, lsn_m), of(piece, rln_a, rln_m)
        return remote(src.at[line_peer[k]], dst.at[l], rs_ls.at[pc], rs_lr.at[pc], line_dev[k])

    def send_plane(piece):
        sib, rpl = of(piece, sib_a, sib_m), of(piece, rpl_a, rpl_m)
        got(sib, rs_sr.at[sem_of(piece)]).wait_recv()
        for at in range(block):
            sib[at] = (sib[at].astype(F32) + w_buf(piece)[t * block + at].astype(F32)).astype(BF16)
        for k in range(1, np_):
            sum_plane_copy(piece, k).start()
        own = pl.ds(p * nl, nl)
        rpl[own] = sib[own]

    def send_line(piece):
        rpl, lsn, rln = of(piece, rpl_a, rpl_m), of(piece, lsn_a, lsn_m), of(piece, rln_a, rln_m)
        got(rpl.at[pl.ds(0, (np_ - 1) * nl)], rs_pr.at[sem_of(piece)]).wait_recv()
        for ll in range(nl):
            lsn[ll] = functools.reduce(
                lambda a, b: a + b, [rpl[pp * nl + ll].astype(F32) for pp in range(np_)]
            ).astype(BF16)
        for k in range(1, nl):
            sum_line_copy(piece, k).start()
        rln[l] = lsn[l]

    def sum_line(piece):
        rln, fin = of(piece, rln_a, rln_m), of(piece, fin_a, fin_m)
        got(rln.at[pl.ds(0, nl - 1)], rs_lr.at[sem_of(piece)]).wait_recv()
        fin[...] = functools.reduce(lambda a, b: a + b, [rln[ll].astype(F32) for ll in range(nl)])

    def sums_sent(piece):
        pc = sem_of(piece)
        sib_copy(piece).wait_send()
        for sent, sem in (
            (of(piece, sib_a, sib_m).at[pl.ds(0, (np_ - 1) * nl)], rs_ps),
            (of(piece, lsn_a, lsn_m).at[pl.ds(0, nl - 1)], rs_ls),
        ):
            remote(sent, sent, sem.at[pc], dma_sem.at[2], other_core).wait_send()

    def ff_chunk(j):
        def step(i):
            here = image_rows(i, G_FF)
            b = back[here, :]
            cols = lanes(j, chunk)
            pre = dot_nn(n2[here, :], w_up[:, cols]) + biases[1:2, cols]
            ga = dot_nn(b, w_down[:, cols])
            value, slope = gelu_parts(pre)
            act[here, cols] = value.astype(BF16)
            gpre = (ga * slope).astype(BF16)
            gp[here, cols] = gpre
            hid[0:1, cols] += jnp.sum(gpre.astype(F32), axis=0, keepdims=True)

        over_images(step, G_FF)

    def ff_grad(j):
        cols = lanes(j, chunk)
        grd[:, 0:chunk] = dot_tn(n2[...], gp[:, cols])
        grd[:, chunk : 2 * chunk] = dot_tn(back[...], act[:, cols])

    def chunk_step(j, carry):
        core_done(("m", j))
        assemble(("m", j))
        ff_chunk(j)

        @pl.when(j == 0)
        def _():
            plane_done(4)

        @pl.when(j == 1)
        def _():
            plane_done(5)

        @pl.when(j > 1)
        def _():
            send_line(("m", j - 2))

        @pl.when(j > 0)
        def _():
            send_plane(("m", j - 1))

        ff_grad(j)
        pack(("m", j))
        sib_copy(("m", j)).start()
        return carry

    lax.fori_loop(0, chunks, chunk_step, 0)
    for j in range(chunks):
        vec[8 + j : 9 + j, :] = hid[0:1, j * chunk : (j + 1) * chunk]

    def back_step(i):
        here = image_rows(i, G_BACK)
        m = mid[here, :]
        xhat, rstd = norm_parts(m)
        dn = dot_nt(gp[here, :], w_up[...])
        bfl = back[here, :].astype(F32)
        gm = bfl + norm_back(dn, xhat, rstd, gain2)
        gmid[here, :] = gm
        g16 = gm.astype(BF16)
        gbr[here, :] = g16
        gatt[here, :] = dot_nn(g16, w_proj[...]).astype(BF16)
        vec[2:3, 0:dim] += jnp.sum(dn * xhat, axis=0, keepdims=True)
        vec[3:4, 0:dim] += jnp.sum(dn, axis=0, keepdims=True)
        vec[4:5, 0:dim] += jnp.sum(g16.astype(F32), axis=0, keepdims=True)
        vec[5:6, 0:dim] += jnp.sum(bfl, axis=0, keepdims=True)

    over_images(back_step, G_BACK)

    def attend_back(c):
        cols = lanes(c, 128)

        def start(i, into):
            here = image_rows(i)
            into[...] = dot_nt(pair_rows(qkv, here, c, 2), both_heads(gatt[here, cols], head_mask))

        def finish(i, dp_ref):
            here = image_rows(i)
            qp, kp = pair_rows(qkv, here, c, 0), pair_rows(qkv, here, c, 1)
            pr = probs[i * pairs + c]
            prf = pr.astype(F32)
            dp = dp_ref[...]
            inner = jnp.sum(prf * dp, axis=0, keepdims=True)
            ds = (prf * (dp - inner)).astype(BF16)
            dv = dot_nn(pr, both_heads(gatt[here, cols], head_mask)).astype(BF16)
            dk = dot_nn(ds, both_heads(qp, head_scale)).astype(BF16)
            first, second = of_heads(ds)
            dq = (dot_tn(first, kp * head_scale[0]) + dot_tn(second, kp * head_scale[1])).astype(BF16)
            for b, grad in enumerate((dq, dk, dv)):
                dqkv[here, lanes(3 * c + b, 128)] = grad
            vec[6:7, cols] += jnp.sum(dq.astype(F32), axis=0, keepdims=True)
            vec[7:8, cols] += jnp.sum(dv.astype(F32), axis=0, keepdims=True)

        start(0, even)

        def step(k):
            start(2 * k + 1, odd)
            finish(2 * k, even)
            start(jnp.minimum(2 * k + 2, images - 1), even)
            finish(2 * k + 1, odd)

        over_images(step, 2, unroll=U_ATB)

    def qkv_grad(c):
        grd[:, 0:384] = dot_tn(n1[...], dqkv[:, lanes(c, 384)])
        grd[:, 384:512] = dot_tn(gbr[...], att[:, lanes(c, 128)])
        pack(("a", c))
        sib_copy(("a", c)).start()

    send_plane(("m", 2))

    def pair_back(c, carry):
        attend_back(c)

        @pl.when(c == 0)
        def _():
            send_line(("m", 1))

        @pl.when(c > 0)
        def _():
            send_plane(("a", c - 1))

        @pl.when(c == 1)
        def _():
            send_line(("m", 2))

        qkv_grad(c)
        return carry

    lax.fori_loop(0, pairs, pair_back, 0)
    send_line(("a", 0))

    def last_step(i):
        here = image_rows(i, G_LAST)
        dn = dot_nt(dqkv[here, :], w_qkv[...])
        xhat, rstd = norm_parts(xpad[here, :].astype(F32))
        gmid[here, :] = (gmid[here, :] + norm_back(dn, xhat, rstd, gain1)) * grad_scale
        vec[0:1, 0:dim] += jnp.sum(dn * xhat, axis=0, keepdims=True)
        vec[1:2, 0:dim] += jnp.sum(dn, axis=0, keepdims=True)

    first_part = images // G_LAST // 2
    lax.fori_loop(0, first_part, lambda i, carry: last_step(i) or carry, 0)
    send_plane(("a", 2))
    lax.fori_loop(first_part, images // G_LAST, lambda i, carry: last_step(i) or carry, 0)
    send(vec, vsib, vs_s.at[0], vs_r.at[0], other_core)

    for i in range(images):
        stage[i * SEQ : (i + 1) * SEQ, :] = gmid[i * PAD : i * PAD + SEQ, :]
    gin_cp = pltpu.make_async_copy(stage.at[0:rows, :], gin_h, dma_sem.at[1])
    gin_cp.start()
    got(vsib, vs_r.at[0]).wait_recv()
    vpl[p] = vec[...] + vsib[...]
    for k in range(1, np_):
        send(vpl.at[p], vpl.at[p], vs_s.at[k], vs_r.at[k], plane_dev[k])
    send_line(("a", 1))

    def out_step(i):
        here = image_rows(i, G_OUT)
        mid[here, :] = mid[here, :] + (dot_nt(act[here, :], w_down[...]) + bias5)

    half_out = images // G_OUT // 2
    lax.fori_loop(0, half_out, lambda i, carry: out_step(i) or carry, 0)
    send_line(("a", 2))
    for k in range(1, np_):
        got(vpl.at[plane_from[k]], vs_r.at[k]).wait_recv()
    vln[l] = functools.reduce(lambda a, b: a + b, [vpl[pp] for pp in range(np_)])
    for k in range(1, nl):
        send(vln.at[l], vln.at[l], vs_s.at[np_ + k], vs_r.at[np_ + k], line_dev[k])
    lax.fori_loop(half_out, images // G_OUT, lambda i, carry: out_step(i) or carry, 0)
    for i in range(images):
        gmid[i * SEQ : (i + 1) * SEQ, :] = mid[i * PAD : i * PAD + SEQ, :]

    def cast_out(c, carry):
        at_row = pl.ds(pl.multiple_of(c * 16, 16), 16)
        n2[at_row, :] = gmid[at_row, :].astype(BF16)
        return carry

    lax.fori_loop(0, rows // 16, cast_out, 0)
    out_cp = pltpu.make_async_copy(n2.at[0:rows, :], out_h, dma_sem.at[0])
    out_cp.start()
    kept_o[...] = kept
    for pc in list(range(pairs, pairs + chunks)) + list(range(pairs)):
        sum_line(kind_of(pc))
    for k in range(1, nl):
        got(vln.at[line_from[k]], vs_r.at[np_ + k]).wait_recv()
    vec_o[...] = functools.reduce(lambda a, b: a + b, [vln[ll] for ll in range(nl)])
    out_cp.wait()
    gin_cp.wait()
    for pc in range(pairs + chunks):
        sums_sent(kind_of(pc))
    for cp in sends:
        cp.wait_send()


def update_kernel(scale_rows, *refs):
    ins, outs, kept_vm = refs[:24], refs[24:48], refs[48:]
    out_in, gin_in = ins[4:6]
    out_h, gin_h = outs[:2]
    small_in = ins[:4] + ins[6:]
    in_v, out_v = kept_vm[:22], list(kept_vm[22:40])
    big_out, big_gin, sems_in, sems_out, sems_a, sems_b = kept_vm[40:]
    copies = (3, 7, 11, 15)
    for k in copies:
        out_v.insert(k, outs[2 + k])
    parts = 3
    size = out_in.shape[0] // parts
    loads, stores = [], []
    for k in range(parts):
        here = pl.ds(k * size, size)
        for j, (src, via, dst) in enumerate(((out_in, big_out, out_h), (gin_in, big_gin, gin_h))):
            loads.append(pltpu.make_async_copy(src.at[here, :], via.at[here, :], sems_in.at[j, k]))
            stores.append(pltpu.make_async_copy(via.at[here, :], dst.at[here, :], sems_out.at[j, k]))
    small = [pltpu.make_async_copy(src, dst, sems_a.at[k]) for k, (src, dst) in enumerate(zip(small_in, in_v))]
    for cp in small + loads:
        cp.start()
    for cp in small:
        cp.wait()
    fin_a, fin_m, vec, kept = in_v[:4]
    states = [in_v[4 + 3 * k : 7 + 3 * k] for k in range(6)]
    results = [pltpu.make_async_copy(src, dst, sems_b.at[k]) for k, (src, dst) in enumerate(zip(out_v, outs[2:])) if k not in copies]
    q_o, p_o, a_o, c_o = (out_v[4 * k : 4 * k + 4] for k in range(4))
    n_o, b_o = out_v[16:19], out_v[19:22]
    qkv, proj, fc1, fc2, norm, bias = states
    r, hw = proj[0].shape
    chunks, _, width = fin_m.shape
    own = lax.axis_index("tp") == 0
    grad_scale = scale_rows / kept[0:1, 0:1]

    def update(grad, state, outs, rate, decay, c=None):
        pick = (lambda ref: ref[...]) if c is None else (lambda ref: ref[c])
        master, first, second = (pick(ref) for ref in state)
        first, second, master = adam(master, first, second, grad * grad_scale, rate, decay)
        for ref, value in zip(outs, (first, second, master, master)):
            if c is None:
                ref[...] = value.astype(ref.dtype)
            else:
                ref[c] = value.astype(ref.dtype)

    pairs = fin_a.shape[0]

    def over_pairs(block, lane_at):
        return jnp.concatenate(
            [fin_a[c, block * r : (block + 1) * r, lane_at : lane_at + 64] for c in range(pairs)], axis=1
        )

    update(over_pairs(0, 0), qkv, q_o, 0.08, matrix_decay, 0)
    update(over_pairs(0, 64), qkv, q_o, 0.08, matrix_decay, 1)
    update(over_pairs(1, 0), qkv, q_o, 0.08, matrix_decay, 2)
    update(over_pairs(1, 64), proj, p_o, 0.8, matrix_decay)
    update(jnp.concatenate([fin_m[j, 0:r, :] for j in range(chunks)], axis=1), fc1, a_o, 0.08, matrix_decay)
    update(jnp.concatenate([fin_m[j, r : 2 * r, :] for j in range(chunks)], axis=1), fc2, c_o, 0.04, matrix_decay)
    update(vec[0:6, 0 : norm[0].shape[1]], norm, n_o, 0.5, 0.0)

    def pick(row, col, cols):
        return jnp.where(
            own, vec[row : row + 1, col : col + cols], vec[row : row + 1, col + cols : col + 2 * cols]
        )

    bias_parts = [pick(row, 128 * c, 64) for row in (6, 7) for c in range(pairs)]
    bias_parts += [pick(8 + j, 0, width) for j in range(chunks)]
    update(jnp.concatenate(bias_parts, axis=1), bias, b_o, 0.5, 0.0)
    for cp in results:
        cp.start()
    for load, store in zip(loads, stores):
        load.wait()
        store.start()
    for cp in results + stores:
        cp.wait()


def body(
    inputs, keep_mask, cotangent,
    qkv_master, qkv_first, qkv_second,
    proj_master, proj_first, proj_second,
    fc1_master, fc1_first, fc1_second,
    fc2_master, fc2_first, fc2_second,
    norm_master, norm_first, norm_second,
    bias_master, bias_first, bias_second,
):
    n = lax.axis_size("dp")
    nl = 4 if n % 4 == 0 else n
    np_ = n // nl
    rows, dim = inputs.shape
    images = rows // SEQ
    padded = images * PAD
    r = qkv_master.shape[1]
    hw = qkv_master.shape[2]
    fw = fc1_master.shape[1]
    width = 256
    chunks = fw // width
    chunk = 2 * width
    slot_a = -(-2 * r // 16) * 16
    pairs = dim // HEAD_DIM // 2
    slot_m = -(-2 * r // 16) * 16
    vm = pl.BlockSpec(memory_space=pltpu.VMEM)
    hbm = pl.BlockSpec(memory_space=pl.ANY)

    def like(a, dtype=None):
        return jax.ShapeDtypeStruct(a.shape, dtype or a.dtype)

    proj_master, proj_first, proj_second = proj_master.T, proj_first.T, proj_second.T
    fc2_master, fc2_first, fc2_second = fc2_master.T, fc2_first.T, fc2_second.T
    large = [like(inputs), like(inputs, F32)]
    sums = [
        jax.ShapeDtypeStruct((pairs, slot_a, 128), F32),
        jax.ShapeDtypeStruct((chunks, slot_m, width), F32),
        jax.ShapeDtypeStruct((16, chunk), F32),
        jax.ShapeDtypeStruct((8, 128), F32),
    ]
    dma = pltpu.SemaphoreType.DMA
    pieces = pairs + chunks
    small = (keep_mask, qkv_master, proj_master, fc1_master, fc2_master, norm_master, bias_master)
    scratch = [pltpu.VMEM(a.shape, a.dtype) for a in small] + [
        pltpu.VMEM((pairs, 2 * np_ * nl, slot_a, 128), BF16),
        pltpu.VMEM((chunks, 2 * np_ * nl, slot_m, width), BF16),
        pltpu.VMEM((dim, 3 * dim), BF16),
        pltpu.VMEM((dim, dim), BF16),
        pltpu.VMEM((dim, chunks * chunk), BF16),
        pltpu.VMEM((dim, chunks * chunk), BF16),
        pltpu.VMEM((dim, 2 * chunk), F32),
        pltpu.VMEM((pairs, np_ * nl, slot_a, 128), BF16),
        pltpu.VMEM((chunks, np_ * nl, slot_m, width), BF16),
        pltpu.VMEM((pairs, np_ * nl, slot_a, 128), BF16),
        pltpu.VMEM((chunks, np_ * nl, slot_m, width), BF16),
        pltpu.VMEM((pairs, nl, slot_a, 128), BF16),
        pltpu.VMEM((chunks, nl, slot_m, width), BF16),
        pltpu.VMEM((pairs, nl, slot_a, 128), BF16),
        pltpu.VMEM((chunks, nl, slot_m, width), BF16),
        pltpu.VMEM((slot_a, 128), F32),
        pltpu.VMEM((slot_m, width), F32),
        pltpu.VMEM((2, 8, bias_master.shape[1]), F32),
        pltpu.VMEM((nl, 8, 128), F32),
        pltpu.VMEM((np_, 8, 128), F32),
        pltpu.VMEM((8, chunks * chunk), F32),
        pltpu.VMEM((8, chunks * chunk), F32),
        pltpu.VMEM((16, chunk), F32),
        pltpu.VMEM((16, chunk), F32),
        pltpu.VMEM((np_, 16, chunk), F32),
        pltpu.VMEM((nl, 16, chunk), F32),
        pltpu.VMEM((-(-(rows - SEQ + PAD) // 16) * 16, dim), F32),
        pltpu.VMEM((padded, dim), F32),
        pltpu.VMEM((padded, dim), F32),
        pltpu.VMEM((images * pairs, PAD, 2 * WIDE), BF16),
        pltpu.VMEM((PAD, 2 * WIDE), F32),
        pltpu.VMEM((PAD, 2 * WIDE), F32),
        pltpu.VMEM((images, PAD, 128), F32),
        pltpu.VMEM((128, 128), F32),
        pltpu.VMEM((padded, dim), BF16),
        pltpu.VMEM((padded, dim), BF16),
        pltpu.VMEM((padded, dim), BF16),
        pltpu.VMEM((padded, 3 * dim), BF16),
        pltpu.VMEM((padded, dim), BF16),
        pltpu.VMEM((padded, dim), BF16),
        pltpu.VMEM((padded, dim), BF16),
        pltpu.VMEM((padded, dim), BF16),
        pltpu.VMEM((padded, chunks * chunk), BF16),
        pltpu.VMEM((padded, chunks * chunk), BF16),
        pltpu.VMEM((padded, 3 * dim), BF16),
        dma((3,)),
        dma((7,)),
        dma((pieces,)),
        dma((pieces, nl - 1)),
        dma((pieces, np_ - 1)),
        dma((pieces,)),
        dma((pieces,)),
        dma((pieces,)),
        dma((pieces,)),
        dma((pieces,)),
        dma((pieces,)),
        dma((pieces,)),
        dma((nl,)),
        dma((nl,)),
        dma((np_,)),
        dma((np_,)),
        dma((np_ + nl,)),
        dma((np_ + nl,)),
    ]
    out, gin, fin_a, fin_m, vec, kept = pl.pallas_call(
        functools.partial(kernel, nl, np_),
        out_shape=large + sums,
        in_specs=[hbm] * 9,
        out_specs=[hbm, hbm] + [vm] * 4,
        scratch_shapes=scratch,
        compiler_params=pltpu.CompilerParams(
            collective_id=0, has_side_effects=True, vmem_limit_bytes=64 * 1024 * 1024
        ),
    )(inputs, keep_mask, cotangent, qkv_master, proj_master, fc1_master, fc2_master, norm_master, bias_master)
    states = [
        qkv_master, qkv_first, qkv_second,
        proj_master, proj_first, proj_second,
        fc1_master, fc1_first, fc1_second,
        fc2_master, fc2_first, fc2_second,
        norm_master, norm_first, norm_second,
        bias_master, bias_first, bias_second,
    ]
    outs = list(large)
    for a in (qkv_master, proj_master, fc1_master, fc2_master):
        outs += [like(a), like(a), like(a), like(a, BF16)]
    for a in (norm_master, bias_master):
        outs += [like(a)] * 3
    res = list(
        pl.pallas_call(
            functools.partial(update_kernel, rows * 2.0 * n),
            out_shape=outs,
            in_specs=[hbm] * 24,
            out_specs=[vm if a.dtype == BF16 and k > 0 else hbm for k, a in enumerate(outs)],
            scratch_shapes=[pltpu.VMEM(a.shape, a.dtype) for a in sums + states + [a for a in outs[2:] if a.dtype == F32]]
            + [pltpu.VMEM((rows, dim), BF16), pltpu.VMEM((rows, dim), F32)]
            + [dma((2, 3)), dma((2, 3)), dma((22,)), dma((22,))],
            compiler_params=pltpu.CompilerParams(vmem_limit_bytes=64 * 1024 * 1024),
        )(fin_a, fin_m, vec, kept, out, gin, *states)
    )
    for k in (6, 7, 8, 9, 14, 15, 16, 17):
        res[k] = res[k].T
    return tuple(res)


def solution(mesh):
    mats = [P(None, "dp", "tp"), P("tp", "dp"), P("dp", "tp"), P("tp", "dp")]
    in_specs = [P(("dp", "tp"), None), P("dp"), P(("dp", "tp"), None)]
    out_specs = [P(("dp", "tp"), None), P(("dp", "tp"), None)]
    for m in mats:
        in_specs += [m] * 3
        out_specs += [m] * 4
    in_specs += [P()] * 3 + [P("tp", None)] * 3
    out_specs += [P()] * 3 + [P("tp", None)] * 3
    return jax.shard_map(
        body, mesh=mesh, in_specs=tuple(in_specs), out_specs=tuple(out_specs), check_vma=False
    )
```

```python
import functools

import jax
import jax.numpy as jnp
from jax import lax
from jax.experimental import pallas as pl
from jax.experimental.pallas import tpu as pltpu
from jax.sharding import PartitionSpec as P

HEAD_DIM = 64
PATCHES = 196
STEP = 5

norm_eps = 1e-06
beta_one = 0.9
beta_two = 0.999
adam_eps = 1e-08
matrix_decay = 0.05

F32 = jnp.float32
BF16 = jnp.bfloat16
MESH = pl.DeviceIdType.MESH
SEQ = PATCHES + 2
PAD = 208
WIDE = 256
NEG = -1000000000.0
SCALE = HEAD_DIM**-0.5
G_QKV, G_MID, G_FF, G_BACK, G_LAST, G_OUT = 8, 4, 8, 4, 4, 4
U_ATT, U_ATB = 8, 4


def dot_nn(a, b):
    return lax.dot_general(a, b, (((1,), (0,)), ((), ())), preferred_element_type=F32)


def dot_nt(a, b):
    return lax.dot_general(a, b, (((1,), (1,)), ((), ())), preferred_element_type=F32)


def dot_tn(a, b):
    return lax.dot_general(a, b, (((0,), (0,)), ((), ())), preferred_element_type=F32)


def norm_parts(v):
    mean = jnp.mean(v, axis=-1, keepdims=True)
    centred = v - mean
    var = jnp.mean(centred * centred, axis=-1, keepdims=True)
    rstd = lax.rsqrt(var + norm_eps)
    return centred * rstd, rstd


def norm_back(grad, xhat, rstd, gain):
    u = grad * gain
    return (
        u
        - jnp.mean(u, axis=-1, keepdims=True)
        - xhat * jnp.mean(u * xhat, axis=-1, keepdims=True)
    ) * rstd


def gelu_parts(u):
    cdf = 0.5 + 0.5 * lax.erf(0.7071067811865476 * u)
    return u * cdf, cdf + u * (0.3989422804014327 * jnp.exp(-0.5 * u * u))


def adam(master, first, second, grad, rate, decay):
    first = beta_one * first + (1.0 - beta_one) * grad
    second = beta_two * second + (1.0 - beta_two) * grad * grad
    first_hat = first / (1.0 - beta_one**STEP)
    second_hat = second / (1.0 - beta_two**STEP)
    master = master - rate * (first_hat / (jnp.sqrt(second_hat) + adam_eps) + decay * master)
    return first, second, master


def piece_parts(kind, tt, width):
    if kind == "a":
        return [(b // 2, 64 * (b % 2), 64, 128 * b + 64 * tt) for b in range(4)]
    return [(0, 0, width, width * tt), (1, 0, width, 2 * width + width * tt)]


def kernel(
    nl,
    np_,
    x_h,
    keep_h,
    cot_h,
    qm_h,
    pm_h,
    am_h,
    cm_h,
    nm_h,
    bm_h,
    out_h,
    gin_h,
    fin_a,
    fin_m,
    vec_o,
    kept_o,
    keep_v,
    qm,
    pm,
    am,
    cm,
    nm,
    bm,
    wba,
    wbm,
    w_qkv,
    w_proj,
    w_up,
    w_down,
    grd,
    gproj,
    sib_a,
    sib_m,
    rpl_a,
    rpl_m,
    lsn_a,
    lsn_m,
    rln_a,
    rln_m,
    pk_a,
    pk_m,
    bias2,
    cntl,
    cntp,
    biases,
    hid,
    vec,
    vsib,
    vpl,
    vln,
    stage,
    mid,
    gmid,
    probs,
    even,
    odd,
    mcol,
    mkt,
    xpad,
    back,
    n1,
    qkv,
    att,
    n2,
    gbr,
    gatt,
    act,
    gp,
    dqkv,
    dma_sem,
    in_sem,
    ag_s,
    ag_lr,
    ag_pr,
    ag_cr,
    rs_ss,
    rs_sr,
    rs_ps,
    rs_pr,
    rs_ls,
    rs_lr,
    cn_s,
    cn_r,
    cm_s,
    cm_r,
    vs_s,
    vs_r,
):
    rows, dim = x_h.shape
    images = rows // SEQ
    r = qm.shape[1]
    hw = qm.shape[2]
    width = wbm.shape[3]
    chunks = wbm.shape[0]
    chunk = 2 * width
    heads = dim // HEAD_DIM
    pairs = heads // 2
    t = lax.axis_index("tp")
    d = lax.axis_index("dp")
    l = d // np_
    p = d - l * np_
    o = 1 - t

    line_peer = [lax.rem(l + k, nl) for k in range(nl)]
    line_from = [lax.rem(l + nl - k, nl) for k in range(nl)]
    plane_peer = [lax.rem(p + k, np_) for k in range(np_)]
    plane_from = [lax.rem(p + np_ - k, np_) for k in range(np_)]
    line_dev = [{"dp": ll * np_ + p} for ll in line_peer]
    plane_dev = [{"dp": l * np_ + pp} for pp in plane_peer]
    other_core = {"tp": o}
    block = nl * np_

    def slot_at(tt, pp, ll):
        return tt * block + pp * nl + ll

    own_slot = slot_at(t, p, l)

    x_in = pltpu.make_async_copy(x_h, dqkv.at[0:rows, 0:dim], dma_sem.at[0])
    c_in = pltpu.make_async_copy(cot_h, dqkv.at[0:rows, dim : 2 * dim], dma_sem.at[1])
    small_in = [
        pltpu.make_async_copy(src, dst, in_sem.at[k])
        for k, (src, dst) in enumerate(
            ((qm_h, qm), (pm_h, pm), (am_h, am), (cm_h, cm), (bm_h, bm), (keep_h, keep_v), (nm_h, nm))
        )
    ]
    for cp in small_in:
        cp.start()
    x_in.start()
    c_in.start()

    barrier = pltpu.get_barrier_semaphore()
    for k in range(1, nl):
        pl.semaphore_signal(barrier, inc=1, device_id=line_dev[k], device_id_type=MESH)
    for k in range(1, np_):
        pl.semaphore_signal(barrier, inc=1, device_id=plane_dev[k], device_id_type=MESH)
    pl.semaphore_signal(barrier, inc=1, device_id=other_core, device_id_type=MESH)

    def kind_of(pc):
        return ("a", pc) if pc < pairs else ("m", pc - pairs)

    def of(piece, a_ref, m_ref):
        kind, at = piece
        return a_ref.at[at] if kind == "a" else m_ref.at[at]

    def w_buf(piece):
        return of(piece, wba, wbm)

    def sem_of(piece):
        kind, at = piece
        return at if kind == "a" else pairs + at

    def stacked(kind, blocks):
        pk = pk_a if kind == "a" else pk_m
        have, need = r * len(blocks), pk.shape[0]
        if r % 8 == 0:
            pad = [jnp.zeros((need - have, pk.shape[1]), F32)] if need > have else []
            return jnp.concatenate(list(blocks) + pad, axis=0)
        if need > have:
            pk[...] = jnp.zeros_like(pk)
        for b, block in enumerate(blocks):
            pk[b * r : (b + 1) * r, :] = block
        return pk[...]

    for cp in small_in:
        cp.wait()
    def pack_own(pc):
        kind, at = kind_of(pc)
        if kind == "a":
            cols = slice(64 * at, 64 * at + 64)
            top = jnp.concatenate([qm[0, :, cols], qm[1, :, cols]], axis=1)
            blocks = [top, jnp.concatenate([qm[2, :, cols], pm[:, cols]], axis=1)]
        else:
            cols = slice(at * width, (at + 1) * width)
            blocks = [am[:, cols], cm[:, cols]]
        w_buf((kind, at))[own_slot] = stacked(kind, blocks).astype(BF16)

    pack_own(0)
    bias2[t] = jnp.broadcast_to(bm[...], bias2.shape[1:])
    full = keep_v.shape[0] // 128
    tail = keep_v.shape[0] - full * 128
    mkt[...] = jnp.zeros_like(mkt)
    mkt[0:full, :] = keep_v[pl.ds(0, full * 128)].reshape(full, 128).astype(F32)
    if tail:
        mkt[full : full + 1, 0:tail] = keep_v[pl.ds(full * 128, tail)].reshape(1, tail).astype(F32)
    count = jnp.sum(jnp.sum(mkt[...], axis=1, keepdims=True), axis=0, keepdims=True)
    cntl[l] = jnp.broadcast_to(count, cntl.shape[1:])

    pl.semaphore_wait(barrier, nl - 1 + np_ - 1 + 1)

    def remote(src, dst, ssem, rsem, device):
        return pltpu.make_async_remote_copy(
            src_ref=src, dst_ref=dst, send_sem=ssem, recv_sem=rsem, device_id=device, device_id_type=MESH
        )

    def got(dst, rsem):
        return remote(dst, dst, dma_sem.at[2], rsem, other_core)

    sends = []

    def send(src, dst, ssem, rsem, device):
        cp = remote(src, dst, ssem, rsem, device)
        cp.start()
        sends.append(cp)

    def line_copy(piece, k):
        pc, here = sem_of(piece), w_buf(piece).at[own_slot]
        return remote(here, here, ag_s.at[pc], ag_lr.at[pc, k - 1], line_dev[k])

    def plane_copy(piece, kl, k):
        pc, here = sem_of(piece), w_buf(piece).at[slot_at(t, p, line_from[kl])]
        return remote(here, here, ag_s.at[pc], ag_pr.at[pc, k - 1], plane_dev[k])

    def core_copy(piece, k):
        pc, here = sem_of(piece), w_buf(piece).at[pl.ds(slot_at(t, plane_from[k], 0), nl)]
        return remote(here, here, ag_s.at[pc], ag_cr.at[pc], other_core)

    def own_to_plane(piece):
        for k in range(1, np_):
            plane_copy(piece, 0, k).start()

    def start_piece(pc):
        piece = kind_of(pc)
        for k in range(1, nl):
            line_copy(piece, k).start()
        if piece[0] == "a":
            own_to_plane(piece)

    def line_done(pc):
        piece = kind_of(pc)
        if piece[0] == "m":
            own_to_plane(piece)
        for k in range(1, nl):
            got(w_buf(piece).at[slot_at(t, p, line_from[k])], ag_lr.at[pc, k - 1]).wait_recv()
            for kp in range(1, np_):
                plane_copy(piece, k, kp).start()
        core_copy(piece, 0).start()

    def plane_done(pc):
        piece = kind_of(pc)
        for k in range(1, np_):
            got(w_buf(piece).at[pl.ds(slot_at(t, plane_from[k], 0), nl)], ag_pr.at[pc, k - 1]).wait_recv()
            core_copy(piece, k).start()

    def core_done(piece):
        got(w_buf(piece).at[pl.ds(o * block, block)], ag_cr.at[sem_of(piece)]).wait_recv()

    def gather_sent(piece):
        sent = w_buf(piece).at[pl.ds(0, 2 * block - 1)]
        remote(sent, sent, ag_s.at[sem_of(piece)], dma_sem.at[2], other_core).wait_send()

    def lanes(at, size):
        return pl.ds(pl.multiple_of(at * size, 128), size)

    def assemble(piece):
        kind, where = piece
        for tt in range(2):
            for ll in range(nl):
                for pp in range(np_):
                    slot = w_buf(piece)[slot_at(tt, pp, ll)].astype(F32)
                    row = (ll * np_ + pp) * r
                    for b, lane_at, cols, col in piece_parts(kind, tt, width):
                        grd[row : row + r, col : col + cols] = slot[b * r : (b + 1) * r, lane_at : lane_at + cols]
        if kind == "a":
            w_qkv[:, lanes(where, 384)] = grd[:, 0:384].astype(BF16)
            w_proj[:, lanes(where, 128)] = grd[:, 384:512].astype(BF16)
        else:
            w_up[:, lanes(where, chunk)] = grd[:, 0:chunk].astype(BF16)
            w_down[:, lanes(where, chunk)] = grd[:, chunk : 2 * chunk].astype(BF16)

    start_piece(0)
    send(bias2.at[t], bias2.at[t], cm_s.at[0], cm_r.at[0], other_core)
    for k in range(1, nl):
        send(cntl.at[l], cntl.at[l], cn_s.at[k], cn_r.at[k], line_dev[k])

    for pc in range(1, pairs):
        pack_own(pc)
        start_piece(pc)
    for pc in range(pairs, pairs + chunks):
        pack_own(pc)

    def cast_in(col):
        def step(c, carry):
            at_row = pl.ds(pl.multiple_of(c * 16, 16), 16)
            stage[at_row, :] = dqkv[at_row, col : col + dim].astype(F32)
            return carry

        lax.fori_loop(0, rows // 16, step, 0)

    stage[rows:, :] = jnp.zeros((stage.shape[0] - rows, dim), F32)
    mask_rows = mkt[...].astype(BF16)
    ones = jnp.ones((128, 128), BF16)
    row_id = lax.broadcasted_iota(jnp.int32, (PAD, 128), 0)
    lane_id = lax.broadcasted_iota(jnp.int32, (PAD, 128), 1)
    for i in range(images):
        token = row_id + (t * rows + i * SEQ)
        picked = dot_nn((lane_id == token // 128).astype(F32).astype(BF16), mask_rows)
        hit = (lane_id == token % 128) & (row_id < SEQ)
        mcol[i] = dot_nn(jnp.where(hit, picked, 0.0).astype(BF16), ones)
    inside = lax.broadcasted_iota(jnp.int32, (PAD, dim), 0) < SEQ
    x_in.wait()
    cast_in(0)
    gain1, shift1 = nm[0:1, :], nm[1:2, :]

    def norm_in(i):
        v = jnp.where(inside, stage[i * SEQ : i * SEQ + PAD, :], 0.0)
        xpad[i * PAD : (i + 1) * PAD, :] = v.astype(BF16)
        xhat, _ = norm_parts(v)
        n1[i * PAD : (i + 1) * PAD, :] = (xhat * gain1 + shift1).astype(BF16)

    def back_in(i):
        v = jnp.where(inside, stage[i * SEQ : i * SEQ + PAD, :], 0.0)
        m = mcol[i]
        back[i * PAD : (i + 1) * PAD, :] = (v * jnp.concatenate([m] * (dim // 128), axis=1)).astype(BF16)

    for i in range(images // 4):
        norm_in(i)
    line_done(0)
    start_piece(3)
    for i in range(images // 4, images // 2):
        norm_in(i)
    line_done(1)
    for k in range(1, nl):
        got(cntl.at[line_from[k]], cn_r.at[k]).wait_recv()
    cntp[p] = functools.reduce(lambda a, b: a + b, [cntl[ll] for ll in range(nl)])
    for k in range(1, np_):
        send(cntp.at[p], cntp.at[p], cm_s.at[k], cm_r.at[k], plane_dev[k])
    line_done(2)
    for i in range(images // 2, images):
        norm_in(i)
    plane_done(0)
    c_in.wait()
    cast_in(dim)
    for i in range(images):
        back_in(i)
    core_done(kind_of(0))
    got(bias2.at[o], cm_r.at[0]).wait_recv()
    assemble(kind_of(0))

    def image_rows(i, many=1):
        return pl.ds(pl.multiple_of(i * (many * PAD), 16), many * PAD)

    def over_images(step, many=1, unroll=1):
        lax.fori_loop(0, images // many, lambda i, carry: step(i) or carry, 0, unroll=unroll)

    both = [bias2[0, 0:1, :], bias2[1, 0:1, :]]
    for j in range(chunks):
        parts = [b[:, 2 * hw + j * width : 2 * hw + (j + 1) * width] for b in both]
        biases[1:2, j * chunk : (j + 1) * chunk] = jnp.concatenate(parts, axis=1)
    for c in range(pairs):
        parts = [b[:, 64 * c : 64 * c + 64] for b in both] + [jnp.zeros((1, 128), F32)]
        parts += [b[:, hw + 64 * c : hw + 64 * c + 64] for b in both]
        biases[0:1, 384 * c : 384 * c + 384] = jnp.concatenate(parts, axis=1)

    def qkv_rows(c):
        cols = lanes(c, 384)

        def step(i):
            here = image_rows(i, G_QKV)
            qkv[here, cols] = (dot_nn(n1[here, :], w_qkv[:, cols]) + biases[0:1, cols]).astype(BF16)

        over_images(step, G_QKV)

    lane = lax.broadcasted_iota(jnp.int32, (1, 128), 1)
    head_mask = [(lane < HEAD_DIM).astype(F32).astype(BF16), (lane >= HEAD_DIM).astype(F32).astype(BF16)]
    head_scale = [(SCALE * mask.astype(F32)).astype(BF16) for mask in head_mask]

    def both_heads(v, scales):
        gap = jnp.zeros((WIDE - PAD, 128), BF16)
        return jnp.concatenate([v * scales[0], gap, v * scales[1], gap], axis=0)

    def of_heads(v):
        return v[:, 0:PAD], v[:, WIDE : WIDE + PAD]

    def pair_rows(ref, here, c, b):
        return ref[here, lanes(3 * c + b, 128)]

    def attend(c):
        def step(i):
            here = image_rows(i)
            qp, kp, vp = (pair_rows(qkv, here, c, b) for b in range(3))
            open_key = jnp.concatenate([mcol[i]] * (2 * WIDE // 128), axis=1) > 0.0
            s = jnp.where(open_key, dot_nt(kp, both_heads(qp, head_scale)), NEG)
            e = jnp.exp(s - jnp.max(s, axis=0, keepdims=True))
            pr = (e * (1.0 / jnp.sum(e, axis=0, keepdims=True))).astype(BF16)
            probs[i * pairs + c] = pr
            first, second = of_heads(pr)
            total = dot_tn(first, vp * head_mask[0]) + dot_tn(second, vp * head_mask[1])
            att[here, lanes(c, 128)] = total.astype(BF16)

        over_images(step, unroll=U_ATT)

    def pair_forward(c, carry):
        qkv_rows(c)

        @pl.when(c == 0)
        def _():
            plane_done(1)
            start_piece(4)

        @pl.when(c == 1)
        def _():
            plane_done(2)
            start_piece(5)

        @pl.when(c == 2)
        def _():
            line_done(4)

        attend(c)

        @pl.when(c < pairs - 1)
        def _():
            core_done(("a", c + 1))
            assemble(("a", c + 1))

        return carry

    line_done(3)
    lax.fori_loop(0, pairs, pair_forward, 0)
    plane_done(3)
    line_done(5)
    for k in range(1, np_):
        got(cntp.at[plane_from[k]], cm_r.at[k]).wait_recv()
    kept = functools.reduce(lambda a, b: a + b, [cntp[pp] for pp in range(np_)])
    grad_scale = (rows * 2.0 * nl * np_) / kept[0:1, 0:1]

    vec[...] = jnp.zeros_like(vec)
    hid[...] = jnp.zeros_like(hid)
    bias4, gain2, shift2, bias5 = nm[4:5, :], nm[2:3, :], nm[3:4, :], nm[5:6, :]

    def mid_step(i):
        here = image_rows(i, G_MID)
        m = xpad[here, :].astype(F32) + (dot_nt(att[here, :], w_proj[...]) + bias4)
        mid[here, :] = m
        xhat, _ = norm_parts(m)
        n2[here, :] = (xhat * gain2 + shift2).astype(BF16)

    over_images(mid_step, G_MID)

    def pack(piece):
        gather_sent(piece)
        kind = piece[0]
        for tt in range(2):
            parts = piece_parts(kind, tt, width)
            for ll in range(nl):
                for pp in range(np_):
                    row = (ll * np_ + pp) * r
                    blocks = []
                    for b in range(2):
                        own = [grd[row : row + r, col : col + cols] for bb, _, cols, col in parts if bb == b]
                        blocks.append(jnp.concatenate(own, axis=1) if len(own) > 1 else own[0])
                    w_buf(piece)[slot_at(tt, pp, ll)] = stacked(kind, blocks).astype(BF16)

    def sib_copy(piece):
        pc, src = sem_of(piece), w_buf(piece).at[pl.ds(o * block, block)]
        return remote(src, of(piece, sib_a, sib_m), rs_ss.at[pc], rs_sr.at[pc], other_core)

    def sum_plane_copy(piece, k):
        pc, src, dst = sem_of(piece), of(piece, sib_a, sib_m), of(piece, rpl_a, rpl_m)
        return remote(
            src.at[pl.ds(plane_peer[k] * nl, nl)], dst.at[pl.ds(p * nl, nl)], rs_ps.at[pc], rs_pr.at[pc], plane_dev[k]
        )

    def sum_line_copy(piece, k):
        pc, src, dst = sem_of(piece), of(piece, lsn_a, lsn_m), of(piece, rln_a, rln_m)
        return remote(src.at[line_peer[k]], dst.at[l], rs_ls.at[pc], rs_lr.at[pc], line_dev[k])

    def send_plane(piece):
        sib, rpl = of(piece, sib_a, sib_m), of(piece, rpl_a, rpl_m)
        got(sib, rs_sr.at[sem_of(piece)]).wait_recv()
        for at in range(block):
            sib[at] = (sib[at].astype(F32) + w_buf(piece)[t * block + at].astype(F32)).astype(BF16)
        for k in range(1, np_):
            sum_plane_copy(piece, k).start()
        own = pl.ds(p * nl, nl)
        rpl[own] = sib[own]

    def send_line(piece):
        rpl, lsn, rln = of(piece, rpl_a, rpl_m), of(piece, lsn_a, lsn_m), of(piece, rln_a, rln_m)
        got(rpl.at[pl.ds(0, (np_ - 1) * nl)], rs_pr.at[sem_of(piece)]).wait_recv()
        for ll in range(nl):
            lsn[ll] = functools.reduce(
                lambda a, b: a + b, [rpl[pp * nl + ll].astype(F32) for pp in range(np_)]
            ).astype(BF16)
        for k in range(1, nl):
            sum_line_copy(piece, k).start()
        rln[l] = lsn[l]

    def sum_line(piece):
        rln, fin = of(piece, rln_a, rln_m), of(piece, fin_a, fin_m)
        got(rln.at[pl.ds(0, nl - 1)], rs_lr.at[sem_of(piece)]).wait_recv()
        fin[...] = functools.reduce(lambda a, b: a + b, [rln[ll].astype(F32) for ll in range(nl)])

    def sums_sent(piece):
        pc = sem_of(piece)
        sib_copy(piece).wait_send()
        for sent, sem in (
            (of(piece, sib_a, sib_m).at[pl.ds(0, (np_ - 1) * nl)], rs_ps),
            (of(piece, lsn_a, lsn_m).at[pl.ds(0, nl - 1)], rs_ls),
        ):
            remote(sent, sent, sem.at[pc], dma_sem.at[2], other_core).wait_send()

    def ff_chunk(j):
        def step(i):
            here = image_rows(i, G_FF)
            b = back[here, :]
            cols = lanes(j, chunk)
            pre = dot_nn(n2[here, :], w_up[:, cols]) + biases[1:2, cols]
            ga = dot_nn(b, w_down[:, cols])
            value, slope = gelu_parts(pre)
            act[here, cols] = value.astype(BF16)
            gpre = (ga * slope).astype(BF16)
            gp[here, cols] = gpre
            hid[0:1, cols] += jnp.sum(gpre.astype(F32), axis=0, keepdims=True)

        over_images(step, G_FF)

    def ff_grad(j):
        cols = lanes(j, chunk)
        grd[:, 0:chunk] = dot_tn(n2[...], gp[:, cols])
        grd[:, chunk : 2 * chunk] = dot_tn(back[...], act[:, cols])

    def chunk_step(j, carry):
        core_done(("m", j))
        assemble(("m", j))
        ff_chunk(j)

        @pl.when(j == 0)
        def _():
            plane_done(4)

        @pl.when(j == 1)
        def _():
            plane_done(5)

        @pl.when(j > 0)
        def _():
            send_plane(("m", j - 1))

        ff_grad(j)
        pack(("m", j))
        sib_copy(("m", j)).start()
        return carry

    lax.fori_loop(0, chunks, chunk_step, 0)

    def vec_copy(part, at):
        ssem, rsem = vs_s.at[part, at], vs_r.at[part, at]
        if at == 0:
            return remote(vec.at[part], vsib.at[part], ssem, rsem, other_core)
        if at < np_:
            return remote(vpl.at[part, p], vpl.at[part, p], ssem, rsem, plane_dev[at])
        return remote(vln.at[part, l], vln.at[part, l], ssem, rsem, line_dev[at - np_ + 1])

    def vec_core(part):
        vec_copy(part, 0).start()

    def vec_plane(part):
        got(vsib.at[part], vs_r.at[part, 0]).wait_recv()
        vpl[part, p] = vec[part] + vsib[part]
        for k in range(1, np_):
            vec_copy(part, k).start()

    def vec_line(part):
        for k in range(1, np_):
            got(vpl.at[part, plane_from[k]], vs_r.at[part, k]).wait_recv()
        vln[part, l] = functools.reduce(lambda a, b: a + b, [vpl[part, pp] for pp in range(np_)])
        for k in range(1, nl):
            vec_copy(part, np_ - 1 + k).start()

    def vec_sum(part):
        for k in range(1, nl):
            got(vln.at[part, line_from[k]], vs_r.at[part, np_ - 1 + k]).wait_recv()
        return functools.reduce(lambda a, b: a + b, [vln[part, ll] for ll in range(nl)])

    def back_step(i):
        here = image_rows(i, G_BACK)
        m = mid[here, :]
        xhat, rstd = norm_parts(m)
        dn = dot_nt(gp[here, :], w_up[...])
        bfl = back[here, :].astype(F32)
        gm = bfl + norm_back(dn, xhat, rstd, gain2)
        gmid[here, :] = gm
        g16 = gm.astype(BF16)
        gbr[here, :] = g16
        gatt[here, :] = dot_nn(g16, w_proj[...]).astype(BF16)
        vec[0, 0:1, 0:dim] += jnp.sum(dn * xhat, axis=0, keepdims=True)
        vec[0, 1:2, 0:dim] += jnp.sum(dn, axis=0, keepdims=True)
        vec[0, 2:3, 0:dim] += jnp.sum(g16.astype(F32), axis=0, keepdims=True)
        vec[0, 3:4, 0:dim] += jnp.sum(bfl, axis=0, keepdims=True)

    over_images(back_step, G_BACK)
    for j in range(chunks):
        vec[0, 4 + j : 5 + j, :] = hid[0:1, j * chunk : (j + 1) * chunk]
    vec_core(0)

    def attend_back(c):
        cols = lanes(c, 128)

        def start(i, into):
            here = image_rows(i)
            into[...] = dot_nt(pair_rows(qkv, here, c, 2), both_heads(gatt[here, cols], head_mask))

        def finish(i, dp_ref):
            here = image_rows(i)
            qp, kp = pair_rows(qkv, here, c, 0), pair_rows(qkv, here, c, 1)
            pr = probs[i * pairs + c]
            prf = pr.astype(F32)
            dp = dp_ref[...]
            inner = jnp.sum(prf * dp, axis=0, keepdims=True)
            ds = (prf * (dp - inner)).astype(BF16)
            dv = dot_nn(pr, both_heads(gatt[here, cols], head_mask)).astype(BF16)
            dk = dot_nn(ds, both_heads(qp, head_scale)).astype(BF16)
            first, second = of_heads(ds)
            dq = (dot_tn(first, kp * head_scale[0]) + dot_tn(second, kp * head_scale[1])).astype(BF16)
            for b, grad in enumerate((dq, dk, dv)):
                dqkv[here, lanes(3 * c + b, 128)] = grad
            vec[1, 2:3, cols] += jnp.sum(dq.astype(F32), axis=0, keepdims=True)
            vec[1, 3:4, cols] += jnp.sum(dv.astype(F32), axis=0, keepdims=True)

        start(0, even)

        def step(k):
            start(2 * k + 1, odd)
            finish(2 * k, even)
            start(jnp.minimum(2 * k + 2, images - 1), even)
            finish(2 * k + 1, odd)

        over_images(step, 2, unroll=U_ATB)

    def qkv_grad(c):
        grd[:, 0:384] = dot_tn(n1[...], dqkv[:, lanes(c, 384)])
        grd[:, 384:512] = gproj[:, lanes(c, 128)]
        pack(("a", c))
        sib_copy(("a", c)).start()

    send_line(("m", 0))
    send_plane(("m", 2))
    gproj[...] = dot_tn(gbr[...], att[...])

    def pair_back(c, carry):
        attend_back(c)

        @pl.when(c == 0)
        def _():
            vec_plane(0)
            send_line(("m", 1))

        @pl.when(c > 0)
        def _():
            send_plane(("a", c - 1))

        @pl.when(c == 1)
        def _():
            vec_line(0)

        @pl.when(c == 2)
        def _():
            send_line(("m", 2))

        qkv_grad(c)
        return carry

    lax.fori_loop(0, pairs, pair_back, 0)
    send_line(("a", 0))

    def last_step(i):
        here = image_rows(i, G_LAST)
        dn = dot_nt(dqkv[here, :], w_qkv[...])
        xhat, rstd = norm_parts(xpad[here, :].astype(F32))
        gmid[here, :] = (gmid[here, :] + norm_back(dn, xhat, rstd, gain1)) * grad_scale
        vec[1, 0:1, 0:dim] += jnp.sum(dn * xhat, axis=0, keepdims=True)
        vec[1, 1:2, 0:dim] += jnp.sum(dn, axis=0, keepdims=True)

    first_part = images // G_LAST // 2
    lax.fori_loop(0, first_part, lambda i, carry: last_step(i) or carry, 0)
    send_plane(("a", 2))
    lax.fori_loop(first_part, images // G_LAST, lambda i, carry: last_step(i) or carry, 0)
    vec_core(1)

    for i in range(images):
        stage[i * SEQ : (i + 1) * SEQ, :] = gmid[i * PAD : i * PAD + SEQ, :]
    gin_cp = pltpu.make_async_copy(stage.at[0:rows, :], gin_h, dma_sem.at[1])
    gin_cp.start()
    vec_plane(1)
    send_line(("a", 1))

    def out_step(i):
        here = image_rows(i, G_OUT)
        mid[here, :] = mid[here, :] + (dot_nt(act[here, :], w_down[...]) + bias5)

    half_out = images // G_OUT // 2
    lax.fori_loop(0, half_out, lambda i, carry: out_step(i) or carry, 0)
    send_line(("a", 2))
    vec_line(1)
    lax.fori_loop(half_out, images // G_OUT, lambda i, carry: out_step(i) or carry, 0)
    for i in range(images):
        gmid[i * SEQ : (i + 1) * SEQ, :] = mid[i * PAD : i * PAD + SEQ, :]

    def cast_out(c, carry):
        at_row = pl.ds(pl.multiple_of(c * 16, 16), 16)
        n2[at_row, :] = gmid[at_row, :].astype(BF16)
        return carry

    lax.fori_loop(0, rows // 16, cast_out, 0)
    out_cp = pltpu.make_async_copy(n2.at[0:rows, :], out_h, dma_sem.at[0])
    out_cp.start()
    kept_o[...] = kept
    for pc in list(range(pairs, pairs + chunks)) + list(range(pairs)):
        sum_line(kind_of(pc))
    early, last = vec_sum(0), vec_sum(1)
    vec_o[0:2, :] = last[0:2, :]
    vec_o[2:6, :] = early[0:4, :]
    vec_o[6:8, :] = last[2:4, :]
    vec_o[8:11, :] = early[4:7, :]
    vec_o[11:16, :] = jnp.zeros((5, chunk), F32)
    out_cp.wait()
    gin_cp.wait()
    for pc in range(pairs + chunks):
        sums_sent(kind_of(pc))
    for part in range(2):
        for at in range(np_ + nl - 1):
            vec_copy(part, at).wait_send()
    for cp in sends:
        cp.wait_send()


def update_kernel(scale_rows, *refs):
    ins, outs, kept_vm = refs[:24], refs[24:48], refs[48:]
    out_in, gin_in = ins[4:6]
    out_h, gin_h = outs[:2]
    small_in = ins[:4] + ins[6:]
    in_v, out_v = kept_vm[:22], list(kept_vm[22:40])
    big_out, big_gin, sems_in, sems_out, sems_a, sems_b = kept_vm[40:]
    copies = (3, 7, 11, 15)
    for k in copies:
        out_v.insert(k, outs[2 + k])
    parts = 3
    size = out_in.shape[0] // parts
    loads, stores = [], []
    for k in range(parts):
        here = pl.ds(k * size, size)
        for j, (src, via, dst) in enumerate(((out_in, big_out, out_h), (gin_in, big_gin, gin_h))):
            loads.append(pltpu.make_async_copy(src.at[here, :], via.at[here, :], sems_in.at[j, k]))
            stores.append(pltpu.make_async_copy(via.at[here, :], dst.at[here, :], sems_out.at[j, k]))
    small = [pltpu.make_async_copy(src, dst, sems_a.at[k]) for k, (src, dst) in enumerate(zip(small_in, in_v))]
    for cp in loads + small:
        cp.start()
    for load, store in zip(loads, stores):
        load.wait()
        store.start()
    for cp in small:
        cp.wait()
    fin_a, fin_m, vec, kept = in_v[:4]
    states = [in_v[4 + 3 * k : 7 + 3 * k] for k in range(6)]
    results = [pltpu.make_async_copy(src, dst, sems_b.at[k]) for k, (src, dst) in enumerate(zip(out_v, outs[2:])) if k not in copies]
    q_o, p_o, a_o, c_o = (out_v[4 * k : 4 * k + 4] for k in range(4))
    n_o, b_o = out_v[16:19], out_v[19:22]
    qkv, proj, fc1, fc2, norm, bias = states
    r, hw = proj[0].shape
    chunks, _, width = fin_m.shape
    own = lax.axis_index("tp") == 0
    grad_scale = scale_rows / kept[0:1, 0:1]

    def update(grad, state, outs, rate, decay, c=None):
        pick = (lambda ref: ref[...]) if c is None else (lambda ref: ref[c])
        master, first, second = (pick(ref) for ref in state)
        first, second, master = adam(master, first, second, grad * grad_scale, rate, decay)
        for ref, value in zip(outs, (first, second, master, master)):
            if c is None:
                ref[...] = value.astype(ref.dtype)
            else:
                ref[c] = value.astype(ref.dtype)

    pairs = fin_a.shape[0]

    def begin(a, b):
        for cp in results[a:b]:
            cp.start()

    def over_pairs(block, lane_at):
        return jnp.concatenate(
            [fin_a[c, block * r : (block + 1) * r, lane_at : lane_at + 64] for c in range(pairs)], axis=1
        )

    update(over_pairs(0, 0), qkv, q_o, 0.08, matrix_decay, 0)
    update(over_pairs(0, 64), qkv, q_o, 0.08, matrix_decay, 1)
    update(over_pairs(1, 0), qkv, q_o, 0.08, matrix_decay, 2)
    begin(0, 3)
    update(over_pairs(1, 64), proj, p_o, 0.8, matrix_decay)
    begin(3, 6)
    update(jnp.concatenate([fin_m[j, 0:r, :] for j in range(chunks)], axis=1), fc1, a_o, 0.08, matrix_decay)
    begin(6, 9)
    update(jnp.concatenate([fin_m[j, r : 2 * r, :] for j in range(chunks)], axis=1), fc2, c_o, 0.04, matrix_decay)
    begin(9, 12)
    update(vec[0:6, 0 : norm[0].shape[1]], norm, n_o, 0.5, 0.0)
    begin(12, 15)

    def pick(row, col, cols):
        return jnp.where(
            own, vec[row : row + 1, col : col + cols], vec[row : row + 1, col + cols : col + 2 * cols]
        )

    bias_parts = [pick(row, 128 * c, 64) for row in (6, 7) for c in range(pairs)]
    bias_parts += [pick(8 + j, 0, width) for j in range(chunks)]
    update(jnp.concatenate(bias_parts, axis=1), bias, b_o, 0.5, 0.0)
    begin(15, 18)
    for cp in results + stores:
        cp.wait()


def body(
    inputs, keep_mask, cotangent,
    qkv_master, qkv_first, qkv_second,
    proj_master, proj_first, proj_second,
    fc1_master, fc1_first, fc1_second,
    fc2_master, fc2_first, fc2_second,
    norm_master, norm_first, norm_second,
    bias_master, bias_first, bias_second,
):
    n = lax.axis_size("dp")
    nl = 4 if n % 4 == 0 else n
    np_ = n // nl
    rows, dim = inputs.shape
    images = rows // SEQ
    padded = images * PAD
    r = qkv_master.shape[1]
    hw = qkv_master.shape[2]
    fw = fc1_master.shape[1]
    width = 256
    chunks = fw // width
    chunk = 2 * width
    slot_a = -(-2 * r // 16) * 16
    pairs = dim // HEAD_DIM // 2
    slot_m = -(-2 * r // 16) * 16
    vm = pl.BlockSpec(memory_space=pltpu.VMEM)
    hbm = pl.BlockSpec(memory_space=pl.ANY)

    def like(a, dtype=None):
        return jax.ShapeDtypeStruct(a.shape, dtype or a.dtype)

    proj_master, proj_first, proj_second = proj_master.T, proj_first.T, proj_second.T
    fc2_master, fc2_first, fc2_second = fc2_master.T, fc2_first.T, fc2_second.T
    large = [like(inputs), like(inputs, F32)]
    sums = [
        jax.ShapeDtypeStruct((pairs, slot_a, 128), F32),
        jax.ShapeDtypeStruct((chunks, slot_m, width), F32),
        jax.ShapeDtypeStruct((16, chunk), F32),
        jax.ShapeDtypeStruct((8, 128), F32),
    ]
    dma = pltpu.SemaphoreType.DMA
    pieces = pairs + chunks
    small = (keep_mask, qkv_master, proj_master, fc1_master, fc2_master, norm_master, bias_master)
    scratch = [pltpu.VMEM(a.shape, a.dtype) for a in small] + [
        pltpu.VMEM((pairs, 2 * np_ * nl, slot_a, 128), BF16),
        pltpu.VMEM((chunks, 2 * np_ * nl, slot_m, width), BF16),
        pltpu.VMEM((dim, 3 * dim), BF16),
        pltpu.VMEM((dim, dim), BF16),
        pltpu.VMEM((dim, chunks * chunk), BF16),
        pltpu.VMEM((dim, chunks * chunk), BF16),
        pltpu.VMEM((dim, 2 * chunk), F32),
        pltpu.VMEM((dim, dim), F32),
        pltpu.VMEM((pairs, np_ * nl, slot_a, 128), BF16),
        pltpu.VMEM((chunks, np_ * nl, slot_m, width), BF16),
        pltpu.VMEM((pairs, np_ * nl, slot_a, 128), BF16),
        pltpu.VMEM((chunks, np_ * nl, slot_m, width), BF16),
        pltpu.VMEM((pairs, nl, slot_a, 128), BF16),
        pltpu.VMEM((chunks, nl, slot_m, width), BF16),
        pltpu.VMEM((pairs, nl, slot_a, 128), BF16),
        pltpu.VMEM((chunks, nl, slot_m, width), BF16),
        pltpu.VMEM((slot_a, 128), F32),
        pltpu.VMEM((slot_m, width), F32),
        pltpu.VMEM((2, 8, bias_master.shape[1]), F32),
        pltpu.VMEM((nl, 8, 128), F32),
        pltpu.VMEM((np_, 8, 128), F32),
        pltpu.VMEM((8, chunks * chunk), F32),
        pltpu.VMEM((8, chunks * chunk), F32),
        pltpu.VMEM((2, 8, chunk), F32),
        pltpu.VMEM((2, 8, chunk), F32),
        pltpu.VMEM((2, np_, 8, chunk), F32),
        pltpu.VMEM((2, nl, 8, chunk), F32),
        pltpu.VMEM((-(-(rows - SEQ + PAD) // 16) * 16, dim), F32),
        pltpu.VMEM((padded, dim), F32),
        pltpu.VMEM((padded, dim), F32),
        pltpu.VMEM((images * pairs, PAD, 2 * WIDE), BF16),
        pltpu.VMEM((PAD, 2 * WIDE), F32),
        pltpu.VMEM((PAD, 2 * WIDE), F32),
        pltpu.VMEM((images, PAD, 128), F32),
        pltpu.VMEM((128, 128), F32),
        pltpu.VMEM((padded, dim), BF16),
        pltpu.VMEM((padded, dim), BF16),
        pltpu.VMEM((padded, dim), BF16),
        pltpu.VMEM((padded, 3 * dim), BF16),
        pltpu.VMEM((padded, dim), BF16),
        pltpu.VMEM((padded, dim), BF16),
        pltpu.VMEM((padded, dim), BF16),
        pltpu.VMEM((padded, dim), BF16),
        pltpu.VMEM((padded, chunks * chunk), BF16),
        pltpu.VMEM((padded, chunks * chunk), BF16),
        pltpu.VMEM((padded, 3 * dim), BF16),
        dma((3,)),
        dma((7,)),
        dma((pieces,)),
        dma((pieces, nl - 1)),
        dma((pieces, np_ - 1)),
        dma((pieces,)),
        dma((pieces,)),
        dma((pieces,)),
        dma((pieces,)),
        dma((pieces,)),
        dma((pieces,)),
        dma((pieces,)),
        dma((nl,)),
        dma((nl,)),
        dma((np_,)),
        dma((np_,)),
        dma((2, np_ + nl - 1)),
        dma((2, np_ + nl - 1)),
    ]
    out, gin, fin_a, fin_m, vec, kept = pl.pallas_call(
        functools.partial(kernel, nl, np_),
        out_shape=large + sums,
        in_specs=[hbm] * 9,
        out_specs=[hbm, hbm] + [vm] * 4,
        scratch_shapes=scratch,
        compiler_params=pltpu.CompilerParams(
            collective_id=0, has_side_effects=True, vmem_limit_bytes=64 * 1024 * 1024
        ),
    )(inputs, keep_mask, cotangent, qkv_master, proj_master, fc1_master, fc2_master, norm_master, bias_master)
    states = [
        qkv_master, qkv_first, qkv_second,
        proj_master, proj_first, proj_second,
        fc1_master, fc1_first, fc1_second,
        fc2_master, fc2_first, fc2_second,
        norm_master, norm_first, norm_second,
        bias_master, bias_first, bias_second,
    ]
    outs = list(large)
    for a in (qkv_master, proj_master, fc1_master, fc2_master):
        outs += [like(a), like(a), like(a), like(a, BF16)]
    for a in (norm_master, bias_master):
        outs += [like(a)] * 3
    res = list(
        pl.pallas_call(
            functools.partial(update_kernel, rows * 2.0 * n),
            out_shape=outs,
            in_specs=[hbm] * 24,
            out_specs=[vm if a.dtype == BF16 and k > 0 else hbm for k, a in enumerate(outs)],
            scratch_shapes=[pltpu.VMEM(a.shape, a.dtype) for a in sums + states + [a for a in outs[2:] if a.dtype == F32]]
            + [pltpu.VMEM((rows, dim), BF16), pltpu.VMEM((rows, dim), F32)]
            + [dma((2, 3)), dma((2, 3)), dma((22,)), dma((22,))],
            compiler_params=pltpu.CompilerParams(vmem_limit_bytes=64 * 1024 * 1024),
        )(fin_a, fin_m, vec, kept, out, gin, *states)
    )
    for k in (6, 7, 8, 9, 14, 15, 16, 17):
        res[k] = res[k].T
    return tuple(res)


def solution(mesh):
    mats = [P(None, "dp", "tp"), P("tp", "dp"), P("dp", "tp"), P("tp", "dp")]
    in_specs = [P(("dp", "tp"), None), P("dp"), P(("dp", "tp"), None)]
    out_specs = [P(("dp", "tp"), None), P(("dp", "tp"), None)]
    for m in mats:
        in_specs += [m] * 3
        out_specs += [m] * 4
    in_specs += [P()] * 3 + [P("tp", None)] * 3
    out_specs += [P()] * 3 + [P("tp", None)] * 3
    return jax.shard_map(
        body, mesh=mesh, in_specs=tuple(in_specs), out_specs=tuple(out_specs), check_vma=False
    )
```

```python
import functools

import jax
import jax.numpy as jnp
from jax import lax
from jax.experimental import pallas as pl
from jax.experimental.pallas import tpu as pltpu
from jax.sharding import PartitionSpec as P

HEAD_DIM = 64
PATCHES = 196
STEP = 5

norm_eps = 1e-06
beta_one = 0.9
beta_two = 0.999
adam_eps = 1e-08
matrix_decay = 0.05

F32 = jnp.float32
BF16 = jnp.bfloat16
MESH = pl.DeviceIdType.MESH
SEQ = PATCHES + 2
PAD = 208
WIDE = 256
NEG = -1000000000.0
SCALE = HEAD_DIM**-0.5
G_QKV, G_MID, G_FF, G_BACK, G_LAST, G_OUT = 8, 4, 8, 4, 4, 4
U_ATT, U_ATB = 8, 4


def dot_nn(a, b):
    return lax.dot_general(a, b, (((1,), (0,)), ((), ())), preferred_element_type=F32)


def dot_nt(a, b):
    return lax.dot_general(a, b, (((1,), (1,)), ((), ())), preferred_element_type=F32)


def dot_tn(a, b):
    return lax.dot_general(a, b, (((0,), (0,)), ((), ())), preferred_element_type=F32)


def norm_parts(v):
    mean = jnp.mean(v, axis=-1, keepdims=True)
    centred = v - mean
    var = jnp.mean(centred * centred, axis=-1, keepdims=True)
    rstd = lax.rsqrt(var + norm_eps)
    return centred * rstd, rstd


def norm_back(grad, xhat, rstd, gain):
    u = grad * gain
    return (
        u
        - jnp.mean(u, axis=-1, keepdims=True)
        - xhat * jnp.mean(u * xhat, axis=-1, keepdims=True)
    ) * rstd


def gelu_parts(u):
    cdf = 0.5 + 0.5 * lax.erf(0.7071067811865476 * u)
    return u * cdf, cdf + u * (0.3989422804014327 * jnp.exp(-0.5 * u * u))


def adam(master, first, second, grad, rate, decay):
    first = beta_one * first + (1.0 - beta_one) * grad
    second = beta_two * second + (1.0 - beta_two) * grad * grad
    first_hat = first / (1.0 - beta_one**STEP)
    second_hat = second / (1.0 - beta_two**STEP)
    master = master - rate * (first_hat / (jnp.sqrt(second_hat) + adam_eps) + decay * master)
    return first, second, master


def piece_parts(kind, tt, width):
    if kind == "a":
        return [(b // 2, 64 * (b % 2), 64, 128 * b + 64 * tt) for b in range(4)]
    return [(0, 0, width, width * tt), (1, 0, width, 2 * width + width * tt)]


def kernel(
    nl,
    np_,
    x_h,
    keep_h,
    cot_h,
    qm_h,
    pm_h,
    am_h,
    cm_h,
    nm_h,
    bm_h,
    out_h,
    gin_h,
    fin_a,
    fin_m,
    vec_o,
    kept_o,
    keep_v,
    qm,
    pm,
    am,
    cm,
    nm,
    bm,
    wba,
    wbm,
    w_qkv,
    w_proj,
    w_up,
    w_down,
    grd,
    gproj,
    sib_a,
    sib_m,
    rpl_a,
    rpl_m,
    lsn_a,
    lsn_m,
    rln_a,
    rln_m,
    pk_a,
    pk_m,
    bias2,
    cntl,
    cntp,
    biases,
    hid,
    vec,
    vpl,
    vln,
    stage,
    mid,
    gmid,
    probs,
    even,
    odd,
    mcol,
    mkt,
    xpad,
    back,
    n1,
    qkv,
    att,
    n2,
    gbr,
    gatt,
    act,
    gp,
    dqkv,
    dma_sem,
    in_sem,
    ag_s,
    ag_lr,
    ag_pr,
    ag_cr,
    rs_ss,
    rs_sr,
    rs_ps,
    rs_pr,
    rs_ls,
    rs_lr,
    cn_s,
    cn_r,
    cm_s,
    cm_r,
    vs_s,
    vs_r,
):
    rows, dim = x_h.shape
    images = rows // SEQ
    r = qm.shape[1]
    hw = qm.shape[2]
    width = wbm.shape[3]
    chunks = wbm.shape[0]
    chunk = 2 * width
    heads = dim // HEAD_DIM
    pairs = heads // 2
    t = lax.axis_index("tp")
    d = lax.axis_index("dp")
    l = d // np_
    p = d - l * np_
    o = 1 - t

    line_peer = [lax.rem(l + k, nl) for k in range(nl)]
    line_from = [lax.rem(l + nl - k, nl) for k in range(nl)]
    plane_peer = [lax.rem(p + k, np_) for k in range(np_)]
    plane_from = [lax.rem(p + np_ - k, np_) for k in range(np_)]
    line_dev = [{"dp": ll * np_ + p} for ll in line_peer]
    plane_dev = [{"dp": l * np_ + pp} for pp in plane_peer]
    other_core = {"tp": o}
    cross_dev = [{"dp": l * np_ + pp, "tp": o} for pp in plane_peer]
    block = nl * np_

    def slot_at(tt, pp, ll):
        return tt * block + pp * nl + ll

    own_slot = slot_at(t, p, l)

    x_in = pltpu.make_async_copy(x_h, dqkv.at[0:rows, 0:dim], dma_sem.at[0])
    c_in = pltpu.make_async_copy(cot_h, dqkv.at[0:rows, dim : 2 * dim], dma_sem.at[1])
    small_in = [
        pltpu.make_async_copy(src, dst, in_sem.at[k])
        for k, (src, dst) in enumerate(
            ((qm_h, qm), (pm_h, pm), (am_h, am), (cm_h, cm), (bm_h, bm), (keep_h, keep_v), (nm_h, nm))
        )
    ]
    for cp in small_in:
        cp.start()
    x_in.start()
    c_in.start()

    barrier = pltpu.get_barrier_semaphore()
    for k in range(1, nl):
        pl.semaphore_signal(barrier, inc=1, device_id=line_dev[k], device_id_type=MESH)
    for k in range(1, np_):
        pl.semaphore_signal(barrier, inc=1, device_id=plane_dev[k], device_id_type=MESH)
        pl.semaphore_signal(barrier, inc=1, device_id=cross_dev[k], device_id_type=MESH)
    pl.semaphore_signal(barrier, inc=1, device_id=other_core, device_id_type=MESH)

    def kind_of(pc):
        return ("a", pc) if pc < pairs else ("m", pc - pairs)

    def of(piece, a_ref, m_ref):
        kind, at = piece
        return a_ref.at[at] if kind == "a" else m_ref.at[at]

    def w_buf(piece):
        return of(piece, wba, wbm)

    def sem_of(piece):
        kind, at = piece
        return at if kind == "a" else pairs + at

    def stacked(kind, blocks):
        pk = pk_a if kind == "a" else pk_m
        have, need = r * len(blocks), pk.shape[0]
        if r % 8 == 0:
            pad = [jnp.zeros((need - have, pk.shape[1]), F32)] if need > have else []
            return jnp.concatenate(list(blocks) + pad, axis=0)
        if need > have:
            pk[...] = jnp.zeros_like(pk)
        for b, block in enumerate(blocks):
            pk[b * r : (b + 1) * r, :] = block
        return pk[...]

    for cp in small_in:
        cp.wait()
    def pack_own(pc):
        kind, at = kind_of(pc)
        if kind == "a":
            cols = slice(64 * at, 64 * at + 64)
            top = jnp.concatenate([qm[0, :, cols], qm[1, :, cols]], axis=1)
            blocks = [top, jnp.concatenate([qm[2, :, cols], pm[:, cols]], axis=1)]
        else:
            cols = slice(at * width, (at + 1) * width)
            blocks = [am[:, cols], cm[:, cols]]
        w_buf((kind, at))[own_slot] = stacked(kind, blocks).astype(BF16)

    pack_own(0)
    bias2[t] = jnp.broadcast_to(bm[...], bias2.shape[1:])
    full = keep_v.shape[0] // 128
    tail = keep_v.shape[0] - full * 128
    mkt[...] = jnp.zeros_like(mkt)
    mkt[0:full, :] = keep_v[pl.ds(0, full * 128)].reshape(full, 128).astype(F32)
    if tail:
        mkt[full : full + 1, 0:tail] = keep_v[pl.ds(full * 128, tail)].reshape(1, tail).astype(F32)
    count = jnp.sum(jnp.sum(mkt[...], axis=1, keepdims=True), axis=0, keepdims=True)
    cntl[l] = jnp.broadcast_to(count, cntl.shape[1:])

    pl.semaphore_wait(barrier, nl - 1 + 2 * (np_ - 1) + 1)

    def remote(src, dst, ssem, rsem, device):
        return pltpu.make_async_remote_copy(
            src_ref=src, dst_ref=dst, send_sem=ssem, recv_sem=rsem, device_id=device, device_id_type=MESH
        )

    def got(dst, rsem):
        return remote(dst, dst, dma_sem.at[2], rsem, other_core)

    sends = []

    def send(src, dst, ssem, rsem, device):
        cp = remote(src, dst, ssem, rsem, device)
        cp.start()
        sends.append(cp)

    def line_copy(piece, k):
        pc, here = sem_of(piece), w_buf(piece).at[own_slot]
        return remote(here, here, ag_s.at[pc], ag_lr.at[pc, k - 1], line_dev[k])

    def plane_copy(piece, kl, k):
        pc, here = sem_of(piece), w_buf(piece).at[slot_at(t, p, line_from[kl])]
        return remote(here, here, ag_s.at[pc], ag_pr.at[pc, k - 1], plane_dev[k])

    def core_copy(piece, k):
        pc, here = sem_of(piece), w_buf(piece).at[pl.ds(slot_at(t, plane_from[k], 0), nl)]
        return remote(here, here, ag_s.at[pc], ag_cr.at[pc], other_core)

    def row_copy(piece, k):
        pc, here = sem_of(piece), w_buf(piece).at[pl.ds(slot_at(t, p, 0), nl)]
        return remote(here, here, ag_s.at[pc], ag_pr.at[pc, k - 1], plane_dev[k])

    def half_copy(piece):
        pc, here = sem_of(piece), w_buf(piece).at[pl.ds(t * block, block)]
        return remote(here, here, ag_s.at[pc], ag_cr.at[pc], other_core)

    def start_piece(pc):
        piece = kind_of(pc)
        for k in range(1, nl):
            line_copy(piece, k).start()
        if pc == 0:
            for k in range(1, np_):
                plane_copy(piece, 0, k).start()

    def line_done(pc):
        piece = kind_of(pc)
        for k in range(1, nl):
            got(w_buf(piece).at[slot_at(t, p, line_from[k])], ag_lr.at[pc, k - 1]).wait_recv()
            if pc == 0:
                for kp in range(1, np_):
                    plane_copy(piece, k, kp).start()
        if pc == 0:
            core_copy(piece, 0).start()
        else:
            for k in range(1, np_):
                row_copy(piece, k).start()

    def plane_done(pc):
        piece = kind_of(pc)
        for k in range(1, np_):
            got(w_buf(piece).at[pl.ds(slot_at(t, plane_from[k], 0), nl)], ag_pr.at[pc, k - 1]).wait_recv()
            if pc == 0:
                core_copy(piece, k).start()
        if pc > 0:
            half_copy(piece).start()

    def core_done(piece):
        got(w_buf(piece).at[pl.ds(o * block, block)], ag_cr.at[sem_of(piece)]).wait_recv()

    def gather_sent(piece):
        sent = w_buf(piece).at[pl.ds(0, 2 * block - 1)]
        remote(sent, sent, ag_s.at[sem_of(piece)], dma_sem.at[2], other_core).wait_send()

    def lanes(at, size):
        return pl.ds(pl.multiple_of(at * size, 128), size)

    def assemble(piece):
        kind, where = piece
        for tt in range(2):
            for ll in range(nl):
                for pp in range(np_):
                    slot = w_buf(piece)[slot_at(tt, pp, ll)].astype(F32)
                    row = (ll * np_ + pp) * r
                    for b, lane_at, cols, col in piece_parts(kind, tt, width):
                        grd[row : row + r, col : col + cols] = slot[b * r : (b + 1) * r, lane_at : lane_at + cols]
        if kind == "a":
            w_qkv[:, lanes(where, 384)] = grd[:, 0:384].astype(BF16)
            w_proj[:, lanes(where, 128)] = grd[:, 384:512].astype(BF16)
        else:
            w_up[:, lanes(where, chunk)] = grd[:, 0:chunk].astype(BF16)
            w_down[:, lanes(where, chunk)] = grd[:, chunk : 2 * chunk].astype(BF16)

    start_piece(0)
    send(bias2.at[t], bias2.at[t], cm_s.at[0], cm_r.at[0], other_core)
    for k in range(1, nl):
        send(cntl.at[l], cntl.at[l], cn_s.at[k], cn_r.at[k], line_dev[k])

    for pc in range(1, pairs):
        pack_own(pc)
        start_piece(pc)
    for pc in range(pairs, pairs + chunks):
        pack_own(pc)

    def cast_in(col):
        def step(c, carry):
            at_row = pl.ds(pl.multiple_of(c * 16, 16), 16)
            stage[at_row, :] = dqkv[at_row, col : col + dim].astype(F32)
            return carry

        lax.fori_loop(0, rows // 16, step, 0)

    stage[rows:, :] = jnp.zeros((stage.shape[0] - rows, dim), F32)
    mask_rows = mkt[...].astype(BF16)
    ones = jnp.ones((128, 128), BF16)
    row_id = lax.broadcasted_iota(jnp.int32, (PAD, 128), 0)
    lane_id = lax.broadcasted_iota(jnp.int32, (PAD, 128), 1)
    for i in range(images):
        token = row_id + (t * rows + i * SEQ)
        picked = dot_nn((lane_id == token // 128).astype(F32).astype(BF16), mask_rows)
        hit = (lane_id == token % 128) & (row_id < SEQ)
        mcol[i] = dot_nn(jnp.where(hit, picked, 0.0).astype(BF16), ones)
    inside = lax.broadcasted_iota(jnp.int32, (PAD, dim), 0) < SEQ
    x_in.wait()
    cast_in(0)
    gain1, shift1 = nm[0:1, :], nm[1:2, :]

    def norm_in(i):
        v = jnp.where(inside, stage[i * SEQ : i * SEQ + PAD, :], 0.0)
        xpad[i * PAD : (i + 1) * PAD, :] = v.astype(BF16)
        xhat, _ = norm_parts(v)
        n1[i * PAD : (i + 1) * PAD, :] = (xhat * gain1 + shift1).astype(BF16)

    def back_in(i):
        v = jnp.where(inside, stage[i * SEQ : i * SEQ + PAD, :], 0.0)
        m = mcol[i]
        back[i * PAD : (i + 1) * PAD, :] = (v * jnp.concatenate([m] * (dim // 128), axis=1)).astype(BF16)

    for i in range(images // 4):
        norm_in(i)
    line_done(0)
    start_piece(3)
    for i in range(images // 4, images // 2):
        norm_in(i)
    line_done(1)
    for k in range(1, nl):
        got(cntl.at[line_from[k]], cn_r.at[k]).wait_recv()
    cntp[p] = functools.reduce(lambda a, b: a + b, [cntl[ll] for ll in range(nl)])
    for k in range(1, np_):
        send(cntp.at[p], cntp.at[p], cm_s.at[k], cm_r.at[k], plane_dev[k])
    line_done(2)
    for i in range(images // 2, images):
        norm_in(i)
    plane_done(0)
    c_in.wait()
    cast_in(dim)
    for i in range(images):
        back_in(i)
    core_done(kind_of(0))
    got(bias2.at[o], cm_r.at[0]).wait_recv()
    assemble(kind_of(0))

    def image_rows(i, many=1):
        return pl.ds(pl.multiple_of(i * (many * PAD), 16), many * PAD)

    def over_images(step, many=1, unroll=1):
        lax.fori_loop(0, images // many, lambda i, carry: step(i) or carry, 0, unroll=unroll)

    both = [bias2[0, 0:1, :], bias2[1, 0:1, :]]
    for j in range(chunks):
        parts = [b[:, 2 * hw + j * width : 2 * hw + (j + 1) * width] for b in both]
        biases[1:2, j * chunk : (j + 1) * chunk] = jnp.concatenate(parts, axis=1)
    for c in range(pairs):
        parts = [b[:, 64 * c : 64 * c + 64] for b in both] + [jnp.zeros((1, 128), F32)]
        parts += [b[:, hw + 64 * c : hw + 64 * c + 64] for b in both]
        biases[0:1, 384 * c : 384 * c + 384] = jnp.concatenate(parts, axis=1)

    def qkv_rows(c):
        cols = lanes(c, 384)

        def step(i):
            here = image_rows(i, G_QKV)
            qkv[here, cols] = (dot_nn(n1[here, :], w_qkv[:, cols]) + biases[0:1, cols]).astype(BF16)

        over_images(step, G_QKV)

    lane = lax.broadcasted_iota(jnp.int32, (1, 128), 1)
    head_mask = [(lane < HEAD_DIM).astype(F32).astype(BF16), (lane >= HEAD_DIM).astype(F32).astype(BF16)]
    head_scale = [(SCALE * mask.astype(F32)).astype(BF16) for mask in head_mask]

    def both_heads(v, scales):
        gap = jnp.zeros((WIDE - PAD, 128), BF16)
        return jnp.concatenate([v * scales[0], gap, v * scales[1], gap], axis=0)

    def of_heads(v):
        return v[:, 0:PAD], v[:, WIDE : WIDE + PAD]

    def pair_rows(ref, here, c, b):
        return ref[here, lanes(3 * c + b, 128)]

    def attend(c):
        def step(i):
            here = image_rows(i)
            qp, kp, vp = (pair_rows(qkv, here, c, b) for b in range(3))
            open_key = jnp.concatenate([mcol[i]] * (2 * WIDE // 128), axis=1) > 0.0
            s = jnp.where(open_key, dot_nt(kp, both_heads(qp, head_scale)), NEG)
            e = jnp.exp(s - jnp.max(s, axis=0, keepdims=True))
            pr = (e * (1.0 / jnp.sum(e, axis=0, keepdims=True))).astype(BF16)
            probs[i * pairs + c] = pr
            first, second = of_heads(pr)
            total = dot_tn(first, vp * head_mask[0]) + dot_tn(second, vp * head_mask[1])
            att[here, lanes(c, 128)] = total.astype(BF16)

        over_images(step, unroll=U_ATT)

    def pair_forward(c, carry):
        qkv_rows(c)

        @pl.when(c == 0)
        def _():
            plane_done(1)
            start_piece(4)

        @pl.when(c == 1)
        def _():
            plane_done(2)
            start_piece(5)

        @pl.when(c == 2)
        def _():
            line_done(4)

        attend(c)

        @pl.when(c < pairs - 1)
        def _():
            core_done(("a", c + 1))
            assemble(("a", c + 1))

        return carry

    line_done(3)
    lax.fori_loop(0, pairs, pair_forward, 0)
    plane_done(3)
    line_done(5)
    for k in range(1, np_):
        got(cntp.at[plane_from[k]], cm_r.at[k]).wait_recv()
    kept = functools.reduce(lambda a, b: a + b, [cntp[pp] for pp in range(np_)])
    grad_scale = (rows * 2.0 * nl * np_) / kept[0:1, 0:1]

    vec[...] = jnp.zeros_like(vec)
    hid[...] = jnp.zeros_like(hid)
    bias4, gain2, shift2, bias5 = nm[4:5, :], nm[2:3, :], nm[3:4, :], nm[5:6, :]

    def mid_step(i):
        here = image_rows(i, G_MID)
        m = xpad[here, :].astype(F32) + (dot_nt(att[here, :], w_proj[...]) + bias4)
        mid[here, :] = m
        xhat, _ = norm_parts(m)
        n2[here, :] = (xhat * gain2 + shift2).astype(BF16)

    over_images(mid_step, G_MID)

    def pack(piece):
        gather_sent(piece)
        kind = piece[0]
        for tt in range(2):
            parts = piece_parts(kind, tt, width)
            for ll in range(nl):
                for pp in range(np_):
                    row = (ll * np_ + pp) * r
                    blocks = []
                    for b in range(2):
                        own = [grd[row : row + r, col : col + cols] for bb, _, cols, col in parts if bb == b]
                        blocks.append(jnp.concatenate(own, axis=1) if len(own) > 1 else own[0])
                    w_buf(piece)[slot_at(tt, pp, ll)] = stacked(kind, blocks).astype(BF16)

    def sib_copy(piece):
        pc, src = sem_of(piece), w_buf(piece).at[pl.ds(o * block, block)]
        return remote(src, of(piece, sib_a, sib_m), rs_ss.at[pc], rs_sr.at[pc], other_core)

    def sum_plane_copy(piece, k):
        pc, src, dst = sem_of(piece), of(piece, sib_a, sib_m), of(piece, rpl_a, rpl_m)
        return remote(
            src.at[pl.ds(plane_peer[k] * nl, nl)], dst.at[pl.ds(p * nl, nl)], rs_ps.at[pc], rs_pr.at[pc], plane_dev[k]
        )

    def sum_line_copy(piece, k):
        pc, src, dst = sem_of(piece), of(piece, lsn_a, lsn_m), of(piece, rln_a, rln_m)
        return remote(src.at[line_peer[k]], dst.at[l], rs_ls.at[pc], rs_lr.at[pc], line_dev[k])

    def send_plane(piece):
        sib, rpl = of(piece, sib_a, sib_m), of(piece, rpl_a, rpl_m)
        got(sib, rs_sr.at[sem_of(piece)]).wait_recv()
        for at in range(block):
            sib[at] = (sib[at].astype(F32) + w_buf(piece)[t * block + at].astype(F32)).astype(BF16)
        for k in range(1, np_):
            sum_plane_copy(piece, k).start()
        own = pl.ds(p * nl, nl)
        rpl[own] = sib[own]

    def send_line(piece):
        rpl, lsn, rln = of(piece, rpl_a, rpl_m), of(piece, lsn_a, lsn_m), of(piece, rln_a, rln_m)
        got(rpl.at[pl.ds(0, (np_ - 1) * nl)], rs_pr.at[sem_of(piece)]).wait_recv()
        for ll in range(nl):
            lsn[ll] = functools.reduce(
                lambda a, b: a + b, [rpl[pp * nl + ll].astype(F32) for pp in range(np_)]
            ).astype(BF16)
        for k in range(1, nl):
            sum_line_copy(piece, k).start()
        rln[l] = lsn[l]

    def sum_line(piece):
        rln, fin = of(piece, rln_a, rln_m), of(piece, fin_a, fin_m)
        got(rln.at[pl.ds(0, nl - 1)], rs_lr.at[sem_of(piece)]).wait_recv()
        fin[...] = functools.reduce(lambda a, b: a + b, [rln[ll].astype(F32) for ll in range(nl)])

    def sums_sent(piece):
        pc = sem_of(piece)
        sib_copy(piece).wait_send()
        for sent, sem in (
            (of(piece, sib_a, sib_m).at[pl.ds(0, (np_ - 1) * nl)], rs_ps),
            (of(piece, lsn_a, lsn_m).at[pl.ds(0, nl - 1)], rs_ls),
        ):
            remote(sent, sent, sem.at[pc], dma_sem.at[2], other_core).wait_send()

    def ff_chunk(j):
        def step(i):
            here = image_rows(i, G_FF)
            b = back[here, :]
            cols = lanes(j, chunk)
            pre = dot_nn(n2[here, :], w_up[:, cols]) + biases[1:2, cols]
            ga = dot_nn(b, w_down[:, cols])
            value, slope = gelu_parts(pre)
            act[here, cols] = value.astype(BF16)
            gpre = (ga * slope).astype(BF16)
            gp[here, cols] = gpre
            hid[0:1, cols] += jnp.sum(gpre.astype(F32), axis=0, keepdims=True)

        over_images(step, G_FF)

    def ff_grad(j):
        cols = lanes(j, chunk)
        grd[:, 0:chunk] = dot_tn(n2[...], gp[:, cols])
        grd[:, chunk : 2 * chunk] = dot_tn(back[...], act[:, cols])

    def chunk_step(j, carry):
        core_done(("m", j))
        assemble(("m", j))
        ff_chunk(j)

        @pl.when(j == 0)
        def _():
            plane_done(4)

        @pl.when(j == 1)
        def _():
            plane_done(5)

        @pl.when(j > 0)
        def _():
            send_plane(("m", j - 1))

        ff_grad(j)
        pack(("m", j))
        sib_copy(("m", j)).start()
        return carry

    lax.fori_loop(0, chunks, chunk_step, 0)

    own_vec = t * np_ + p
    near = 2 * np_ - 1

    def vec_copy(part, at):
        ssem, rsem = vs_s.at[part, at], vs_r.at[part, at]
        here = (vpl if at < near else vln).at[part, own_vec if at < near else l]
        if at == 0:
            device = other_core
        elif at < np_:
            device = plane_dev[at]
        elif at < near:
            device = cross_dev[at - np_ + 1]
        else:
            device = line_dev[at - near + 1]
        return remote(here, here, ssem, rsem, device)

    def vec_start(part):
        vpl[part, own_vec] = vec[part]
        for at in range(near):
            vec_copy(part, at).start()

    def vec_line(part):
        for at in range(near):
            if at == 0:
                slot = o * np_ + p
            elif at < np_:
                slot = t * np_ + plane_from[at]
            else:
                slot = o * np_ + plane_from[at - np_ + 1]
            got(vpl.at[part, slot], vs_r.at[part, at]).wait_recv()
        vln[part, l] = functools.reduce(lambda a, b: a + b, [vpl[part, at] for at in range(2 * np_)])
        for k in range(1, nl):
            vec_copy(part, near - 1 + k).start()

    def vec_sum(part):
        for k in range(1, nl):
            got(vln.at[part, line_from[k]], vs_r.at[part, near - 1 + k]).wait_recv()
        return functools.reduce(lambda a, b: a + b, [vln[part, ll] for ll in range(nl)])

    def back_step(i):
        here = image_rows(i, G_BACK)
        m = mid[here, :]
        xhat, rstd = norm_parts(m)
        dn = dot_nt(gp[here, :], w_up[...])
        bfl = back[here, :].astype(F32)
        gm = bfl + norm_back(dn, xhat, rstd, gain2)
        gmid[here, :] = gm
        g16 = gm.astype(BF16)
        gbr[here, :] = g16
        gatt[here, :] = dot_nn(g16, w_proj[...]).astype(BF16)
        vec[0, 0:1, 0:dim] += jnp.sum(dn * xhat, axis=0, keepdims=True)
        vec[0, 1:2, 0:dim] += jnp.sum(dn, axis=0, keepdims=True)
        vec[0, 2:3, 0:dim] += jnp.sum(g16.astype(F32), axis=0, keepdims=True)
        vec[0, 3:4, 0:dim] += jnp.sum(bfl, axis=0, keepdims=True)

    over_images(back_step, G_BACK)
    for j in range(chunks):
        vec[0, 4 + j : 5 + j, :] = hid[0:1, j * chunk : (j + 1) * chunk]
    vec_start(0)

    def attend_back(c):
        cols = lanes(c, 128)

        def start(i, into):
            here = image_rows(i)
            into[...] = dot_nt(pair_rows(qkv, here, c, 2), both_heads(gatt[here, cols], head_mask))

        def finish(i, dp_ref):
            here = image_rows(i)
            qp, kp = pair_rows(qkv, here, c, 0), pair_rows(qkv, here, c, 1)
            pr = probs[i * pairs + c]
            prf = pr.astype(F32)
            dp = dp_ref[...]
            inner = jnp.sum(prf * dp, axis=0, keepdims=True)
            ds = (prf * (dp - inner)).astype(BF16)
            dv = dot_nn(pr, both_heads(gatt[here, cols], head_mask)).astype(BF16)
            dk = dot_nn(ds, both_heads(qp, head_scale)).astype(BF16)
            first, second = of_heads(ds)
            dq = (dot_tn(first, kp * head_scale[0]) + dot_tn(second, kp * head_scale[1])).astype(BF16)
            for b, grad in enumerate((dq, dk, dv)):
                dqkv[here, lanes(3 * c + b, 128)] = grad
            vec[1, 2:3, cols] += jnp.sum(dq.astype(F32), axis=0, keepdims=True)
            vec[1, 3:4, cols] += jnp.sum(dv.astype(F32), axis=0, keepdims=True)

        start(0, even)

        def step(k):
            start(2 * k + 1, odd)
            finish(2 * k, even)
            start(jnp.minimum(2 * k + 2, images - 1), even)
            finish(2 * k + 1, odd)

        over_images(step, 2, unroll=U_ATB)

    def qkv_grad(c):
        grd[:, 0:384] = dot_tn(n1[...], dqkv[:, lanes(c, 384)])
        grd[:, 384:512] = gproj[:, lanes(c, 128)]
        pack(("a", c))
        sib_copy(("a", c)).start()

    send_line(("m", 0))
    send_plane(("m", 2))
    gproj[...] = dot_tn(gbr[...], att[...])

    def pair_back(c, carry):
        attend_back(c)

        @pl.when(c == 0)
        def _():
            send_line(("m", 1))

        @pl.when(c > 0)
        def _():
            send_plane(("a", c - 1))

        @pl.when(c == 1)
        def _():
            vec_line(0)

        @pl.when(c == 2)
        def _():
            send_line(("m", 2))

        qkv_grad(c)
        return carry

    lax.fori_loop(0, pairs, pair_back, 0)
    send_line(("a", 0))

    def last_step(i):
        here = image_rows(i, G_LAST)
        dn = dot_nt(dqkv[here, :], w_qkv[...])
        xhat, rstd = norm_parts(xpad[here, :].astype(F32))
        gmid[here, :] = (gmid[here, :] + norm_back(dn, xhat, rstd, gain1)) * grad_scale
        vec[1, 0:1, 0:dim] += jnp.sum(dn * xhat, axis=0, keepdims=True)
        vec[1, 1:2, 0:dim] += jnp.sum(dn, axis=0, keepdims=True)

    first_part = images // G_LAST // 2
    lax.fori_loop(0, first_part, lambda i, carry: last_step(i) or carry, 0)
    send_plane(("a", 2))
    lax.fori_loop(first_part, images // G_LAST, lambda i, carry: last_step(i) or carry, 0)
    vec_start(1)

    for i in range(images):
        stage[i * SEQ : (i + 1) * SEQ, :] = gmid[i * PAD : i * PAD + SEQ, :]
    gin_cp = pltpu.make_async_copy(stage.at[0:rows, :], gin_h, dma_sem.at[1])
    gin_cp.start()
    send_line(("a", 1))

    def out_step(i):
        here = image_rows(i, G_OUT)
        mid[here, :] = mid[here, :] + (dot_nt(act[here, :], w_down[...]) + bias5)

    half_out = images // G_OUT // 2
    lax.fori_loop(0, half_out, lambda i, carry: out_step(i) or carry, 0)
    send_line(("a", 2))
    vec_line(1)
    early_rows = images // 2 * SEQ // 16 * 16

    def take_out(first, last, row, stop, sem):
        for i in range(first, last):
            gmid[i * SEQ : (i + 1) * SEQ, :] = mid[i * PAD : i * PAD + SEQ, :]

        def cast_out(c, carry):
            at_row = pl.ds(pl.multiple_of(row + c * 16, 16), 16)
            n2[at_row, :] = gmid[at_row, :].astype(BF16)
            return carry

        lax.fori_loop(0, (stop - row) // 16, cast_out, 0, unroll=True)
        here = pl.ds(row, stop - row)
        cp = pltpu.make_async_copy(n2.at[here, :], out_h.at[here, :], dma_sem.at[sem])
        cp.start()
        return cp

    out_first = take_out(0, images // 2, 0, early_rows, 0)
    for pc in range(pairs, pairs + chunks):
        sum_line(kind_of(pc))
    sum_line(kind_of(0))
    lax.fori_loop(half_out, images // G_OUT, lambda i, carry: out_step(i) or carry, 0)
    out_rest = take_out(images // 2, images, early_rows, rows, 3)
    kept_o[...] = kept
    for pc in range(1, pairs):
        sum_line(kind_of(pc))
    early, last = vec_sum(0), vec_sum(1)
    vec_o[0:2, :] = last[0:2, :]
    vec_o[2:6, :] = early[0:4, :]
    vec_o[6:8, :] = last[2:4, :]
    vec_o[8:11, :] = early[4:7, :]
    vec_o[11:16, :] = jnp.zeros((5, chunk), F32)
    out_first.wait()
    out_rest.wait()
    gin_cp.wait()
    for pc in range(pairs + chunks):
        sums_sent(kind_of(pc))
    for part in range(2):
        for at in range(near + nl - 1):
            vec_copy(part, at).wait_send()
    for cp in sends:
        cp.wait_send()


def update_kernel(scale_rows, *refs):
    ins, outs, kept_vm = refs[:24], refs[24:48], refs[48:]
    out_in, gin_in = ins[4:6]
    out_h, gin_h = outs[:2]
    small_in = ins[:4] + ins[6:]
    in_v, out_v = kept_vm[:22], list(kept_vm[22:40])
    big_out, big_gin, sems_in, sems_out, sems_a, sems_b = kept_vm[40:]
    copies = (3, 7, 11, 15)
    for k in copies:
        out_v.insert(k, outs[2 + k])
    parts = 3
    size = out_in.shape[0] // parts
    loads, stores = [], []
    for k in range(parts):
        here = pl.ds(k * size, size)
        for j, (src, via, dst) in enumerate(((out_in, big_out, out_h), (gin_in, big_gin, gin_h))):
            loads.append(pltpu.make_async_copy(src.at[here, :], via.at[here, :], sems_in.at[j, k]))
            stores.append(pltpu.make_async_copy(via.at[here, :], dst.at[here, :], sems_out.at[j, k]))
    small = [pltpu.make_async_copy(src, dst, sems_a.at[k]) for k, (src, dst) in enumerate(zip(small_in, in_v))]
    for cp in loads + small:
        cp.start()
    for load, store in zip(loads, stores):
        load.wait()
        store.start()
    for cp in small:
        cp.wait()
    fin_a, fin_m, vec, kept = in_v[:4]
    states = [in_v[4 + 3 * k : 7 + 3 * k] for k in range(6)]
    results = [pltpu.make_async_copy(src, dst, sems_b.at[k]) for k, (src, dst) in enumerate(zip(out_v, outs[2:])) if k not in copies]
    q_o, p_o, a_o, c_o = (out_v[4 * k : 4 * k + 4] for k in range(4))
    n_o, b_o = out_v[16:19], out_v[19:22]
    qkv, proj, fc1, fc2, norm, bias = states
    r, hw = proj[0].shape
    chunks, _, width = fin_m.shape
    own = lax.axis_index("tp") == 0
    grad_scale = scale_rows / kept[0:1, 0:1]

    def update(grad, state, outs, rate, decay, c=None):
        pick = (lambda ref: ref[...]) if c is None else (lambda ref: ref[c])
        master, first, second = (pick(ref) for ref in state)
        first, second, master = adam(master, first, second, grad * grad_scale, rate, decay)
        for ref, value in zip(outs, (first, second, master, master)):
            if c is None:
                ref[...] = value.astype(ref.dtype)
            else:
                ref[c] = value.astype(ref.dtype)

    pairs = fin_a.shape[0]

    def begin(a, b):
        for cp in results[a:b]:
            cp.start()

    def over_pairs(block, lane_at):
        return jnp.concatenate(
            [fin_a[c, block * r : (block + 1) * r, lane_at : lane_at + 64] for c in range(pairs)], axis=1
        )

    update(over_pairs(0, 0), qkv, q_o, 0.08, matrix_decay, 0)
    update(over_pairs(0, 64), qkv, q_o, 0.08, matrix_decay, 1)
    update(over_pairs(1, 0), qkv, q_o, 0.08, matrix_decay, 2)
    begin(0, 3)
    update(over_pairs(1, 64), proj, p_o, 0.8, matrix_decay)
    begin(3, 6)
    update(jnp.concatenate([fin_m[j, 0:r, :] for j in range(chunks)], axis=1), fc1, a_o, 0.08, matrix_decay)
    begin(6, 9)
    update(jnp.concatenate([fin_m[j, r : 2 * r, :] for j in range(chunks)], axis=1), fc2, c_o, 0.04, matrix_decay)
    begin(9, 12)
    update(vec[0:6, 0 : norm[0].shape[1]], norm, n_o, 0.5, 0.0)
    begin(12, 15)

    def pick(row, col, cols):
        return jnp.where(
            own, vec[row : row + 1, col : col + cols], vec[row : row + 1, col + cols : col + 2 * cols]
        )

    bias_parts = [pick(row, 128 * c, 64) for row in (6, 7) for c in range(pairs)]
    bias_parts += [pick(8 + j, 0, width) for j in range(chunks)]
    update(jnp.concatenate(bias_parts, axis=1), bias, b_o, 0.5, 0.0)
    begin(15, 18)
    for cp in results + stores:
        cp.wait()


def body(
    inputs, keep_mask, cotangent,
    qkv_master, qkv_first, qkv_second,
    proj_master, proj_first, proj_second,
    fc1_master, fc1_first, fc1_second,
    fc2_master, fc2_first, fc2_second,
    norm_master, norm_first, norm_second,
    bias_master, bias_first, bias_second,
):
    n = lax.axis_size("dp")
    nl = 4 if n % 4 == 0 else n
    np_ = n // nl
    rows, dim = inputs.shape
    images = rows // SEQ
    padded = images * PAD
    r = qkv_master.shape[1]
    hw = qkv_master.shape[2]
    fw = fc1_master.shape[1]
    width = 256
    chunks = fw // width
    chunk = 2 * width
    slot_a = -(-2 * r // 16) * 16
    pairs = dim // HEAD_DIM // 2
    slot_m = -(-2 * r // 16) * 16
    vm = pl.BlockSpec(memory_space=pltpu.VMEM)
    hbm = pl.BlockSpec(memory_space=pl.ANY)

    def like(a, dtype=None):
        return jax.ShapeDtypeStruct(a.shape, dtype or a.dtype)

    proj_master, proj_first, proj_second = proj_master.T, proj_first.T, proj_second.T
    fc2_master, fc2_first, fc2_second = fc2_master.T, fc2_first.T, fc2_second.T
    large = [like(inputs), like(inputs, F32)]
    sums = [
        jax.ShapeDtypeStruct((pairs, slot_a, 128), F32),
        jax.ShapeDtypeStruct((chunks, slot_m, width), F32),
        jax.ShapeDtypeStruct((16, chunk), F32),
        jax.ShapeDtypeStruct((8, 128), F32),
    ]
    dma = pltpu.SemaphoreType.DMA
    pieces = pairs + chunks
    small = (keep_mask, qkv_master, proj_master, fc1_master, fc2_master, norm_master, bias_master)
    scratch = [pltpu.VMEM(a.shape, a.dtype) for a in small] + [
        pltpu.VMEM((pairs, 2 * np_ * nl, slot_a, 128), BF16),
        pltpu.VMEM((chunks, 2 * np_ * nl, slot_m, width), BF16),
        pltpu.VMEM((dim, 3 * dim), BF16),
        pltpu.VMEM((dim, dim), BF16),
        pltpu.VMEM((dim, chunks * chunk), BF16),
        pltpu.VMEM((dim, chunks * chunk), BF16),
        pltpu.VMEM((dim, 2 * chunk), F32),
        pltpu.VMEM((dim, dim), F32),
        pltpu.VMEM((pairs, np_ * nl, slot_a, 128), BF16),
        pltpu.VMEM((chunks, np_ * nl, slot_m, width), BF16),
        pltpu.VMEM((pairs, np_ * nl, slot_a, 128), BF16),
        pltpu.VMEM((chunks, np_ * nl, slot_m, width), BF16),
        pltpu.VMEM((pairs, nl, slot_a, 128), BF16),
        pltpu.VMEM((chunks, nl, slot_m, width), BF16),
        pltpu.VMEM((pairs, nl, slot_a, 128), BF16),
        pltpu.VMEM((chunks, nl, slot_m, width), BF16),
        pltpu.VMEM((slot_a, 128), F32),
        pltpu.VMEM((slot_m, width), F32),
        pltpu.VMEM((2, 8, bias_master.shape[1]), F32),
        pltpu.VMEM((nl, 8, 128), F32),
        pltpu.VMEM((np_, 8, 128), F32),
        pltpu.VMEM((8, chunks * chunk), F32),
        pltpu.VMEM((8, chunks * chunk), F32),
        pltpu.VMEM((2, 8, chunk), F32),
        pltpu.VMEM((2, 2 * np_, 8, chunk), F32),
        pltpu.VMEM((2, nl, 8, chunk), F32),
        pltpu.VMEM((-(-(rows - SEQ + PAD) // 16) * 16, dim), F32),
        pltpu.VMEM((padded, dim), F32),
        pltpu.VMEM((padded, dim), F32),
        pltpu.VMEM((images * pairs, PAD, 2 * WIDE), BF16),
        pltpu.VMEM((PAD, 2 * WIDE), F32),
        pltpu.VMEM((PAD, 2 * WIDE), F32),
        pltpu.VMEM((images, PAD, 128), F32),
        pltpu.VMEM((128, 128), F32),
        pltpu.VMEM((padded, dim), BF16),
        pltpu.VMEM((padded, dim), BF16),
        pltpu.VMEM((padded, dim), BF16),
        pltpu.VMEM((padded, 3 * dim), BF16),
        pltpu.VMEM((padded, dim), BF16),
        pltpu.VMEM((padded, dim), BF16),
        pltpu.VMEM((padded, dim), BF16),
        pltpu.VMEM((padded, dim), BF16),
        pltpu.VMEM((padded, chunks * chunk), BF16),
        pltpu.VMEM((padded, chunks * chunk), BF16),
        pltpu.VMEM((padded, 3 * dim), BF16),
        dma((4,)),
        dma((7,)),
        dma((pieces,)),
        dma((pieces, nl - 1)),
        dma((pieces, np_ - 1)),
        dma((pieces,)),
        dma((pieces,)),
        dma((pieces,)),
        dma((pieces,)),
        dma((pieces,)),
        dma((pieces,)),
        dma((pieces,)),
        dma((nl,)),
        dma((nl,)),
        dma((np_,)),
        dma((np_,)),
        dma((2, 2 * np_ + nl - 2)),
        dma((2, 2 * np_ + nl - 2)),
    ]
    out, gin, fin_a, fin_m, vec, kept = pl.pallas_call(
        functools.partial(kernel, nl, np_),
        out_shape=large + sums,
        in_specs=[hbm] * 9,
        out_specs=[hbm, hbm] + [vm] * 4,
        scratch_shapes=scratch,
        compiler_params=pltpu.CompilerParams(
            collective_id=0, has_side_effects=True, vmem_limit_bytes=64 * 1024 * 1024
        ),
    )(inputs, keep_mask, cotangent, qkv_master, proj_master, fc1_master, fc2_master, norm_master, bias_master)
    states = [
        qkv_master, qkv_first, qkv_second,
        proj_master, proj_first, proj_second,
        fc1_master, fc1_first, fc1_second,
        fc2_master, fc2_first, fc2_second,
        norm_master, norm_first, norm_second,
        bias_master, bias_first, bias_second,
    ]
    outs = list(large)
    for a in (qkv_master, proj_master, fc1_master, fc2_master):
        outs += [like(a), like(a), like(a), like(a, BF16)]
    for a in (norm_master, bias_master):
        outs += [like(a)] * 3
    res = list(
        pl.pallas_call(
            functools.partial(update_kernel, rows * 2.0 * n),
            out_shape=outs,
            in_specs=[hbm] * 24,
            out_specs=[vm if a.dtype == BF16 and k > 0 else hbm for k, a in enumerate(outs)],
            scratch_shapes=[pltpu.VMEM(a.shape, a.dtype) for a in sums + states + [a for a in outs[2:] if a.dtype == F32]]
            + [pltpu.VMEM((rows, dim), BF16), pltpu.VMEM((rows, dim), F32)]
            + [dma((2, 3)), dma((2, 3)), dma((22,)), dma((22,))],
            compiler_params=pltpu.CompilerParams(vmem_limit_bytes=64 * 1024 * 1024),
        )(fin_a, fin_m, vec, kept, out, gin, *states)
    )
    for k in (6, 7, 8, 9, 14, 15, 16, 17):
        res[k] = res[k].T
    return tuple(res)


def solution(mesh):
    mats = [P(None, "dp", "tp"), P("tp", "dp"), P("dp", "tp"), P("tp", "dp")]
    in_specs = [P(("dp", "tp"), None), P("dp"), P(("dp", "tp"), None)]
    out_specs = [P(("dp", "tp"), None), P(("dp", "tp"), None)]
    for m in mats:
        in_specs += [m] * 3
        out_specs += [m] * 4
    in_specs += [P()] * 3 + [P("tp", None)] * 3
    out_specs += [P()] * 3 + [P("tp", None)] * 3
    return jax.shard_map(
        body, mesh=mesh, in_specs=tuple(in_specs), out_specs=tuple(out_specs), check_vma=False
    )
```
